32 devices in a mesh: section: 2 (over x), dp: 4 (over y, core), seq: 4 (over z).
Axes of the slice: x: 2, y: 2, z: 4, core: 2. Of those that a mesh axis runs over, the one named last changes fastest.
Arguments:
- cell_tokens: bfloat16 [8, 2048, 768], P('dp', 'seq'), may hold values from -6 to 6
- cell_lengths: int32 [8, 16], P('dp'), may hold values from 1 to 1537, as said below
- out_grad: bfloat16 [8, 2048, 768], P('dp', 'seq'), may hold values from -6 to 6
- norm1_gain: bfloat16 [2, 768], P('section'), may hold values from 0.25 to 1.75
- norm1_bias: bfloat16 [2, 768], P('section'), may hold values from -1.75 to 1.75
- qkv_weight: bfloat16 [2, 768, 2304], P('section'), may hold values from -0.21875 to 0.21875
- query_bias: bfloat16 [2, 768], P('section'), may hold values from -3 to 3
- value_bias: bfloat16 [2, 768], P('section'), may hold values from -0.625 to 0.625
- out_weight: bfloat16 [2, 768, 768], P('section'), may hold values from -1.25 to 1.25
- out_bias: bfloat16 [2, 768], P('section'), may hold values from -1.75 to 1.75
- norm2_gain: bfloat16 [2, 768], P('section'), may hold values from 0.25 to 1.75
- norm2_bias: bfloat16 [2, 768], P('section'), may hold values from -1.75 to 1.75
- in_weight: bfloat16 [2, 768, 3072], P('section'), may hold values from -0.21875 to 0.21875
- in_bias: bfloat16 [2, 3072], P('section'), may hold values from -3 to 3
- back_weight: bfloat16 [2, 3072, 768], P('section'), may hold values from -0.109375 to 0.109375
- back_bias: bfloat16 [2, 768], P('section'), may hold values from -1.75 to 1.75
Outputs:
- layer_outputs: bfloat16 [2, 8, 2048, 768], P('section', 'dp', 'seq')
- input_grads: float32 [2, 8, 2048, 768], P('section', 'dp', 'seq')
- norm1_gain_grad: float32 [2, 768], P('section', ('dp', 'seq'))
- norm1_bias_grad: float32 [2, 768], P('section', ('dp', 'seq'))
- qkv_weight_grad: float32 [2, 768, 2304], P('section', ('dp', 'seq'))
- query_bias_grad: float32 [2, 768], P('section', ('dp', 'seq'))
- value_bias_grad: float32 [2, 768], P('section', ('dp', 'seq'))
- out_weight_grad: float32 [2, 768, 768], P('section', ('dp', 'seq'))
- out_bias_grad: float32 [2, 768], P('section', ('dp', 'seq'))
- norm2_gain_grad: float32 [2, 768], P('section', ('dp', 'seq'))
- norm2_bias_grad: float32 [2, 768], P('section', ('dp', 'seq'))
- in_weight_grad: float32 [2, 768, 3072], P('section', ('dp', 'seq'))
- in_bias_grad: float32 [2, 3072], P('section', ('dp', 'seq'))
- back_weight_grad: float32 [2, 3072, 768], P('section', ('dp', 'seq'))
- back_bias_grad: float32 [2, 768], P('section', ('dp', 'seq'))
The draws below stay inside these ranges and needn't reach their ends.
Inputs may be any that keep to these rules, and one draw needn't show every extreme that they name: `cell_lengths`: each row holds 16 cells whose lengths sum to 2048. In each group of 2 consecutive rows, one row drawn from the seed has a cell of 1537 positions that starts within the first 512 positions.
All inputs are finite; a program needn't handle non-finite values.
Results may differ from the reference program's by a relative error of at most 0.014.
Values may be sent and summed in bfloat16 or wider, within the bound.
A program may use at most 384 MiB of HBM per device.

```python
import jax
import jax.numpy as jnp
from jax import lax

D = 768
HEADS = 12
HEAD = 64
FF = 3072
ROW_LEN = 2048
CELLS = 16
MB = 2
POS_DEV = 512
LONGEST = 1537
ROWS = 8
LAYERS = 2
N_DP = 4


def draw_cell_lengths(key, part):
    key = jax.random.fold_in(key, 11)
    key_rows, key_pick, key_start, key_middle = jax.random.split(key, 4)
    places = jnp.arange(1, ROW_LEN, dtype=jnp.int32)[None, :]
    noise = jax.random.randint(key_rows, (ROWS, ROW_LEN - 1), 0, 2 ** 18, dtype=jnp.int32)
    group_pick = jax.random.randint(key_pick, (N_DP,), 0, MB, dtype=jnp.int32)
    row_ids = jnp.arange(ROWS, dtype=jnp.int32)
    chosen = (row_ids % MB == group_pick[row_ids // MB])[:, None]
    start = jax.random.randint(key_start, (ROWS, 1), 1, POS_DEV - 1, dtype=jnp.int32)
    finish = start + LONGEST
    middle = jax.random.randint(key_middle, (ROWS, 1), ROW_LEN // 4, 3 * ROW_LEN // 4, dtype=jnp.int32)
    forced = jnp.where(chosen, (places == start) | (places == finish), places == middle)
    inside = chosen & (places > start) & (places < finish)
    scores = jnp.where(forced, -places, jnp.where(inside, 2 ** 30 + places, noise * ROW_LEN + places))
    picked_vals, picked = lax.top_k(-scores, CELLS - 1)
    cuts = jnp.sort(picked.astype(jnp.int32) + 1, axis=-1)
    bounds = jnp.concatenate([jnp.zeros((ROWS, 1), jnp.int32), cuts, jnp.full((ROWS, 1), ROW_LEN, jnp.int32)], axis=1)
    return bounds[:, 1:] - bounds[:, :-1]


def block_scale(rng, shape, pieces, smallest, top_value):
    def one(dim, blocks):
        steps = jax.random.uniform(jax.random.fold_in(jax.random.fold_in(rng, 6), dim), (blocks,), jnp.float32, smallest / len(pieces), top_value / len(pieces))
        return jnp.repeat(jnp.exp(steps), shape[dim] // blocks).reshape((-1,) + (1,) * (len(shape) - dim - 1))

    loudness = one(*pieces[0])
    for cut in pieces[1:]:
        loudness = loudness * one(*cut)
    return loudness


def normal_values(stream_key, dims, width, limit, cuts=(), held_as=jnp.bfloat16):
    result = jax.random.normal(stream_key, dims, jnp.float32) * width
    if len(cuts) > 0:
        result = block_scale(stream_key, dims, cuts, -0.22, 0.18) * result
    return jnp.clip(result, min=-limit, max=limit).astype(held_as)


def setup_inputs(seed: int = 0) -> dict:
    seeds = jax.random.split(jax.random.key(seed), 17)
    return {
        "cell_tokens": normal_values(seeds[0], (ROWS, ROW_LEN, D), 1.0, 6.0, ((0, 4), (1, 4))),
        "cell_lengths": draw_cell_lengths(jax.random.fold_in(seeds[16], 71), 0),
        "out_grad": normal_values(seeds[2], (ROWS, ROW_LEN, D), 1.0, 6.0, ((0, 4), (1, 4))),
        "norm1_gain": jnp.clip(1.0 + 0.15 * jax.random.normal(seeds[3], (LAYERS, D), jnp.float32), 0.25, 1.75).astype(jnp.bfloat16),
        "norm1_bias": normal_values(seeds[4], (LAYERS, D), 0.3, 1.75, ((0, 2),)),
        "qkv_weight": normal_values(seeds[5], (LAYERS, D, 3 * D), D ** -0.5, 0.21875, ((0, 2),)),
        "query_bias": normal_values(seeds[6], (LAYERS, D), 0.5, 3.0, ((0, 2),)),
        "value_bias": normal_values(seeds[7], (LAYERS, D), 0.1, 0.625, ((0, 2),)),
        "out_weight": normal_values(seeds[8], (LAYERS, D, D), (D // 32) ** -0.5, 1.25, ((0, 2),)),
        "out_bias": normal_values(seeds[9], (LAYERS, D), 0.3, 1.75, ((0, 2),)),
        "norm2_gain": jnp.clip(1.0 + 0.15 * jax.random.normal(seeds[10], (LAYERS, D), jnp.float32), 0.25, 1.75).astype(jnp.bfloat16),
        "norm2_bias": normal_values(seeds[11], (LAYERS, D), 0.3, 1.75, ((0, 2),)),
        "in_weight": normal_values(seeds[12], (LAYERS, D, FF), D ** -0.5, 0.21875, ((0, 2),)),
        "in_bias": normal_values(seeds[13], (LAYERS, FF), 0.5, 3.0, ((0, 2),)),
        "back_weight": normal_values(seeds[14], (LAYERS, FF, D), FF ** -0.5, 0.109375, ((0, 2),)),
        "back_bias": normal_values(seeds[15], (LAYERS, D), 0.3, 1.75, ((0, 2),)),
    }


HIGH = lax.Precision.HIGHEST
SCALE = 0.125
EPS = 1e-05
MASKED = -1e+30

@jax.custom_vjp
def low(v):
    return lax.optimization_barrier(v.astype(jnp.bfloat16)).astype(jnp.float32)

@jax.custom_vjp
def low_back(v):
    return v

def low_keep(v):
    return (low(v), None)

def low_pass(kept, grad):
    return (grad,)

def back_keep(v):
    return (v, None)

def back_low(kept, grad):
    return (low(grad),)
low.defvjp(low_keep, low_pass)
low_back.defvjp(back_keep, back_low)

def norm_rows(values, gain_vec, bias_vec):
    centre = lax.optimization_barrier(jnp.mean(values, axis=-1, keepdims=True))
    offset = values - centre
    spread = lax.optimization_barrier(jnp.mean(offset * offset, axis=-1, keepdims=True))
    return offset * lax.rsqrt(spread + EPS) * gain_vec + bias_vec

def row_segments(lengths):
    limits = jnp.cumsum(lengths, axis=-1)
    places = jnp.arange(ROW_LEN, dtype=jnp.int32)
    return lax.optimization_barrier(jnp.sum((places[None, :, None] >= limits[:, None, :]).astype(jnp.int32), axis=-1))

def layer_row(values, seg_row, layer_weights):
    gain_one, bias_one, w_qkv, q_bias, v_bias, w_out, b_out, gain_two, bias_two, w_in, b_in, w_back, b_back = layer_weights
    normed = low(norm_rows(values, gain_one, bias_one))
    joined = jnp.dot(normed, w_qkv, precision=HIGH)
    queries = low_back(low(joined[:, :D] + q_bias)).reshape(ROW_LEN, HEADS, HEAD)
    keys_in = low_back(low(joined[:, D:2 * D])).reshape(ROW_LEN, HEADS, HEAD)
    values_in = low_back(low(joined[:, 2 * D:] + v_bias)).reshape(ROW_LEN, HEADS, HEAD)
    block_rows = min(512, ROW_LEN)

    def attend_block(block_pair):
        query_block, seg_block = block_pair
        scores = jnp.einsum('qhe,khe->hqk', query_block, keys_in, precision=HIGH) * SCALE
        scores = low_back(jnp.where((seg_block[:, None] == seg_row[None, :])[None], scores, MASKED))
        highest = lax.optimization_barrier(jnp.max(scores, axis=-1, keepdims=True))
        raised = jnp.exp(scores - highest)
        soft_probs = low(raised / lax.optimization_barrier(jnp.sum(raised, axis=-1, keepdims=True)))
        return jnp.einsum('hqk,khe->qhe', soft_probs, values_in, precision=HIGH)
    attended = lax.map(jax.checkpoint(attend_block), (queries.reshape(ROW_LEN // block_rows, block_rows, HEADS, HEAD), seg_row.reshape(ROW_LEN // block_rows, block_rows)))
    attended = low_back(low(attended.reshape(ROW_LEN, D)))
    resid_sum = values + low_back(jnp.dot(attended, w_out, precision=HIGH) + b_out)
    normed_two = low(norm_rows(resid_sum, gain_two, bias_two))
    hidden_pre = low_back(jnp.dot(normed_two, w_in, precision=HIGH) + b_in)
    active = low(jax.nn.gelu(hidden_pre, approximate=False))
    return resid_sum + low_back(jnp.dot(active, w_back, precision=HIGH) + b_back)

def run_layer(hidden, segments, layer_weights):

    def one_row(row_pair):
        return layer_row(row_pair[0], row_pair[1], layer_weights)
    return lax.map(jax.checkpoint(one_row), (hidden, segments))

def forward(inputs, zeros_mid, all_weights, segments):
    hidden = inputs
    shown = []
    for layer_index in range(LAYERS):
        if layer_index > 0:
            hidden = low_back(low(hidden) + zeros_mid[layer_index])
        layer_weights = tuple((weight[layer_index] for weight in all_weights))
        hidden = run_layer(hidden, segments, layer_weights)
        shown.append(hidden)
    return (hidden, jnp.stack(shown))

def reference(cell_tokens, cell_lengths, out_grad, norm1_gain, norm1_bias, qkv_weight, query_bias, value_bias, out_weight, out_bias, norm2_gain, norm2_bias, in_weight, in_bias, back_weight, back_bias):
    all_weights = tuple((weight.astype(jnp.float32) for weight in (norm1_gain, norm1_bias, qkv_weight, query_bias, value_bias, out_weight, out_bias, norm2_gain, norm2_bias, in_weight, in_bias, back_weight, back_bias)))
    segments = row_segments(cell_lengths)
    inputs = cell_tokens.astype(jnp.float32)
    zeros_mid = jnp.zeros((LAYERS,) + inputs.shape, jnp.float32)

    def wrapped(inputs_now, zeros_now, weights_now):
        return forward(inputs_now, zeros_now, weights_now, segments)
    final_out, pullback, shown_full = jax.vjp(wrapped, inputs, zeros_mid, all_weights, has_aux=True)
    shown = shown_full.astype(jnp.bfloat16)
    grad_in, grad_mid, grad_weights = pullback(out_grad.astype(jnp.float32))
    input_grads = jnp.concatenate([grad_in[None], grad_mid[1:]], axis=0)
    return (shown, input_grads, grad_weights[0], grad_weights[1], grad_weights[2], grad_weights[3], grad_weights[4], grad_weights[5], grad_weights[6], grad_weights[7], grad_weights[8], grad_weights[9], grad_weights[10], grad_weights[11], grad_weights[12])
```

```python
from functools import partial

import jax
import jax.numpy as jnp
from jax import lax
from jax.experimental import pallas as pl
from jax.experimental.pallas import tpu as pltpu
from jax.sharding import PartitionSpec as P

HEADS = 12


SCALE = 0.125
EPS = 1e-05
MASKED = -1e30


def from_behind(x, axis, by):
    peers = lax.axis_size(axis)
    pairs = [(i, i + by) for i in range(peers) if 0 <= i + by < peers]
    return lax.ppermute(x, axis, pairs)


def norm_rows(values, gain_vec, bias_vec):
    centre = jnp.mean(values, axis=-1, keepdims=True)
    offset = values - centre
    spread = jnp.mean(offset * offset, axis=-1, keepdims=True)
    return offset * lax.rsqrt(spread + EPS) * gain_vec + bias_vec


def row_segments(lengths, row_length):
    limits = jnp.cumsum(lengths, axis=-1)
    places = jnp.arange(row_length, dtype=jnp.int32)
    return jnp.sum((places[None, :, None] >= limits[:, None, :]).astype(jnp.int32), axis=-1)


def split_heads(values):
    return values.reshape(values.shape[0], HEADS, values.shape[1] // HEADS)


def masked_scores(queries, keys_in, seg_query, seg_keys):
    scores = (
        jnp.einsum(
            "qhe,khe->hqk",
            split_heads(queries),
            split_heads(keys_in),
            preferred_element_type=jnp.float32,
        )
        * SCALE
    )
    return jnp.where((seg_query[:, None] == seg_keys[None, :])[None], scores, MASKED)


def softmax_parts(scores):
    highest = jnp.max(scores, axis=-1)
    raised = jnp.exp(scores - highest[..., None])
    summed = jnp.sum(raised, axis=-1)
    return (raised / summed[..., None], highest, summed)


def project_in(inputs, weights):
    normed = norm_rows(inputs, weights[0], weights[1]).astype(jnp.bfloat16)
    joined = jnp.dot(normed, weights[2], preferred_element_type=jnp.float32)
    model_width = inputs.shape[1]
    queries = (joined[:, :model_width] + weights[3]).astype(jnp.bfloat16)
    keys_out = joined[:, model_width : 2 * model_width].astype(jnp.bfloat16)
    values_out = (joined[:, 2 * model_width :] + weights[4]).astype(jnp.bfloat16)
    return (normed, queries, keys_out, values_out)


def attend(queries, keys_all, values_all, seg_own, seg_row):
    soft_probs, highest, summed = softmax_parts(masked_scores(queries, keys_all, seg_own, seg_row))
    low_probs = soft_probs.astype(jnp.bfloat16)
    combined = jnp.einsum(
        "hqk,khe->qhe", low_probs, split_heads(values_all), preferred_element_type=jnp.float32
    )
    return (
        combined.reshape(queries.shape).astype(jnp.bfloat16),
        soft_probs,
        low_probs,
        highest,
        summed,
    )


def finish(inputs, attended, weights):
    resid_sum = (
        inputs + jnp.dot(attended, weights[5], preferred_element_type=jnp.float32) + weights[6]
    )
    normed = norm_rows(resid_sum, weights[7], weights[8]).astype(jnp.bfloat16)
    hidden_pre = jnp.dot(normed, weights[9], preferred_element_type=jnp.float32) + weights[10]
    active = jax.nn.gelu(hidden_pre, approximate=False).astype(jnp.bfloat16)
    result = (
        resid_sum + jnp.dot(active, weights[11], preferred_element_type=jnp.float32) + weights[12]
    )
    return (result, resid_sum, normed, hidden_pre, active)


def store_slot(buffer, item_new, slot_idx, is_valid):
    current = lax.dynamic_index_in_dim(buffer, slot_idx, 0, keepdims=False)
    return lax.dynamic_update_index_in_dim(
        buffer, jnp.where(is_valid, item_new, current), slot_idx, 0
    )


def token_sum(values):
    return jnp.sum(values.astype(jnp.float32), axis=0)


def on_device(
    cell_tokens,
    cell_lengths,
    out_grad,
    norm1_gain,
    norm1_bias,
    qkv_weight,
    query_bias,
    value_bias,
    out_weight,
    out_bias,
    norm2_gain,
    norm2_bias,
    in_weight,
    in_bias,
    back_weight,
    back_bias,
):
    raw_weights = (
        norm1_gain,
        norm1_bias,
        qkv_weight,
        query_bias,
        value_bias,
        out_weight,
        out_bias,
        norm2_gain,
        norm2_bias,
        in_weight,
        in_bias,
        back_weight,
        back_bias,
    )
    weights = tuple(
        (weight[0].astype(jnp.float32) if weight.ndim == 2 else weight[0] for weight in raw_weights)
    )
    sections = lax.axis_size("section")
    section_rank = lax.axis_index("section")
    micro_count, local_len, model_width = cell_tokens.shape
    row_length = local_len * lax.axis_size("seq")
    own_start = lax.axis_index("seq") * local_len
    segments = row_segments(cell_lengths, row_length)
    tick_count = micro_count + sections - 1
    kept_depth = 1

    def row_segs(slot_idx):
        seg_row = lax.dynamic_index_in_dim(segments, slot_idx, 0, keepdims=False)
        return (seg_row, lax.dynamic_slice_in_dim(seg_row, own_start, local_len))

    def forward_tick(tick_now, state_now):
        incoming, kept_in, outputs, kept_keys, kept_values = state_now
        index_now = tick_now - section_rank
        is_valid = (index_now >= 0) & (index_now < micro_count)
        slot_idx = jnp.clip(index_now, 0, micro_count - 1)
        first_in = lax.dynamic_index_in_dim(cell_tokens, slot_idx, 0, keepdims=False)
        layer_in = jnp.where(section_rank == 0, first_in, incoming)
        seg_row, seg_own = row_segs(slot_idx)
        inputs = layer_in.astype(jnp.float32)
        normed, queries, keys_out, values_out = project_in(inputs, weights)
        keys_all, values_all = (
            lax.all_gather(keys_out, "seq", axis=0, tiled=True),
            lax.all_gather(values_out, "seq", axis=0, tiled=True),
        )
        attended = attend(queries, keys_all, values_all, seg_own, seg_row)[0]
        result = finish(inputs, attended, weights)[0].astype(jnp.bfloat16)
        kept_in = store_slot(kept_in, layer_in, slot_idx, is_valid)
        outputs = store_slot(outputs, result, slot_idx, is_valid)
        passed = from_behind(result, "section", 1)
        return (passed, kept_in, outputs, kept_keys, kept_values)

    start_state = (
        jnp.zeros((local_len, model_width), jnp.bfloat16),
        jnp.zeros((micro_count, local_len, model_width), jnp.bfloat16),
        jnp.zeros((micro_count, local_len, model_width), jnp.bfloat16),
        jnp.zeros((kept_depth, row_length, model_width), jnp.bfloat16),
        jnp.zeros((kept_depth, row_length, model_width), jnp.bfloat16),
    )
    ignored, kept_in, outputs, kept_keys, kept_values = lax.fori_loop(
        0, tick_count, forward_tick, start_state
    )

    def backward_tick(tick_now, state_now):
        incoming, in_grads, totals = state_now
        index_now = tick_now - (sections - 1 - section_rank)
        is_valid = (index_now >= 0) & (index_now < micro_count)
        slot_idx = jnp.clip(index_now, 0, micro_count - 1)
        from_out = lax.dynamic_index_in_dim(out_grad, slot_idx, 0, keepdims=False)
        grad_out = jnp.where(section_rank == sections - 1, from_out, incoming).astype(jnp.float32)
        inputs = lax.dynamic_index_in_dim(kept_in, slot_idx, 0, keepdims=False).astype(jnp.float32)
        seg_row, seg_own = row_segs(slot_idx)
        normed_one, queries, keys_out, values_out = project_in(inputs, weights)
        keys_all, values_all = (
            lax.all_gather(keys_out, "seq", axis=0, tiled=True),
            lax.all_gather(values_out, "seq", axis=0, tiled=True),
        )
        attended, soft_probs, low_probs, highest, summed = attend(
            queries, keys_all, values_all, seg_own, seg_row
        )
        result, resid_sum, normed_two, hidden_pre, active = finish(inputs, attended, weights)
        d_result = grad_out.astype(jnp.bfloat16)
        g_back_w = jnp.einsum("tf,td->fd", active, d_result, preferred_element_type=jnp.float32)
        g_back_b = token_sum(d_result)
        d_active = jnp.einsum(
            "td,fd->tf", d_result, weights[11], preferred_element_type=jnp.float32
        )
        gelu_value, gelu_back = jax.vjp(partial(jax.nn.gelu, approximate=False), hidden_pre)
        d_hidden = gelu_back(d_active)[0].astype(jnp.bfloat16)
        g_in_w = jnp.einsum("td,tf->df", normed_two, d_hidden, preferred_element_type=jnp.float32)
        g_in_b = token_sum(d_hidden)
        d_normed_two = jnp.einsum(
            "tf,df->td", d_hidden, weights[9], preferred_element_type=jnp.float32
        )
        norm_value, norm_two_back = jax.vjp(norm_rows, resid_sum, weights[7], weights[8])
        d_resid_norm, g_gain_two, g_bias_two = norm_two_back(d_normed_two)
        d_resid = grad_out + d_resid_norm
        d_proj = d_resid.astype(jnp.bfloat16)
        g_out_w = jnp.einsum("td,te->de", attended, d_proj, preferred_element_type=jnp.float32)
        g_out_b = token_sum(d_proj)
        d_attended = jnp.einsum(
            "te,de->td", d_proj, weights[5], preferred_element_type=jnp.float32
        ).astype(jnp.bfloat16)
        dout_heads = split_heads(d_attended)
        d_probs = jnp.einsum(
            "qhe,khe->hqk", dout_heads, split_heads(values_all), preferred_element_type=jnp.float32
        )
        delta_rows = jnp.sum(soft_probs * d_probs, axis=-1)
        d_scores = (soft_probs * (d_probs - delta_rows[..., None])).astype(jnp.bfloat16)
        d_query = (
            (
                jnp.einsum(
                    "hqk,khe->qhe",
                    d_scores,
                    split_heads(keys_all),
                    preferred_element_type=jnp.float32,
                )
                * SCALE
            )
            .reshape(local_len, model_width)
            .astype(jnp.bfloat16)
        )
        key_part = (
            jnp.einsum(
                "hqk,qhe->khe", d_scores, split_heads(queries), preferred_element_type=jnp.float32
            )
            * SCALE
        ).reshape(row_length, model_width)
        value_part = jnp.einsum(
            "hqk,qhe->khe", low_probs, dout_heads, preferred_element_type=jnp.float32
        ).reshape(row_length, model_width)
        d_keys, d_values = (
            lax.psum_scatter(
                key_part.astype(jnp.bfloat16), "seq", scatter_dimension=0, tiled=True
            ).astype(jnp.float32),
            lax.psum_scatter(
                value_part.astype(jnp.bfloat16), "seq", scatter_dimension=0, tiled=True
            ).astype(jnp.float32),
        )
        d_values_low = d_values.astype(jnp.bfloat16)
        d_joined = jnp.concatenate([d_query, d_keys.astype(jnp.bfloat16), d_values_low], axis=1)
        g_qkv_w = jnp.einsum("td,tf->df", normed_one, d_joined, preferred_element_type=jnp.float32)
        g_q_b = token_sum(d_query)
        g_v_b = token_sum(d_values_low)
        d_normed_one = jnp.einsum(
            "tf,df->td", d_joined, weights[2], preferred_element_type=jnp.float32
        )
        norm_value_one, norm_one_back = jax.vjp(norm_rows, inputs, weights[0], weights[1])
        d_inputs_norm, g_gain_one, g_bias_one = norm_one_back(d_normed_one)
        d_inputs = d_resid + d_inputs_norm
        new_grads = (
            g_gain_one,
            g_bias_one,
            g_qkv_w,
            g_q_b,
            g_v_b,
            g_out_w,
            g_out_b,
            g_gain_two,
            g_bias_two,
            g_in_w,
            g_in_b,
            g_back_w,
            g_back_b,
        )
        totals = tuple(
            (
                running + jnp.where(is_valid, grad_new, 0.0)
                for running, grad_new in zip(totals, new_grads)
            )
        )
        shown = jnp.where(
            section_rank == 0, d_inputs, d_inputs.astype(jnp.bfloat16).astype(jnp.float32)
        )
        in_grads = store_slot(in_grads, shown, slot_idx, is_valid)
        passed = from_behind(d_inputs.astype(jnp.bfloat16), "section", -1)
        return (passed, in_grads, totals)

    back_state = (
        jnp.zeros((local_len, model_width), jnp.bfloat16),
        jnp.zeros((micro_count, local_len, model_width), jnp.float32),
        tuple((jnp.zeros(weight.shape, jnp.float32) for weight in weights)),
    )
    ignored_grad, in_grads, totals = lax.fori_loop(0, tick_count, backward_tick, back_state)
    reduced = lax.psum_scatter(totals, ("dp", "seq"), scatter_dimension=0, tiled=True)
    return (
        outputs[None],
        in_grads[None],
        reduced[0][None],
        reduced[1][None],
        reduced[2][None],
        reduced[3][None],
        reduced[4][None],
        reduced[5][None],
        reduced[6][None],
        reduced[7][None],
        reduced[8][None],
        reduced[9][None],
        reduced[10][None],
        reduced[11][None],
        reduced[12][None],
    )


HEAD = 64
BIG = 1e30
NT = (((1,), (1,)), ((), ()))
F32 = jnp.float32
BF16 = jnp.bfloat16
BLK = 256
CH = 256
UN = 4

def lane_mask(shape, h):
    lane = lax.broadcasted_iota(jnp.int32, shape, len(shape) - 1)
    return (lane < HEAD) if h == 0 else (lane >= HEAD)

def only(x, h):
    return jnp.where(lane_mask(x.shape, h), x, jnp.zeros_like(x))

def fwd_kernel(lo_ref, hi_ref, q_ref, k_ref, v_ref, fq_ref, fk_ref, o_ref, lse_ref, kaug, vaug):
    i = pl.program_id(0)
    n = k_ref.shape[0]
    pairs = k_ref.shape[1] // 128
    @pl.when(i == 0)
    def _():
        for p in range(pairs):
            kaug[p, :, :128] = k_ref[:, p * 128:(p + 1) * 128]
            kaug[p, :, 128:] = fk_ref[...]
            vaug[p, :, :128] = v_ref[:, p * 128:(p + 1) * 128]
            vaug[p, :, 128:] = jnp.ones((n, 128), BF16)
    lo = lo_ref[i]
    count = hi_ref[i] - lo

    def run(c):
        fq = fq_ref[...]
        rows = pl.ds(pl.multiple_of(lo * BLK, BLK), c * BLK)
        for p in range(pairs):
            cols = slice(p * 128, (p + 1) * 128)
            q = q_ref[:, cols] * jnp.asarray(SCALE, BF16)
            kb = kaug[p, rows, :]
            vb = vaug[p, rows, :]
            outs = []
            lses = []
            for h in range(2):
                qa = jnp.concatenate([only(q, h), fq], axis=1)
                s = lax.dot_general(qa, kb, NT, preferred_element_type=F32)
                m = jnp.max(s, axis=1, keepdims=True)
                pr = jnp.exp(s - m).astype(BF16)
                r = jnp.dot(pr, vb, preferred_element_type=F32)
                l = r[:, 128:]
                outs.append(r[:, :128] / l)
                lses.append(m + jnp.log(l))
            mask = lane_mask(q.shape, 0)
            o_ref[:, cols] = jnp.where(mask, outs[0], outs[1]).astype(BF16)
            lse_ref[:, cols] = jnp.where(mask, lses[0], lses[1])

    for c in range(1, n // BLK + 1):
        @pl.when(count == c)
        def _(c=c):
            run(c)

def attn_fwd(lo, hi, q, k, v, fq, fk):
    n, w = q.shape
    pairs = w // 128
    blk = lambda i, lo, hi: (i, 0)
    full = lambda i, lo, hi: (0, 0)
    return pl.pallas_call(
        fwd_kernel,
        grid_spec=pltpu.PrefetchScalarGridSpec(
            num_scalar_prefetch=2,
            grid=(n // BLK,),
            in_specs=[pl.BlockSpec((BLK, w), blk), pl.BlockSpec((n, w), full), pl.BlockSpec((n, w), full),
                      pl.BlockSpec((BLK, 128), blk), pl.BlockSpec((n, 128), full)],
            out_specs=[pl.BlockSpec((BLK, w), blk), pl.BlockSpec((BLK, w), blk)],
            scratch_shapes=[pltpu.VMEM((pairs, n, 256), BF16), pltpu.VMEM((pairs, n, 256), BF16)],
        ),
        out_shape=[jax.ShapeDtypeStruct((n, w), BF16), jax.ShapeDtypeStruct((n, w), F32)],
        compiler_params=pltpu.CompilerParams(vmem_limit_bytes=56 * 2 ** 20),
        name="attn_fwd",
    )(lo, hi, q, k, v, fq, fk)

def bwd_kernel(lo_ref, hi_ref, q_ref, k_ref, v_ref, do_ref, o_ref, lse_ref, fq_ref, fk_ref,
               dq_ref, dk_ref, dv_ref, qaug, dom, stat, dqt, dk_acc, dv_acc):
    j = pl.program_id(0)
    nb = pl.num_programs(0)
    n, w = q_ref.shape
    pairs = w // 128

    @pl.when(j == 0)
    def _():
        def prep(b, c):
            rows = pl.ds(pl.multiple_of(b * CH, CH), CH)
            for p in range(pairs):
                cols = slice(p * 128, (p + 1) * 128)
                q = q_ref[rows, cols] * jnp.asarray(SCALE, BF16)
                do = do_ref[rows, cols]
                prod = do.astype(F32) * o_ref[rows, cols].astype(F32)
                lt = lse_ref[rows, cols].T
                hi = prod.astype(BF16)
                lo = (prod - hi.astype(F32)).astype(BF16)
                for h in range(2):
                    qaug[2 * p + h, rows, :128] = only(q, h)
                    qaug[2 * p + h, rows, 128:] = fq_ref[rows, :]
                    dom[2 * p + h, rows, :] = only(do, h)
                    sel = lane_mask((16, 128), h).astype(F32).astype(BF16)
                    d = lax.dot_general(sel, hi, NT, preferred_element_type=F32) + lax.dot_general(sel, lo, NT, preferred_element_type=F32)
                    stat[p, h:h + 1, rows] = d[0:1, :]
                    stat[p, 2 + h:3 + h, rows] = lt[h * HEAD:h * HEAD + 1, :]
                dqt[p, :, rows] = jnp.zeros((128, CH), F32)
            return c
        lax.fori_loop(0, n // CH, prep, 0)

    lo = lo_ref[j]
    count = hi_ref[j] - lo
    dk_acc[...] = jnp.zeros_like(dk_acc)
    dv_acc[...] = jnp.zeros_like(dv_acc)

    def run(first, c):
        rows = pl.ds(pl.multiple_of(first * BLK, BLK), c * BLK)
        fk = fk_ref[...]
        for p in range(pairs):
            cols = slice(p * 128, (p + 1) * 128)
            kp = k_ref[:, cols]
            kb = jnp.concatenate([kp, fk], axis=1)
            ktb = kp.T
            vb = v_ref[:, cols]
            dk = dk_acc[:, cols]
            dv = dv_acc[:, cols]
            for h in range(2):
                qa = qaug[2 * p + h, rows, :]
                do = dom[2 * p + h, rows, :]
                s = lax.dot_general(kb, qa, NT, preferred_element_type=F32)
                dp = lax.dot_general(vb, do, NT, preferred_element_type=F32)
                pr = jnp.exp(s - stat[p, 2 + h:3 + h, rows])
                ds = (pr * (dp - stat[p, h:h + 1, rows])).astype(BF16)
                dv = dv + jnp.dot(pr.astype(BF16), do, preferred_element_type=F32)
                dk = dk + jnp.dot(ds, qa[:, :128], preferred_element_type=F32)
                dqt[p, h * HEAD:(h + 1) * HEAD, rows] += jnp.dot(ktb[h * HEAD:(h + 1) * HEAD, :], ds, preferred_element_type=F32)
            dk_acc[:, cols] = dk
            dv_acc[:, cols] = dv

    @pl.loop(0, count // UN)
    def _(t):
        run(lo + t * UN, UN)

    left = count % UN
    for c in range(1, UN):
        @pl.when(left == c)
        def _(c=c):
            run(lo + (count - left), c)
    dk_ref[...] = dk_acc[...].astype(BF16)
    dv_ref[...] = dv_acc[...].astype(BF16)

    @pl.when(j == nb - 1)
    def _():
        def fin(b, c):
            rows = pl.ds(pl.multiple_of(b * CH, CH), CH)
            for p in range(pairs):
                dq_ref[rows, p * 128:(p + 1) * 128] = (dqt[p, :, rows] * SCALE).T.astype(BF16)
            return c
        lax.fori_loop(0, n // CH, fin, 0)

def attn_bwd(lo, hi, q, k, v, do, o, lse, fq, fk):
    n, w = q.shape
    pairs = w // 128
    full = lambda j, lo, hi: (0, 0)
    blk = lambda j, lo, hi: (j, 0)
    sh = jax.ShapeDtypeStruct((n, w), BF16)
    big = pl.BlockSpec((n, w), full, pipeline_mode=pl.Buffered(1))
    return pl.pallas_call(
        bwd_kernel,
        grid_spec=pltpu.PrefetchScalarGridSpec(
            num_scalar_prefetch=2,
            grid=(n // BLK,),
            in_specs=[big, pl.BlockSpec((BLK, w), blk), pl.BlockSpec((BLK, w), blk), big, big, big,
                      pl.BlockSpec((n, 128), full), pl.BlockSpec((BLK, 128), blk)],
            out_specs=[pl.BlockSpec((n, w), full), pl.BlockSpec((BLK, w), blk), pl.BlockSpec((BLK, w), blk)],
            scratch_shapes=[
                pltpu.VMEM((2 * pairs, n, 256), BF16),
                pltpu.VMEM((2 * pairs, n, 128), BF16),
                pltpu.VMEM((pairs, 8, n), F32),
                pltpu.VMEM((pairs, 128, n), F32),
                pltpu.VMEM((BLK, w), F32),
                pltpu.VMEM((BLK, w), F32),
            ],
        ),
        out_shape=[sh, sh, sh],
        compiler_params=pltpu.CompilerParams(vmem_limit_bytes=60 * 2 ** 20),
        name="attn_bwd",
    )(lo, hi, q, k, v, do, o, lse, fq, fk)

def seg_info(lengths, n):
    ends = jnp.cumsum(lengths)
    pos = jnp.arange(n, dtype=jnp.int32)
    seg = jnp.sum((pos[:, None] >= ends[None, :]).astype(jnp.int32), axis=-1)
    cells = lengths.shape[0]
    lane = jnp.arange(128, dtype=jnp.int32)
    hot = seg[:, None] == lane[None, :]
    fq = jnp.where(hot, -BIG, 0.0).astype(BF16)
    fk = jnp.where((~hot) & (lane < cells)[None, :], 1.0, 0.0).astype(BF16)
    first = jnp.arange(n // BLK, dtype=jnp.int32) * BLK
    last = first + BLK - 1
    starts = ends - lengths
    lo = jnp.max(jnp.where(starts[None, :] <= first[:, None], starts[None, :], 0), axis=1) // BLK
    hi = (jnp.min(jnp.where(ends[None, :] > last[:, None], ends[None, :], n), axis=1) + BLK - 1) // BLK
    return seg, fq, fk, lo.astype(jnp.int32), hi.astype(jnp.int32)


def swap_cores(x):
    size = lax.axis_size("dp")
    return lax.ppermute(x, "dp", [(i, i ^ 1) for i in range(size)])


def row_moves(rows_each, back):
    n_dp, n_seq = lax.axis_size("dp"), lax.axis_size("seq")
    steps = []
    for k in range(rows_each):
        pairs = []
        for d in range(n_dp):
            for z in range(n_seq):
                m = (z + k) % rows_each
                to = (2 * (d // 2) + z // rows_each) * n_seq + (d % 2) * rows_each + m
                pairs.append((to, d * n_seq + z) if back else (d * n_seq + z, to))
        steps.append(pairs)
    return steps


def to_rows(x):
    rows_each, local, width = x.shape
    z = lax.axis_index("seq")
    out = jnp.zeros((rows_each, local, width), x.dtype)
    for k, pairs in enumerate(row_moves(rows_each, False)):
        block = lax.dynamic_index_in_dim(x, (z + k) % rows_each, 0, keepdims=False)
        got = lax.ppermute(block, ("dp", "seq"), pairs)
        out = lax.dynamic_update_index_in_dim(out, got, (z - k) % rows_each, 0)
    return out.reshape(rows_each * local, width)


def from_rows(x, rows_each):
    z = lax.axis_index("seq")
    parts = x.reshape(rows_each, x.shape[0] // rows_each, x.shape[1])
    out = jnp.zeros(parts.shape, x.dtype)
    for k, pairs in enumerate(row_moves(rows_each, True)):
        block = lax.dynamic_index_in_dim(parts, (z - k) % rows_each, 0, keepdims=False)
        got = lax.ppermute(block, ("dp", "seq"), pairs)
        out = lax.dynamic_update_index_in_dim(out, got, (z + k) % rows_each, 0)
    return out


def heads_in(parts):
    core = lax.axis_index("dp") % 2
    half = parts[0].shape[1] // 2
    tokens = parts[0].shape[0]
    send = jnp.concatenate(
        [lax.dynamic_slice_in_dim(p, (1 - core) * half, half, 1) for p in parts], axis=1
    )
    got = swap_cores(send)
    outs = []
    for i, p in enumerate(parts):
        own = lax.dynamic_slice_in_dim(p, core * half, half, 1)
        full = jnp.zeros((2 * tokens, half), p.dtype)
        full = lax.dynamic_update_slice_in_dim(full, own, core * tokens, 0)
        full = lax.dynamic_update_slice_in_dim(
            full, got[:, i * half : (i + 1) * half], (1 - core) * tokens, 0
        )
        outs.append(full)
    return outs


def heads_out(parts):
    core = lax.axis_index("dp") % 2
    tokens, half = parts[0].shape[0] // 2, parts[0].shape[1]
    send = jnp.concatenate(
        [lax.dynamic_slice_in_dim(p, (1 - core) * tokens, tokens, 0) for p in parts], axis=1
    )
    got = swap_cores(send)
    outs = []
    for i, p in enumerate(parts):
        own = lax.dynamic_slice_in_dim(p, core * tokens, tokens, 0)
        full = jnp.zeros((tokens, 2 * half), p.dtype)
        full = lax.dynamic_update_slice_in_dim(full, own, core * half, 1)
        full = lax.dynamic_update_slice_in_dim(
            full, got[:, i * half : (i + 1) * half], (1 - core) * half, 1
        )
        outs.append(full)
    return outs


def norm_stats(values):
    centre = jnp.mean(values, axis=-1, keepdims=True)
    offset = values - centre
    spread = jnp.mean(offset * offset, axis=-1, keepdims=True)
    rstd = lax.rsqrt(spread + EPS)
    return offset * rstd, rstd


def norm_back(grad, hat, rstd, gain):
    d_hat = grad * gain
    mean_d = jnp.mean(d_hat, axis=-1, keepdims=True)
    mean_dh = jnp.mean(d_hat * hat, axis=-1, keepdims=True)
    return rstd * (d_hat - mean_d - hat * mean_dh)


def row_forward(x, weights, info):
    fq, fk, lo, hi = info
    inputs = x.astype(F32)
    normed, queries, keys_out, values_out = project_in(inputs, weights)
    q, k, v = heads_in([queries, keys_out, values_out])
    o, lse = attn_fwd(lo, hi, q, k, v, fq, fk)
    (attended,) = heads_out([o])
    resid = inputs + jnp.dot(attended, weights[5], preferred_element_type=F32) + weights[6]
    hat, rstd = norm_stats(resid)
    c = (hat * weights[7] + weights[8]).astype(BF16)
    inner = jnp.dot(c, weights[9], preferred_element_type=F32) + weights[10]
    phi = 0.5 * (1.0 + lax.erf(inner * 0.7071067811865476))
    slope = (phi + inner * jnp.exp(-0.5 * inner * inner) * 0.3989422804014327).astype(BF16)
    active = (inner * phi).astype(BF16)
    y = (resid + jnp.dot(active, weights[11], preferred_element_type=F32) + weights[12]).astype(BF16)
    return y, (x, normed, q, k, v, o, lse, attended, resid, c, active, slope)


def row_backward(grad, weights, kept, info):
    fq, fk, lo, hi = info
    x, normed, q, k, v, o, lse, attended, resid, c, active, slope = kept
    dy = grad
    d_active = lax.dot_general(dy, weights[11], NT, preferred_element_type=F32)
    d_inner = (d_active * slope.astype(F32)).astype(BF16)
    d_c = lax.dot_general(d_inner, weights[9], NT, preferred_element_type=F32)
    hat2, rstd2 = norm_stats(resid)
    d_resid = dy.astype(F32) + norm_back(d_c, hat2, rstd2, weights[7])
    d_proj = d_resid.astype(BF16)
    d_att = lax.dot_general(d_proj, weights[5], NT, preferred_element_type=F32).astype(BF16)
    (do,) = heads_in([d_att])
    dqh, dkh, dvh = attn_bwd(lo, hi, q, k, v, do, o, lse, fq, fk)
    d_q, d_k, d_v = heads_out([dqh, dkh, dvh])
    d_joined = jnp.concatenate([d_q, d_k, d_v], axis=1)
    d_a = lax.dot_general(d_joined, weights[2], NT, preferred_element_type=F32)
    hat1, rstd1 = norm_stats(x.astype(F32))
    d_x = d_resid + norm_back(d_a, hat1, rstd1, weights[0])

    def totals():
        tt = lambda a, b: lax.dot_general(a, b, (((0,), (0,)), ((), ())), preferred_element_type=F32)
        big = (tt(normed, d_joined), tt(attended, d_proj), tt(c, d_inner), tt(active, dy))
        small = (
            jnp.sum(d_a * hat1, axis=0),
            jnp.sum(d_a, axis=0),
            token_sum(d_q),
            token_sum(d_v),
            token_sum(d_proj),
            jnp.sum(d_c * hat2, axis=0),
            jnp.sum(d_c, axis=0),
            token_sum(d_inner),
            token_sum(dy),
        )
        return big, small

    return d_x, totals


def on_device_rows(cell_tokens, cell_lengths, out_grad, *raw_weights):
    weights = tuple(
        (w[0].astype(jnp.float32) if w.ndim == 2 else w[0] for w in raw_weights)
    )
    sections = lax.axis_size("section")
    section = lax.axis_index("section")
    rows_each, local, width = cell_tokens.shape
    row_length = local * lax.axis_size("seq")
    core = lax.axis_index("dp") % 2
    z = lax.axis_index("seq")

    x0 = to_rows(cell_tokens)
    lengths = jnp.where(z // rows_each == core, cell_lengths, swap_cores(cell_lengths))
    lengths = lax.dynamic_index_in_dim(lengths, z % rows_each, 0, keepdims=False)
    info = seg_info(lengths, row_length)[1:]

    x = x0
    for t in range(sections):
        y, kept = row_forward(x, weights, info)
        if t + 1 < sections:
            x = jnp.where(section == 0, x0, from_behind(y, "section", 1))
    outputs = from_rows(y, rows_each)

    g0 = to_rows(out_grad)
    grad = g0
    for t in range(sections):
        d_x, totals = row_backward(grad, weights, kept, info)
        if t + 1 < sections:
            passed = from_behind(d_x.astype(BF16), "section", -1)
            grad = jnp.where(section == sections - 1, g0, passed)
    in_grads = from_rows(d_x.astype(BF16), rows_each).astype(F32)

    big, small = totals()
    parts = lax.axis_size("dp") * lax.axis_size("seq")
    axes = ("dp", "seq")
    big = [
        lax.psum_scatter(w.astype(BF16), axes, scatter_dimension=0, tiled=True).astype(F32)
        for w in big
    ]
    joined = jnp.concatenate([s.reshape(parts, -1) for s in small], axis=1)
    joined = lax.psum_scatter(joined, axes, scatter_dimension=0, tiled=True)[0]
    shares, at = [], 0
    for s in small:
        size = s.shape[0] // parts
        shares.append(joined[at : at + size])
        at += size
    return (
        outputs[None],
        in_grads[None],
        shares[0][None],
        shares[1][None],
        big[0][None],
        shares[2][None],
        shares[3][None],
        big[1][None],
        shares[4][None],
        shares[5][None],
        shares[6][None],
        big[2][None],
        shares[7][None],
        big[3][None],
        shares[8][None],
    )


def either_plan(cell_tokens, *others):
    one_chip = lax.axis_size("dp") % 2 == 0 and lax.axis_size("seq") == 2 * cell_tokens.shape[0]
    return (on_device_rows if one_chip else on_device)(cell_tokens, *others)


def solution(mesh):
    in_specs = (
        P("dp", "seq", None),
        P("dp", None),
        P("dp", "seq", None),
        P("section", None),
        P("section", None),
        P("section", None, None),
        P("section", None),
        P("section", None),
        P("section", None, None),
        P("section", None),
        P("section", None),
        P("section", None),
        P("section", None, None),
        P("section", None),
        P("section", None, None),
        P("section", None),
    )
    out_specs = (
        P("section", "dp", "seq", None),
        P("section", "dp", "seq", None),
        P("section", ("dp", "seq")),
        P("section", ("dp", "seq")),
        P("section", ("dp", "seq"), None),
        P("section", ("dp", "seq")),
        P("section", ("dp", "seq")),
        P("section", ("dp", "seq"), None),
        P("section", ("dp", "seq")),
        P("section", ("dp", "seq")),
        P("section", ("dp", "seq")),
        P("section", ("dp", "seq"), None),
        P("section", ("dp", "seq")),
        P("section", ("dp", "seq"), None),
        P("section", ("dp", "seq")),
    )
    return jax.shard_map(
        either_plan, mesh=mesh, in_specs=in_specs, out_specs=out_specs, check_vma=False
    )
```

```python
from functools import partial

import jax
import jax.numpy as jnp
from jax import lax
from jax.experimental import pallas as pl
from jax.experimental.pallas import tpu as pltpu
from jax.sharding import PartitionSpec as P

HEADS = 12


SCALE = 0.125
EPS = 1e-05
MASKED = -1e30


def from_behind(x, axis, by):
    peers = lax.axis_size(axis)
    pairs = [(i, i + by) for i in range(peers) if 0 <= i + by < peers]
    return lax.ppermute(x, axis, pairs)


def norm_rows(values, gain_vec, bias_vec):
    centre = jnp.mean(values, axis=-1, keepdims=True)
    offset = values - centre
    spread = jnp.mean(offset * offset, axis=-1, keepdims=True)
    return offset * lax.rsqrt(spread + EPS) * gain_vec + bias_vec


def row_segments(lengths, row_length):
    limits = jnp.cumsum(lengths, axis=-1)
    places = jnp.arange(row_length, dtype=jnp.int32)
    return jnp.sum((places[None, :, None] >= limits[:, None, :]).astype(jnp.int32), axis=-1)


def split_heads(values):
    return values.reshape(values.shape[0], HEADS, values.shape[1] // HEADS)


def masked_scores(queries, keys_in, seg_query, seg_keys):
    scores = (
        jnp.einsum(
            "qhe,khe->hqk",
            split_heads(queries),
            split_heads(keys_in),
            preferred_element_type=jnp.float32,
        )
        * SCALE
    )
    return jnp.where((seg_query[:, None] == seg_keys[None, :])[None], scores, MASKED)


def softmax_parts(scores):
    highest = jnp.max(scores, axis=-1)
    raised = jnp.exp(scores - highest[..., None])
    summed = jnp.sum(raised, axis=-1)
    return (raised / summed[..., None], highest, summed)


def project_in(inputs, weights):
    normed = norm_rows(inputs, weights[0], weights[1]).astype(jnp.bfloat16)
    joined = jnp.dot(normed, weights[2], preferred_element_type=jnp.float32)
    model_width = inputs.shape[1]
    queries = (joined[:, :model_width] + weights[3]).astype(jnp.bfloat16)
    keys_out = joined[:, model_width : 2 * model_width].astype(jnp.bfloat16)
    values_out = (joined[:, 2 * model_width :] + weights[4]).astype(jnp.bfloat16)
    return (normed, queries, keys_out, values_out)


def attend(queries, keys_all, values_all, seg_own, seg_row):
    soft_probs, highest, summed = softmax_parts(masked_scores(queries, keys_all, seg_own, seg_row))
    low_probs = soft_probs.astype(jnp.bfloat16)
    combined = jnp.einsum(
        "hqk,khe->qhe", low_probs, split_heads(values_all), preferred_element_type=jnp.float32
    )
    return (
        combined.reshape(queries.shape).astype(jnp.bfloat16),
        soft_probs,
        low_probs,
        highest,
        summed,
    )


def finish(inputs, attended, weights):
    resid_sum = (
        inputs + jnp.dot(attended, weights[5], preferred_element_type=jnp.float32) + weights[6]
    )
    normed = norm_rows(resid_sum, weights[7], weights[8]).astype(jnp.bfloat16)
    hidden_pre = jnp.dot(normed, weights[9], preferred_element_type=jnp.float32) + weights[10]
    active = jax.nn.gelu(hidden_pre, approximate=False).astype(jnp.bfloat16)
    result = (
        resid_sum + jnp.dot(active, weights[11], preferred_element_type=jnp.float32) + weights[12]
    )
    return (result, resid_sum, normed, hidden_pre, active)


def store_slot(buffer, item_new, slot_idx, is_valid):
    current = lax.dynamic_index_in_dim(buffer, slot_idx, 0, keepdims=False)
    return lax.dynamic_update_index_in_dim(
        buffer, jnp.where(is_valid, item_new, current), slot_idx, 0
    )


def token_sum(values):
    return jnp.sum(values.astype(jnp.float32), axis=0)


def on_device(
    cell_tokens,
    cell_lengths,
    out_grad,
    norm1_gain,
    norm1_bias,
    qkv_weight,
    query_bias,
    value_bias,
    out_weight,
    out_bias,
    norm2_gain,
    norm2_bias,
    in_weight,
    in_bias,
    back_weight,
    back_bias,
):
    raw_weights = (
        norm1_gain,
        norm1_bias,
        qkv_weight,
        query_bias,
        value_bias,
        out_weight,
        out_bias,
        norm2_gain,
        norm2_bias,
        in_weight,
        in_bias,
        back_weight,
        back_bias,
    )
    weights = tuple(
        (weight[0].astype(jnp.float32) if weight.ndim == 2 else weight[0] for weight in raw_weights)
    )
    sections = lax.axis_size("section")
    section_rank = lax.axis_index("section")
    micro_count, local_len, model_width = cell_tokens.shape
    row_length = local_len * lax.axis_size("seq")
    own_start = lax.axis_index("seq") * local_len
    segments = row_segments(cell_lengths, row_length)
    tick_count = micro_count + sections - 1
    kept_depth = 1

    def row_segs(slot_idx):
        seg_row = lax.dynamic_index_in_dim(segments, slot_idx, 0, keepdims=False)
        return (seg_row, lax.dynamic_slice_in_dim(seg_row, own_start, local_len))

    def forward_tick(tick_now, state_now):
        incoming, kept_in, outputs, kept_keys, kept_values = state_now
        index_now = tick_now - section_rank
        is_valid = (index_now >= 0) & (index_now < micro_count)
        slot_idx = jnp.clip(index_now, 0, micro_count - 1)
        first_in = lax.dynamic_index_in_dim(cell_tokens, slot_idx, 0, keepdims=False)
        layer_in = jnp.where(section_rank == 0, first_in, incoming)
        seg_row, seg_own = row_segs(slot_idx)
        inputs = layer_in.astype(jnp.float32)
        normed, queries, keys_out, values_out = project_in(inputs, weights)
        keys_all, values_all = (
            lax.all_gather(keys_out, "seq", axis=0, tiled=True),
            lax.all_gather(values_out, "seq", axis=0, tiled=True),
        )
        attended = attend(queries, keys_all, values_all, seg_own, seg_row)[0]
        result = finish(inputs, attended, weights)[0].astype(jnp.bfloat16)
        kept_in = store_slot(kept_in, layer_in, slot_idx, is_valid)
        outputs = store_slot(outputs, result, slot_idx, is_valid)
        passed = from_behind(result, "section", 1)
        return (passed, kept_in, outputs, kept_keys, kept_values)

    start_state = (
        jnp.zeros((local_len, model_width), jnp.bfloat16),
        jnp.zeros((micro_count, local_len, model_width), jnp.bfloat16),
        jnp.zeros((micro_count, local_len, model_width), jnp.bfloat16),
        jnp.zeros((kept_depth, row_length, model_width), jnp.bfloat16),
        jnp.zeros((kept_depth, row_length, model_width), jnp.bfloat16),
    )
    ignored, kept_in, outputs, kept_keys, kept_values = lax.fori_loop(
        0, tick_count, forward_tick, start_state
    )

    def backward_tick(tick_now, state_now):
        incoming, in_grads, totals = state_now
        index_now = tick_now - (sections - 1 - section_rank)
        is_valid = (index_now >= 0) & (index_now < micro_count)
        slot_idx = jnp.clip(index_now, 0, micro_count - 1)
        from_out = lax.dynamic_index_in_dim(out_grad, slot_idx, 0, keepdims=False)
        grad_out = jnp.where(section_rank == sections - 1, from_out, incoming).astype(jnp.float32)
        inputs = lax.dynamic_index_in_dim(kept_in, slot_idx, 0, keepdims=False).astype(jnp.float32)
        seg_row, seg_own = row_segs(slot_idx)
        normed_one, queries, keys_out, values_out = project_in(inputs, weights)
        keys_all, values_all = (
            lax.all_gather(keys_out, "seq", axis=0, tiled=True),
            lax.all_gather(values_out, "seq", axis=0, tiled=True),
        )
        attended, soft_probs, low_probs, highest, summed = attend(
            queries, keys_all, values_all, seg_own, seg_row
        )
        result, resid_sum, normed_two, hidden_pre, active = finish(inputs, attended, weights)
        d_result = grad_out.astype(jnp.bfloat16)
        g_back_w = jnp.einsum("tf,td->fd", active, d_result, preferred_element_type=jnp.float32)
        g_back_b = token_sum(d_result)
        d_active = jnp.einsum(
            "td,fd->tf", d_result, weights[11], preferred_element_type=jnp.float32
        )
        gelu_value, gelu_back = jax.vjp(partial(jax.nn.gelu, approximate=False), hidden_pre)
        d_hidden = gelu_back(d_active)[0].astype(jnp.bfloat16)
        g_in_w = jnp.einsum("td,tf->df", normed_two, d_hidden, preferred_element_type=jnp.float32)
        g_in_b = token_sum(d_hidden)
        d_normed_two = jnp.einsum(
            "tf,df->td", d_hidden, weights[9], preferred_element_type=jnp.float32
        )
        norm_value, norm_two_back = jax.vjp(norm_rows, resid_sum, weights[7], weights[8])
        d_resid_norm, g_gain_two, g_bias_two = norm_two_back(d_normed_two)
        d_resid = grad_out + d_resid_norm
        d_proj = d_resid.astype(jnp.bfloat16)
        g_out_w = jnp.einsum("td,te->de", attended, d_proj, preferred_element_type=jnp.float32)
        g_out_b = token_sum(d_proj)
        d_attended = jnp.einsum(
            "te,de->td", d_proj, weights[5], preferred_element_type=jnp.float32
        ).astype(jnp.bfloat16)
        dout_heads = split_heads(d_attended)
        d_probs = jnp.einsum(
            "qhe,khe->hqk", dout_heads, split_heads(values_all), preferred_element_type=jnp.float32
        )
        delta_rows = jnp.sum(soft_probs * d_probs, axis=-1)
        d_scores = (soft_probs * (d_probs - delta_rows[..., None])).astype(jnp.bfloat16)
        d_query = (
            (
                jnp.einsum(
                    "hqk,khe->qhe",
                    d_scores,
                    split_heads(keys_all),
                    preferred_element_type=jnp.float32,
                )
                * SCALE
            )
            .reshape(local_len, model_width)
            .astype(jnp.bfloat16)
        )
        key_part = (
            jnp.einsum(
                "hqk,qhe->khe", d_scores, split_heads(queries), preferred_element_type=jnp.float32
            )
            * SCALE
        ).reshape(row_length, model_width)
        value_part = jnp.einsum(
            "hqk,qhe->khe", low_probs, dout_heads, preferred_element_type=jnp.float32
        ).reshape(row_length, model_width)
        d_keys, d_values = (
            lax.psum_scatter(
                key_part.astype(jnp.bfloat16), "seq", scatter_dimension=0, tiled=True
            ).astype(jnp.float32),
            lax.psum_scatter(
                value_part.astype(jnp.bfloat16), "seq", scatter_dimension=0, tiled=True
            ).astype(jnp.float32),
        )
        d_values_low = d_values.astype(jnp.bfloat16)
        d_joined = jnp.concatenate([d_query, d_keys.astype(jnp.bfloat16), d_values_low], axis=1)
        g_qkv_w = jnp.einsum("td,tf->df", normed_one, d_joined, preferred_element_type=jnp.float32)
        g_q_b = token_sum(d_query)
        g_v_b = token_sum(d_values_low)
        d_normed_one = jnp.einsum(
            "tf,df->td", d_joined, weights[2], preferred_element_type=jnp.float32
        )
        norm_value_one, norm_one_back = jax.vjp(norm_rows, inputs, weights[0], weights[1])
        d_inputs_norm, g_gain_one, g_bias_one = norm_one_back(d_normed_one)
        d_inputs = d_resid + d_inputs_norm
        new_grads = (
            g_gain_one,
            g_bias_one,
            g_qkv_w,
            g_q_b,
            g_v_b,
            g_out_w,
            g_out_b,
            g_gain_two,
            g_bias_two,
            g_in_w,
            g_in_b,
            g_back_w,
            g_back_b,
        )
        totals = tuple(
            (
                running + jnp.where(is_valid, grad_new, 0.0)
                for running, grad_new in zip(totals, new_grads)
            )
        )
        shown = jnp.where(
            section_rank == 0, d_inputs, d_inputs.astype(jnp.bfloat16).astype(jnp.float32)
        )
        in_grads = store_slot(in_grads, shown, slot_idx, is_valid)
        passed = from_behind(d_inputs.astype(jnp.bfloat16), "section", -1)
        return (passed, in_grads, totals)

    back_state = (
        jnp.zeros((local_len, model_width), jnp.bfloat16),
        jnp.zeros((micro_count, local_len, model_width), jnp.float32),
        tuple((jnp.zeros(weight.shape, jnp.float32) for weight in weights)),
    )
    ignored_grad, in_grads, totals = lax.fori_loop(0, tick_count, backward_tick, back_state)
    reduced = lax.psum_scatter(totals, ("dp", "seq"), scatter_dimension=0, tiled=True)
    return (
        outputs[None],
        in_grads[None],
        reduced[0][None],
        reduced[1][None],
        reduced[2][None],
        reduced[3][None],
        reduced[4][None],
        reduced[5][None],
        reduced[6][None],
        reduced[7][None],
        reduced[8][None],
        reduced[9][None],
        reduced[10][None],
        reduced[11][None],
        reduced[12][None],
    )


HEAD = 64
BIG = 1e30
NT = (((1,), (1,)), ((), ()))
F32 = jnp.float32
BF16 = jnp.bfloat16
BLK = 256
CH = 256
FINE = 128
PIECE = 512
UN = 8

def lane_mask(shape, h):
    lane = lax.broadcasted_iota(jnp.int32, shape, len(shape) - 1)
    return (lane < HEAD) if h == 0 else (lane >= HEAD)

def only(x, h):
    return jnp.where(lane_mask(x.shape, h), x, jnp.zeros_like(x))

def fwd_kernel(lo_ref, hi_ref, q_ref, k_ref, v_ref, fq_ref, fk_ref, o_ref, lse_ref):
    i = pl.program_id(0)
    n, w = k_ref.shape
    pairs = w // 128
    lo = lo_ref[i]
    count = hi_ref[i] - lo

    def run(lo, c):
        fq = fq_ref[...]
        at = pl.multiple_of(lo * FINE, FINE)
        pieces = []
        done = 0
        while done < c * FINE:
            size = min(PIECE, c * FINE - done)
            pieces.append(pl.ds(pl.multiple_of(at + done, FINE), size))
            done += size

        def scores(u, rows):
            p, h = divmod(u, 2)
            cols = slice(p * 128, (p + 1) * 128)
            q = q_ref[:, cols] * jnp.asarray(SCALE, BF16)
            qa = jnp.concatenate([only(q, h), fq], axis=1)
            kb = jnp.concatenate([k_ref[rows, cols], fk_ref[rows, :]], axis=1)
            return lax.dot_general(qa, kb, NT, preferred_element_type=F32)

        now = [scores(0, rows) for rows in pieces]
        outs, lses = [], []
        for u in range(2 * pairs):
            p, h = divmod(u, 2)
            cols = slice(p * 128, (p + 1) * 128)
            m = jnp.max(now[0], axis=1, keepdims=True)
            for s in now[1:]:
                m = jnp.maximum(m, jnp.max(s, axis=1, keepdims=True))
            r = None
            later = []
            for s, rows in zip(now, pieces):
                if u + 1 < 2 * pairs:
                    later.append(scores(u + 1, rows))
                pr = jnp.exp(s - m).astype(BF16)
                vb = jnp.concatenate([v_ref[rows, cols], jnp.ones((s.shape[1], 128), BF16)], axis=1)
                part = jnp.dot(pr, vb, preferred_element_type=F32)
                r = part if r is None else r + part
            now = later
            l = r[:, 128:]
            outs.append(r[:, :128] / l)
            lses.append(m + jnp.log(l))
            if h == 1:
                mask = lane_mask((BLK, 128), 0)
                o_ref[:, cols] = jnp.where(mask, outs[0], outs[1]).astype(BF16)
                both = jnp.where(mask, lses[0], lses[1]).T
                lse_ref[p, 0:1, :] = both[0:1, :]
                lse_ref[p, 1:2, :] = both[HEAD:HEAD + 1, :]
                outs, lses = [], []

    most = n // FINE
    below = 0
    for c in sorted({max(BLK // FINE, most * e // 16) for e in (2, 4, 6, 8, 11, 13, 14, 16)}):
        @pl.when((count > below) & (count <= c))
        def _(c=c):
            run(jnp.minimum(lo, most - c), c)
        below = c

def attn_fwd(lo, hi, q, k, v, fq, fk):
    n, w = q.shape
    pairs = w // 128
    blk = lambda i, lo, hi: (i, 0)
    full = lambda i, lo, hi: (0, 0)
    return pl.pallas_call(
        fwd_kernel,
        grid_spec=pltpu.PrefetchScalarGridSpec(
            num_scalar_prefetch=2,
            grid=(n // BLK,),
            in_specs=[pl.BlockSpec((BLK, w), blk), pl.BlockSpec((n, w), full), pl.BlockSpec((n, w), full),
                      pl.BlockSpec((BLK, 128), blk), pl.BlockSpec((n, 128), full)],
            out_specs=[pl.BlockSpec((BLK, w), blk), pl.BlockSpec((pairs, 8, BLK), lambda i, lo, hi: (0, 0, i))],
        ),
        out_shape=[jax.ShapeDtypeStruct((n, w), BF16), jax.ShapeDtypeStruct((pairs, 8, n), F32)],
        compiler_params=pltpu.CompilerParams(vmem_limit_bytes=62 * 2 ** 20),
        name="attn_fwd",
    )(lo, hi, q, k, v, fq, fk)

def bwd_kernel(lo_ref, hi_ref, q_ref, k_ref, v_ref, do_ref, o_ref, lse_ref, fq_ref, fk_ref,
               dq_ref, dk_ref, dv_ref, delta, dqt, dk_acc, dv_acc):
    j = pl.program_id(0)
    nb = pl.num_programs(0)
    n, w = q_ref.shape
    pairs = w // 128

    @pl.when(j == 0)
    def _():
        head = lax.broadcasted_iota(jnp.int32, (16, 128), 0)
        lane = lax.broadcasted_iota(jnp.int32, (16, 128), 1)
        sel = jnp.where(lane // HEAD == head, 1.0, 0.0).astype(BF16)

        def prep(b, c):
            rows = pl.ds(pl.multiple_of(b * CH, CH), CH)
            for p in range(pairs):
                cols = slice(p * 128, (p + 1) * 128)
                prod = do_ref[rows, cols].astype(F32) * o_ref[rows, cols].astype(F32)
                hi = prod.astype(BF16)
                lo = (prod - hi.astype(F32)).astype(BF16)
                d = lax.dot_general(sel, hi, NT, preferred_element_type=F32) + lax.dot_general(sel, lo, NT, preferred_element_type=F32)
                delta[p, :, rows] = d[0:8, :]
                dqt[p, :, rows] = jnp.zeros((128, CH), F32)
            return c
        lax.fori_loop(0, n // CH, prep, 0)

    lo = lo_ref[j]
    count = hi_ref[j] - lo
    dk_acc[...] = jnp.zeros_like(dk_acc)
    dv_acc[...] = jnp.zeros_like(dv_acc)

    def run(first, c):
        rows = pl.ds(pl.multiple_of(first * FINE, FINE), c * FINE)
        units = 2 * pairs

        def scores(u):
            p, h = divmod(u, 2)
            cols = slice(p * 128, (p + 1) * 128)
            kb = jnp.concatenate([only(k_ref[:, cols] * jnp.asarray(SCALE, BF16), h), fk_ref[...]], axis=1)
            qa = jnp.concatenate([q_ref[rows, cols], fq_ref[rows, :]], axis=1)
            s = lax.dot_general(kb, qa, NT, preferred_element_type=F32)
            dp = lax.dot_general(only(v_ref[:, cols], h), do_ref[rows, cols], NT, preferred_element_type=F32)
            return s, dp

        now = scores(0)
        dk, dv = [], []
        for u in range(units):
            p, h = divmod(u, 2)
            cols = slice(p * 128, (p + 1) * 128)
            later = scores(u + 1) if u + 1 < units else None
            s, dp = now
            pr = jnp.exp(s - lse_ref[p, h:h + 1, rows])
            ds = (pr * (dp - delta[p, h:h + 1, rows])).astype(BF16)
            dv.append(jnp.dot(pr.astype(BF16), do_ref[rows, cols], preferred_element_type=F32))
            dk.append(jnp.dot(ds, q_ref[rows, cols], preferred_element_type=F32))
            kt = (k_ref[:, cols] * jnp.asarray(SCALE, BF16)).T
            dqt[p, h * HEAD:(h + 1) * HEAD, rows] += jnp.dot(kt[h * HEAD:(h + 1) * HEAD, :], ds, preferred_element_type=F32)
            now = later
            if h == 1:
                mask = lane_mask((BLK, 128), 0)
                dk_acc[:, cols] += jnp.where(mask, dk[0], dk[1])
                dv_acc[:, cols] += jnp.where(mask, dv[0], dv[1])
                dk, dv = [], []

    @pl.loop(0, count // UN)
    def _(t):
        run(lo + t * UN, UN)

    left = count % UN
    for c in range(1, UN):
        @pl.when(left == c)
        def _(c=c):
            run(lo + (count - left), c)
    dk_ref[...] = (dk_acc[...] * SCALE).astype(BF16)
    dv_ref[...] = dv_acc[...].astype(BF16)

    @pl.when(j == nb - 1)
    def _():
        def fin(b, c):
            rows = pl.ds(pl.multiple_of(b * CH, CH), CH)
            for p in range(pairs):
                dq_ref[rows, p * 128:(p + 1) * 128] = dqt[p, :, rows].T.astype(BF16)
            return c
        lax.fori_loop(0, n // CH, fin, 0)

def attn_bwd(lo, hi, q, k, v, do, o, lse, fq, fk):
    n, w = q.shape
    pairs = w // 128
    full = lambda j, lo, hi: (0, 0)
    blk = lambda j, lo, hi: (j, 0)
    sh = jax.ShapeDtypeStruct((n, w), BF16)
    big = pl.BlockSpec((n, w), full, pipeline_mode=pl.Buffered(1))
    return pl.pallas_call(
        bwd_kernel,
        grid_spec=pltpu.PrefetchScalarGridSpec(
            num_scalar_prefetch=2,
            grid=(n // BLK,),
            in_specs=[big, pl.BlockSpec((BLK, w), blk), pl.BlockSpec((BLK, w), blk), big, big, pl.BlockSpec((pairs, 8, n), lambda j, lo, hi: (0, 0, 0)),
                      pl.BlockSpec((n, 128), full), pl.BlockSpec((BLK, 128), blk)],
            out_specs=[pl.BlockSpec((n, w), full), pl.BlockSpec((BLK, w), blk), pl.BlockSpec((BLK, w), blk)],
            scratch_shapes=[
                pltpu.VMEM((pairs, 8, n), F32),
                pltpu.VMEM((pairs, 128, n), F32),
                pltpu.VMEM((BLK, w), F32),
                pltpu.VMEM((BLK, w), F32),
            ],
        ),
        out_shape=[sh, sh, sh],
        compiler_params=pltpu.CompilerParams(vmem_limit_bytes=62 * 2 ** 20),
        name="attn_bwd",
    )(lo, hi, q, k, v, do, o, lse, fq, fk)

def segment_terms(lengths, n):
    cells = lengths.shape[0]
    place_of = jnp.arange(cells)
    ends = jnp.sum(jnp.where(place_of[:, None] <= place_of[None, :], lengths[:, None], 0), axis=0)
    starts = ends - lengths
    pos = jnp.arange(n, dtype=jnp.int32)[:, None]
    pad = lambda v: jnp.pad(v, (0, 128 - cells))[None, :]
    hot = (pos >= pad(starts)) & (pos < pad(ends))
    used = (jnp.arange(128) < cells)[None, :]
    fq = jnp.where(hot, -BIG, 0.0).astype(BF16)
    fk = jnp.where(used & ~hot, 1.0, 0.0).astype(BF16)
    first = jnp.arange(n // BLK, dtype=jnp.int32)[:, None] * BLK
    lo = jnp.max(jnp.where(starts[None, :] <= first, starts[None, :], 0), axis=1) // FINE
    hi = (jnp.min(jnp.where(ends[None, :] > first + BLK - 1, ends[None, :], n), axis=1) + FINE - 1) // FINE
    return fq, fk, lo.astype(jnp.int32), hi.astype(jnp.int32)


MIB = 2 ** 20
MESH = pl.DeviceIdType.MESH
ANY = pl.BlockSpec(memory_space=pl.ANY)
VMEM = pl.BlockSpec(memory_space=pltpu.VMEM)
DMA = pltpu.SemaphoreType.DMA
TOK = 256
COLS = 768


def sds(shape, dtype):
    return jax.ShapeDtypeStruct(shape, dtype)


def place():
    section, dp, seq = lax.axis_index("section"), lax.axis_index("dp"), lax.axis_index("seq")
    core = lax.rem(dp, 2)
    return section, dp, seq, core


def greet(*devices):
    barrier = pltpu.get_barrier_semaphore()
    for device in devices:
        pl.semaphore_signal(barrier, 1, device_id=device, device_id_type=MESH)
    pl.semaphore_wait(barrier, len(devices))


def column_mates(section, dp, seq, core):
    mates = [(section, dp, lax.rem(seq + t, 4)) for t in range(1, 4)]
    mates += [(section, dp + 1 - 2 * core, lax.rem(seq + t, 4)) for t in range(4)]
    return mates


def remote(src, dst, send_sem, recv_sem, device):
    return pltpu.make_async_remote_copy(
        src_ref=src, dst_ref=dst, send_sem=send_sem, recv_sem=recv_sem,
        device_id=device, device_id_type=MESH,
    )


def span(start, size):
    return pl.ds(pl.multiple_of(start, size), size)


def chunk(i):
    return span(i * TOK, TOK)


def row_norm(values):
    centre = jnp.mean(values, axis=-1, keepdims=True)
    offset = values - centre
    spread = jnp.mean(offset * offset, axis=-1, keepdims=True)
    rstd = lax.rsqrt(spread + EPS)
    return offset * rstd, rstd


def row_norm_back(grad, hat, rstd, gain):
    d_hat = grad * gain
    mean_d = jnp.mean(d_hat, axis=-1, keepdims=True)
    mean_dh = jnp.mean(d_hat * hat, axis=-1, keepdims=True)
    return rstd * (d_hat - mean_d - hat * mean_dh)


def fold(values):
    return jnp.sum(values.reshape(values.shape[0] // 8, 8, values.shape[1]), axis=0)


def up(ref):
    return ref[...].astype(F32)


def gelu_parts(x):
    size = jnp.abs(x)
    d = 1.0 + 0.2316418882 * size
    t = pl.reciprocal(d, approx=True)
    t = t * (2.0 - d * t)
    density = jnp.exp(-0.5 * (x * x)) * 0.3989422804014327
    poly = ((((1.330274429 * t - 1.821255978) * t + 1.781477937) * t - 0.356563782) * t + 0.319381530) * t
    tail = density * poly
    phi = jnp.where(x >= 0.0, 1.0 - tail, tail)
    return x * phi, phi + x * density


def ffn_loads(wo_in, win_in, wback_in, wo, win, wback, sem):
    pairs = [(wo_in, wo)]
    for f in range(win.shape[1] // COLS):
        cols = pl.ds(f * COLS, COLS)
        pairs += [(win_in.at[:, cols], win.at[:, cols]), (wback_in.at[cols], wback.at[cols])]
    return [pltpu.make_async_copy(a, b, sem.at[n]) for n, (a, b) in enumerate(pairs)]


class ToHeads:
    def __init__(self, buf, outs, tokens, width, sems, core, sibling):
        self.buf, self.outs, self.tokens, self.width = buf, outs, tokens, width
        self.own_sem, self.send_sem, self.recv_sem = sems
        self.core, self.sibling = core, sibling

    def _cols(self, part, core):
        return span(part * self.width + core * (self.width // 2), self.width // 2)

    def _sent(self, i, part, owner):
        rows = span(owner * self.tokens + i * TOK, TOK)
        return remote(self.buf.at[chunk(i), self._cols(part, 1 - self.core)], self.outs[part].at[rows],
                      self.send_sem.at[part, i], self.recv_sem.at[part, i], self.sibling)

    def _own(self, i, part):
        rows = span(self.core * self.tokens + i * TOK, TOK)
        return pltpu.make_async_copy(self.buf.at[chunk(i), self._cols(part, self.core)],
                                     self.outs[part].at[rows], self.own_sem.at[part, i])

    def start(self, i):
        for part in range(len(self.outs)):
            self._own(i, part).start()
            self._sent(i, part, self.core).start()

    def wait(self, i):
        for part in range(len(self.outs)):
            self._own(i, part).wait()
            self._sent(i, part, self.core).wait_send()
            self._sent(i, part, 1 - self.core).wait_recv()


class ToTokens:
    def __init__(self, ins, buf, tokens, width, sems, core, sibling):
        self.ins, self.buf, self.tokens, self.width = ins, buf, tokens, width
        self.own_sem, self.send_sem, self.recv_sem = sems
        self.core, self.sibling = core, sibling

    def _cols(self, part, core):
        return span(part * self.width + core * (self.width // 2), self.width // 2)

    def _sent(self, i, part, owner):
        rows = span((1 - self.core) * self.tokens + i * TOK, TOK)
        return remote(self.ins[part].at[rows], self.buf.at[chunk(i), self._cols(part, owner)],
                      self.send_sem.at[part, i], self.recv_sem.at[part, i], self.sibling)

    def _own(self, i, part):
        rows = span(self.core * self.tokens + i * TOK, TOK)
        return pltpu.make_async_copy(self.ins[part].at[rows], self.buf.at[chunk(i), self._cols(part, self.core)],
                                     self.own_sem.at[part, i])

    def start(self, i):
        for part in range(len(self.ins)):
            self._own(i, part).start()
            self._sent(i, part, self.core).start()

    def wait(self, i):
        for part in range(len(self.ins)):
            self._own(i, part).wait()
            self._sent(i, part, 1 - self.core).wait_recv()

    def wait_sent(self, i):
        for part in range(len(self.ins)):
            self._sent(i, part, self.core).wait_send()


def swap_sems(parts, steps):
    return [DMA((parts, steps))] * 3


class Blocks:
    def __init__(self, rows_ref, blocks_ref, gather, sems, section, dp, seq, core):
        self.rows, self.blocks, self.gather = rows_ref, blocks_ref, gather
        self.own_sem, self.send_sem, self.recv_sem = sems
        self.section, self.seq, self.core, self.column = section, seq, core, dp - core
        self.each, self.local, _ = blocks_ref.shape

    def _move(self, j):
        target_core, target_seq = self.seq // self.each, self.core * self.each + j
        slot = lax.rem(self.seq, self.each)
        here = (target_core == self.core) & (target_seq == self.seq)
        if self.gather:
            src, dst = self.blocks.at[j], self.rows.at[span(slot * self.local, self.local)]
        else:
            src, dst = self.rows.at[pl.ds(j * self.local, self.local)], self.blocks.at[slot]
        target = (self.section, self.column + target_core, target_seq)
        return here, src, dst, slot, target

    def start(self):
        for j in range(self.each):
            here, src, dst, slot, target = self._move(j)

            @pl.when(here)
            def _():
                pltpu.make_async_copy(src, dst, self.own_sem).start()

            @pl.when(jnp.logical_not(here))
            def _():
                remote(src, dst, self.send_sem.at[j], self.recv_sem.at[slot], target).start()

    def wait(self):
        for j in range(self.each):
            here, src, dst, slot, target = self._move(j)

            @pl.when(here)
            def _():
                pltpu.make_async_copy(src, dst, self.own_sem).wait()

            @pl.when(jnp.logical_not(here))
            def _():
                remote(src, dst, self.send_sem.at[j], self.recv_sem.at[slot], target).wait_send()
        for j in range(self.each):
            here = (self.seq // self.each == self.core) & (self.core * self.each + j == self.seq)
            mate = (self.section, self.column + 1 - self.core, self.seq)
            if self.gather:
                dst = self.rows.at[pl.ds(j * self.local, self.local)]
                src = self.blocks.at[0]
            else:
                dst = self.blocks.at[j]
                src = self.rows.at[pl.ds(0, self.local)]

            @pl.when(jnp.logical_not(here))
            def _():
                remote(src, dst, self.send_sem.at[0], self.recv_sem.at[j], mate).wait_recv()


def block_sems(each):
    return [DMA, DMA((each,)), DMA((each,))]


def project(x, gain, bias, w, qb, vb, buf, rows):
    width = x.shape[1]
    hat, _ = row_norm(x)
    a = (hat * up(gain) + up(bias)).astype(BF16)
    for part in range(3):
        cols = slice(part * width, (part + 1) * width)
        m = jnp.dot(a, w[:, cols], preferred_element_type=F32)
        if part == 0:
            m = m + up(qb)
        if part == 2:
            m = m + up(vb)
        buf[rows, cols] = m.astype(BF16)
    return a


def first_kernel(x_ref, w_in, gain, bias, qb, vb, x_out, q_ref, k_ref, v_ref,
                 xb, w, buf, w_sem, out_sem, own_sem, send_sem, recv_sem, *sems):
    section, dp, seq, core = place()
    sibling = (section, dp + 1 - 2 * core, seq)
    each, local, width = x_ref.shape
    part = local // 2
    column = dp - core
    load = pltpu.make_async_copy(w_in, w, w_sem)
    load.start()
    greet(*[(s, column + c, z) for s in range(2) for c in range(2) for z in range(2 * each)])

    def move(m):
        target_core, target_seq = seq // each, core * each + m
        slot = lax.rem(seq, each)
        here = (section == 0) & (target_core == core) & (target_seq == seq)
        src = x_ref.at[m, span(section * part, part)]
        dst = xb.at[span(slot * local + section * part, part)]
        return here, src, dst, slot, (0, column + target_core, target_seq)

    for m in range(each):
        here, src, dst, slot, target = move(m)

        @pl.when(here)
        def _():
            pltpu.make_async_copy(src, dst, own_sem).start()

        @pl.when(jnp.logical_not(here))
        def _():
            remote(src, dst, send_sem.at[m], recv_sem.at[section, slot], target).start()
    load.wait()

    @pl.when(section == 0)
    def _():
        swap = ToHeads(buf, (q_ref, k_ref, v_ref), each * local, width, sems, core, sibling)

        def out(i):
            return pltpu.make_async_copy(xb.at[chunk(i)], x_out.at[chunk(i)], out_sem.at[i])

        for h in range(2):
            for j in range(each):
                here = (seq // each == core) & (core * each + j == seq) & (h == 0)
                dst = xb.at[pl.ds(j * local + h * part, part)]

                @pl.when(here)
                def _():
                    pltpu.make_async_copy(x_ref.at[0, pl.ds(0, part)], dst, own_sem).wait()

                @pl.when(jnp.logical_not(here))
                def _():
                    remote(x_ref.at[0, pl.ds(0, part)], dst, send_sem.at[0], recv_sem.at[h, j], sibling).wait_recv()

                for i in range((j * local + h * part) // TOK, (j * local + (h + 1) * part) // TOK):
                    rows = slice(i * TOK, (i + 1) * TOK)
                    project(xb[rows, :].astype(F32), gain, bias, w, qb, vb, buf, rows)
                    out(i).start()
                    swap.start(i)
        for i in range(each * local // TOK):
            out(i).wait()
            swap.wait(i)

    for m in range(each):
        here, src, dst, slot, target = move(m)

        @pl.when(jnp.logical_not(here))
        def _():
            remote(src, dst, send_sem.at[m], recv_sem.at[section, slot], target).wait_send()


def first_call(x, w, gain, bias, qb, vb):
    each, local, width = x.shape
    tokens = each * local
    steps = tokens // TOK
    out = sds((2 * tokens, width // 2), BF16)
    return pl.pallas_call(
        first_kernel,
        in_specs=[ANY, ANY] + [VMEM] * 4,
        out_specs=[ANY] * 4,
        out_shape=[sds((tokens, width), BF16), out, out, out],
        scratch_shapes=[
            pltpu.VMEM((tokens, width), BF16), pltpu.VMEM(w.shape, BF16), pltpu.VMEM((tokens, 3 * width), BF16),
            DMA, DMA((steps,)), DMA, DMA((each,)), DMA((2, each))] + swap_sems(3, steps),
        compiler_params=pltpu.CompilerParams(collective_id=1, has_side_effects=True, vmem_limit_bytes=62 * MIB),
        name="rows_qkv",
    )(x, w, gain, bias, qb, vb)


def feed(i, att, x, wo, win, wback, bo, g2, b2, bi, bb, keep=None, ready=None):
    rows = chunk(i)
    hidden = win.shape[1]
    if ready:
        ready[0].wait()
    resid = x[rows, :].astype(F32) + up(bo) + jnp.dot(att[rows, :], wo[...], preferred_element_type=F32)
    hat, rstd = row_norm(resid)
    c = (hat * up(g2) + up(b2)).astype(BF16)
    if keep is not None:
        resid_b, slope_b, att_t, c_t, act_t = keep
        resid_b[rows, :] = resid
        att_t[:, rows] = att[rows, :].T
        c_t[:, rows] = c.T
    total = resid + up(bb)
    for f in range(hidden // COLS):
        cols = slice(f * COLS, (f + 1) * COLS)
        if ready:
            ready[1 + 2 * f].wait()
            ready[2 + 2 * f].wait()
        inner = jnp.dot(c, win[:, cols], preferred_element_type=F32) + bi[:, cols].astype(F32)
        active, slope = gelu_parts(inner)
        active = active.astype(BF16)
        if keep is not None:
            slope_b[rows, cols] = slope.astype(BF16)
            act_t[cols, rows] = active.T
        total = total + jnp.dot(active, wback[cols, :], preferred_element_type=F32)
    return total


def feed_back(i, dy, slope_b, resid_b, wo, win, wback, g2, di_b, dr_b, dp_b, da_b, sums):
    rows = chunk(i)
    hidden = win.shape[1]
    g = dy.astype(F32)
    d_c = jnp.zeros(dy.shape, F32)
    for f in range(hidden // COLS):
        cols = slice(f * COLS, (f + 1) * COLS)
        d_active = lax.dot_general(dy, wback[cols, :], NT, preferred_element_type=F32)
        d_inner = d_active * slope_b[rows, cols].astype(F32)
        if sums:
            sums[3][:, cols] += fold(d_inner)
        d_inner = d_inner.astype(BF16)
        if di_b is not None:
            di_b[rows, cols] = d_inner
        d_c = d_c + lax.dot_general(d_inner, win[:, cols], NT, preferred_element_type=F32)
    hat, rstd = row_norm(resid_b[rows, :])
    d_resid = g + row_norm_back(d_c, hat, rstd, up(g2))
    d_proj = d_resid.astype(BF16)
    dr_b[rows, :] = d_resid
    if sums:
        s_gain, s_bias, s_out, _, s_back = sums
        s_gain[...] += fold(d_c * hat)
        s_bias[...] += fold(d_c)
        s_out[...] += fold(d_resid)
        s_back[...] += fold(g)
    if dp_b is not None:
        dp_b[rows, :] = d_proj
    da_b[rows, :] = lax.dot_general(d_proj, wo[...], NT, preferred_element_type=F32).astype(BF16)


def pass_kernel(o_ref, x_ref, g_ref, wo_in, win_in, wback_in, wqkv_in, bo, g2, b2, bi, bb, g1, b1, qb, vb,
                x_out, g_out, n_out, q_ref, k_ref, v_ref,
                wo, win, wback, wqkv, att, yb, xn, buf, w_sem, x_send, x_recv, x_sem, *sems):
    section, dp, seq, core = place()
    sibling = (section, dp + 1 - 2 * core, seq)
    across = (1 - section, dp, seq)
    tokens, width = x_ref.shape
    steps = tokens // TOK
    loads = ffn_loads(wo_in, win_in, wback_in, wo, win, wback, w_sem)
    load_qkv = pltpu.make_async_copy(wqkv_in, wqkv, w_sem.at[len(loads)])
    loads[0].start()
    greet(across, *column_mates(section, dp, seq, core))
    to_tokens = ToTokens((o_ref,), att, tokens, width, sems[:3], core, sibling)
    to_heads = ToHeads(buf, (q_ref, k_ref, v_ref), tokens, width, sems[3:6], core, sibling)
    blocks = Blocks(g_out, g_ref, True, sems[6:9], section, dp, seq, core)
    to_tokens.start(0)
    for load in loads[1:]:
        load.start()

    @pl.loop(1, steps)
    def _(i):
        to_tokens.start(i)

    load_qkv.start()

    @pl.when(section == 1)
    def _():
        blocks.start()

    def passed(i):
        return remote(yb.at[chunk(i)], xn.at[chunk(i)], x_send.at[i], x_recv.at[i], across)

    def kept(i):
        return pltpu.make_async_copy(xn.at[chunk(i)], x_out.at[chunk(i)], x_sem.at[i])

    def send_chunk(i, ready=None):
        total = feed(i, att, x_ref, wo, win, wback, bo, g2, b2, bi, bb, ready=ready)
        yb[chunk(i), :] = total.astype(BF16)
        passed(i).start()
        xn[chunk(i), :] = x_ref[chunk(i), :]

    to_tokens.wait(0)

    @pl.when(section == 0)
    def _():
        send_chunk(0, loads)

    @pl.when(section == 1)
    def _():
        for load in loads:
            load.wait()

    @pl.loop(1, steps)
    def _(i):
        to_tokens.wait(i)

        @pl.when(section == 0)
        def _():
            send_chunk(i)

    load_qkv.wait()

    @pl.loop(0, steps)
    def _(i):
        @pl.when(section == 1)
        def _():
            passed(i).wait_recv()

        kept(i).start()
        a = project(xn[chunk(i), :].astype(F32), g1, b1, wqkv, qb, vb, buf, chunk(i))
        n_out[:, chunk(i)] = a.T
        to_heads.start(i)

    @pl.loop(0, steps)
    def _(i):
        to_tokens.wait_sent(i)
        to_heads.wait(i)
        kept(i).wait()

        @pl.when(section == 0)
        def _():
            passed(i).wait_send()

    @pl.when(section == 1)
    def _():
        blocks.wait()


def pass_call(o, x, g, wo, win, wback, wqkv, vectors):
    tokens, width = x.shape
    steps = tokens // TOK
    each = g.shape[0]
    out = sds((2 * tokens, width // 2), BF16)
    low = sds(x.shape, BF16)
    low_buf = pltpu.VMEM(x.shape, BF16)
    return pl.pallas_call(
        pass_kernel,
        in_specs=[ANY, VMEM, ANY, ANY, ANY, ANY, ANY] + [VMEM] * len(vectors),
        out_specs=[ANY, ANY, VMEM, ANY, ANY, ANY],
        out_shape=[low, low, sds((width, tokens), BF16), out, out, out],
        scratch_shapes=[pltpu.VMEM(w.shape, BF16) for w in (wo, win, wback, wqkv)]
        + [low_buf, low_buf, low_buf, pltpu.VMEM((tokens, 3 * width), BF16),
           DMA((2 + 2 * (win.shape[1] // COLS),)), DMA((steps,)), DMA((steps,)), DMA((steps,))]
        + swap_sems(1, steps) + swap_sems(3, steps) + block_sems(each),
        compiler_params=pltpu.CompilerParams(collective_id=2, has_side_effects=True, vmem_limit_bytes=62 * MIB),
        name="ffn_pass_qkv",
    )(o, x, g, wo, win, wback, wqkv, *vectors)


def turn_kernel(o_ref, x_ref, g_ref, wo_in, win_in, wback_in, bo, g2, b2, bi, bb,
                y_out, resid_out, slope_out, att_out, c_out, act_out, dr_out, da_ref,
                wo, win, wback, att, yb, resid_b, slope_b, att_t, c_t, act_t, dr_b, da_b,
                w_sem, out_sem, *sems):
    section, dp, seq, core = place()
    sibling = (section, dp + 1 - 2 * core, seq)
    tokens, width = x_ref.shape
    steps = tokens // TOK
    loads = ffn_loads(wo_in, win_in, wback_in, wo, win, wback, w_sem)
    loads[0].start()
    greet(sibling)
    to_tokens = ToTokens((o_ref,), att, tokens, width, sems[:3], core, sibling)
    to_heads = ToHeads(da_b, (da_ref,), tokens, width, sems[3:6], core, sibling)
    to_tokens.start(0)
    for load in loads[1:]:
        load.start()

    @pl.loop(1, steps)
    def _(i):
        to_tokens.start(i)

    def results(i):
        here = [(yb, y_out), (resid_b, resid_out), (slope_b, slope_out), (dr_b, dr_out)]
        turned = [(att_t, att_out), (c_t, c_out), (act_t, act_out)]
        return [pltpu.make_async_copy(b.at[chunk(i)], o.at[chunk(i)], out_sem.at[n, i])
                for n, (b, o) in enumerate(here)] + [
            pltpu.make_async_copy(b.at[:, chunk(i)], o.at[:, chunk(i)], out_sem.at[4 + n, i])
            for n, (b, o) in enumerate(turned)]

    def step(i, ready=None):
        to_tokens.wait(i)
        total = feed(i, att, x_ref, wo, win, wback, bo, g2, b2, bi, bb, (resid_b, slope_b, att_t, c_t, act_t), ready)
        yb[chunk(i), :] = total.astype(BF16)
        feed_back(i, g_ref[chunk(i), :], slope_b, resid_b, wo, win, wback, g2, None, dr_b, None, da_b, None)
        to_heads.start(i)
        for copy in results(i):
            copy.start()

    step(0, loads)

    @pl.loop(1, steps)
    def _(i):
        step(i)

    @pl.loop(0, steps)
    def _(i):
        to_tokens.wait_sent(i)
        to_heads.wait(i)
        for copy in results(i):
            copy.wait()


def turn_call(o, x, g, wo, win, wback, vectors):
    tokens, width = x.shape
    hidden = win.shape[1]
    steps = tokens // TOK
    low, full = sds(x.shape, BF16), sds(x.shape, F32)
    turned = sds((width, tokens), BF16)
    outs = [low, full, sds((tokens, hidden), BF16), turned, turned, sds((hidden, tokens), BF16), full]
    buf = lambda s: pltpu.VMEM(s.shape, s.dtype)
    return pl.pallas_call(
        turn_kernel,
        in_specs=[ANY, VMEM, VMEM, ANY, ANY, ANY] + [VMEM] * len(vectors),
        out_specs=[ANY] * 8,
        out_shape=outs + [sds((2 * tokens, width // 2), BF16)],
        scratch_shapes=[buf(wo), buf(win), buf(wback), buf(low)] + [buf(s) for s in outs] + [buf(low)]
        + [DMA((1 + 2 * (hidden // COLS),)), DMA((7, steps))] + swap_sems(1, steps) + swap_sems(1, steps),
        compiler_params=pltpu.CompilerParams(collective_id=3, has_side_effects=True, vmem_limit_bytes=62 * MIB),
        name="ffn_turn",
    )(o, x, g, wo, win, wback, *vectors)


def input_back(i, dj, dr, x, w, gain, sums):
    rows = chunk(i)
    width = x.shape[1]
    d_a = lax.dot_general(dj[rows, :], w[...], NT, preferred_element_type=F32)
    hat, rstd = row_norm(x[rows, :].astype(F32))
    if sums:
        s_gain, s_bias, s_q, s_v = sums
        s_q[...] += fold(dj[rows, :width].astype(F32))
        s_v[...] += fold(dj[rows, 2 * width:].astype(F32))
        s_gain[...] += fold(d_a * hat)
        s_bias[...] += fold(d_a)
    return (dr[rows, :] + row_norm_back(d_a, hat, rstd, up(gain))).astype(BF16)


def back_kernel(dq_ref, dk_ref, dv_ref, dr_ref, x_ref, y_ref, g_in, slope_in, resid_in,
                wqkv_in, wo_in, win_in, wback_in, g1, g2,
                y_out, g_out, di_out, dr_out, dp_out, da_ref, s_gain, s_bias, s_out, s_in, s_back,
                wqkv, wo, win, wback, dj, dx, gb, slope_b, resid_b, di_b, dr_b, dp_b, da_b,
                w_sem, in_sem, out_sem, g_sem, x_send, x_recv, *sems):
    section, dp, seq, core = place()
    sibling = (section, dp + 1 - 2 * core, seq)
    across = (1 - section, dp, seq)
    tokens, width = x_ref.shape
    steps = tokens // TOK
    loads = [pltpu.make_async_copy(a, b, w_sem.at[n]) for n, (a, b) in enumerate(
        ((wqkv_in, wqkv), (wback_in, wback), (win_in, win), (wo_in, wo)))]
    loads[0].start()

    def kept(i):
        return [pltpu.make_async_copy(a.at[chunk(i)], b.at[chunk(i)], in_sem.at[n, i])
                for n, (a, b) in enumerate(((slope_in, slope_b), (resid_in, resid_b)))]

    def last(i):
        return pltpu.make_async_copy(g_in.at[chunk(i)], gb.at[chunk(i)], g_sem.at[i])

    greet(across, *column_mates(section, dp, seq, core))
    to_tokens = ToTokens((dq_ref, dk_ref, dv_ref), dj, tokens, width, sems[:3], core, sibling)
    to_heads = ToHeads(da_b, (da_ref,), tokens, width, sems[3:6], core, sibling)
    blocks = Blocks(y_ref, y_out, False, sems[6:9], section, dp, seq, core)

    @pl.loop(0, steps)
    def _(i):
        to_tokens.start(i)

    sums = (s_gain, s_bias, s_out, s_in, s_back)
    for s in sums:
        s[...] = jnp.zeros_like(s)

    def passed(i):
        return remote(dx.at[chunk(i)], gb.at[chunk(i)], x_send.at[i], x_recv.at[i], across)

    def results(i):
        return [pltpu.make_async_copy(b.at[chunk(i)], o.at[chunk(i)], out_sem.at[n, i])
                for n, (b, o) in enumerate(((gb, g_out), (di_b, di_out), (dr_b, dr_out), (dp_b, dp_out)))]

    loads[0].wait()

    @pl.loop(0, steps)
    def _(i):
        to_tokens.wait(i)

        @pl.when(i == 0)
        def _():
            for load in loads[1:]:
                load.start()

        for copy in kept(i):
            copy.start()

        @pl.when(section == 1)
        def _():
            last(i).start()
            dx[chunk(i), :] = input_back(i, dj, dr_ref, x_ref, wqkv, g1, None)
            passed(i).start()

    blocks.start()

    for load in loads[1:]:
        load.wait()

    @pl.loop(0, steps)
    def _(i):
        for copy in kept(i):
            copy.wait()

        @pl.when(section == 0)
        def _():
            passed(i).wait_recv()

        @pl.when(section == 1)
        def _():
            last(i).wait()

        feed_back(i, gb[chunk(i), :], slope_b, resid_b, wo, win, wback, g2, di_b, dr_b, dp_b, da_b, sums)
        to_heads.start(i)
        for copy in results(i):
            copy.start()

    @pl.loop(0, steps)
    def _(i):
        to_tokens.wait_sent(i)
        to_heads.wait(i)
        for copy in results(i):
            copy.wait()

        @pl.when(section == 1)
        def _():
            passed(i).wait_send()

    blocks.wait()


def back_call(dq, dk, dv, dr, x, y, g, slope, resid, wqkv, wo, win, wback, g1, g2, each):
    tokens, width = x.shape
    hidden = win.shape[1]
    steps = tokens // TOK
    low, full, wide = sds(x.shape, BF16), sds(x.shape, F32), sds((tokens, hidden), BF16)
    one = sds((8, width), F32)
    buf = lambda s: pltpu.VMEM(s.shape, s.dtype)
    return pl.pallas_call(
        back_kernel,
        in_specs=[ANY, ANY, ANY, VMEM, VMEM] + [ANY] * 8 + [VMEM, VMEM],
        out_specs=[ANY] * 6 + [VMEM] * 5,
        out_shape=[sds((each, tokens // each, width), BF16), low, wide, full, low, sds((2 * tokens, width // 2), BF16),
                   one, one, one, sds((8, hidden), F32), one],
        scratch_shapes=[buf(wqkv), buf(wo), buf(win), buf(wback), pltpu.VMEM((tokens, 3 * width), BF16),
                        buf(low), buf(low), buf(wide), buf(full), buf(wide), buf(full), buf(low), buf(low),
                        DMA((4,)), DMA((2, steps)), DMA((4, steps)), DMA((steps,)), DMA((steps,)), DMA((steps,))]
        + swap_sems(3, steps) + swap_sems(1, steps) + block_sems(each),
        compiler_params=pltpu.CompilerParams(collective_id=4, has_side_effects=True, vmem_limit_bytes=62 * MIB),
        name="qkv_back_pass",
    )(dq, dk, dv, dr, x, y, g, slope, resid, wqkv, wo, win, wback, g1, g2)


def last_kernel(dq_ref, dk_ref, dv_ref, dr_ref, x_ref, w_in, gain,
                dj_out, dx_out, s_gain, s_bias, s_q, s_v, w, dj, dxb, w_sem, out_sem, *sems):
    section, dp, seq, core = place()
    sibling = (section, dp + 1 - 2 * core, seq)
    tokens, width = x_ref.shape
    steps = tokens // TOK
    load = pltpu.make_async_copy(w_in, w, w_sem)
    load.start()
    greet(sibling)
    to_tokens = ToTokens((dq_ref, dk_ref, dv_ref), dj, tokens, width, sems, core, sibling)

    def results(i):
        return [pltpu.make_async_copy(b.at[chunk(i)], o.at[chunk(i)], out_sem.at[n, i])
                for n, (b, o) in enumerate(((dj, dj_out), (dxb, dx_out)))]

    @pl.loop(0, steps)
    def _(i):
        to_tokens.start(i)

    sums = (s_gain, s_bias, s_q, s_v)
    for s in sums:
        s[...] = jnp.zeros_like(s)
    load.wait()

    @pl.loop(0, steps)
    def _(i):
        to_tokens.wait(i)
        dxb[chunk(i), :] = input_back(i, dj, dr_ref, x_ref, w, gain, sums)
        for copy in results(i):
            copy.start()

    @pl.loop(0, steps)
    def _(i):
        to_tokens.wait_sent(i)
        for copy in results(i):
            copy.wait()


def last_call(dq, dk, dv, dr, x, w, gain):
    tokens, width = x.shape
    steps = tokens // TOK
    joined = sds((tokens, 3 * width), BF16)
    low, one = sds(x.shape, BF16), sds((8, width), F32)
    buf = lambda s: pltpu.VMEM(s.shape, s.dtype)
    return pl.pallas_call(
        last_kernel,
        in_specs=[ANY, ANY, ANY, VMEM, VMEM, ANY, VMEM],
        out_specs=[ANY, ANY] + [VMEM] * 4,
        out_shape=[joined, low] + [one] * 4,
        scratch_shapes=[buf(w), buf(joined), buf(low), DMA, DMA((2, steps))] + swap_sems(3, steps),
        compiler_params=pltpu.CompilerParams(collective_id=5, has_side_effects=True, vmem_limit_bytes=62 * MIB),
        name="qkv_back",
    )(dq, dk, dv, dr, x, w, gain)


def core_rows(size, yy, core):
    return span((2 * yy + core) * 4 * size, 4 * size)


def attn_plan(width):
    return [(width, width, 0, 0)] + [(width, width, 1, i * width) for i in range(3)]


def piece(left, right, at, cols, out):
    step = min(left.shape[0], 1024)

    @pl.loop(0, left.shape[0] // step)
    def _(r):
        block = span(r * step, step)
        out[block, :] = jnp.dot(left[block, :], right[:, at:at + cols], preferred_element_type=F32).astype(BF16)


def ffn_grads_kernel(plan, left_in, right_in, out, left, right, *refs):
    count = len(plan)
    buf, rec = refs[:count], refs[count:2 * count]
    load_sem, s_send, s_recv = refs[2 * count:]
    section, dp, seq, core = place()
    sibling = (section, dp + 1 - 2 * core, seq)
    loads = [pltpu.make_async_copy(left_in, left, load_sem.at[0])]
    loads += [pltpu.make_async_copy(right_in.at[:, at:at + cols], right.at[:, at:at + cols], load_sem.at[1 + p])
              for p, (_, cols, at) in enumerate(plan)]
    for load in loads:
        load.start()
    greet(sibling)

    def sent(p, yy):
        size = plan[p][0] // 16
        return remote(buf[p].at[core_rows(size, yy, 1 - core)], rec[p].at[pl.ds(yy * 4 * size, 4 * size)],
                      s_send.at[p, yy], s_recv.at[p, yy], sibling)

    def add(p):
        rows, cols, at = plan[p]
        size = rows // 16
        for yy in range(2):
            sent(p, yy).wait_recv()
            total = (buf[p][core_rows(size, yy, core), :].astype(F32)
                     + rec[p][yy * 4 * size:(yy + 1) * 4 * size, :].astype(F32)).astype(BF16)
            for zz in range(4):
                out[zz * 2 * size + yy * size:zz * 2 * size + (yy + 1) * size, at:at + cols] = (
                    total[zz * size:(zz + 1) * size, :])

    loads[0].wait()
    for p, (rows, cols, at) in enumerate(plan):
        loads[1 + p].wait()
        piece(left, right, at, cols, buf[p])
        for yy in range(2):
            sent(p, yy).start()
        if p > 0:
            add(p - 1)
    add(count - 1)
    for p in range(count):
        for yy in range(2):
            sent(p, yy).wait_send()


def ffn_grads_call(number, left, right):
    rows, columns = left.shape[0], right.shape[1]
    cols = 768 if rows <= columns else 256
    plan = [(rows, cols, at) for at in range(0, columns, cols)]
    count = len(plan)
    return pl.pallas_call(
        partial(ffn_grads_kernel, plan),
        in_specs=[ANY] * 2,
        out_specs=VMEM,
        out_shape=sds((rows // 2, columns), BF16),
        scratch_shapes=[pltpu.VMEM(left.shape, BF16), pltpu.VMEM(right.shape, BF16)]
        + [pltpu.VMEM((r, c), BF16) for r, c, _ in plan]
        + [pltpu.VMEM((r // 2, c), BF16) for r, c, _ in plan]
        + [DMA((1 + count,)), DMA((count, 2)), DMA((count, 2))],
        compiler_params=pltpu.CompilerParams(collective_id=number, has_side_effects=True, vmem_limit_bytes=62 * MIB),
        name="ffn_weight_grads",
    )(left, right)


def grads_kernel(n_small, *refs):
    refs = list(refs)
    lefts = [refs.pop(0) for _ in range(2)]
    rights = [refs.pop(0) for _ in range(2)]
    ffn_in = [refs.pop(0) for _ in range(2)]
    dx = refs.pop(0)
    sums = [refs.pop(0) for _ in range(n_small)]
    outs = [refs.pop(0) for _ in range(2)]
    ffn_out = [refs.pop(0) for _ in range(2)]
    small_out, dx_out = refs.pop(0), refs.pop(0)
    left_buf = [refs.pop(0) for _ in range(2)]
    right_buf = [refs.pop(0) for _ in range(2)]
    ffn_rec = [refs.pop(0) for _ in range(2)]
    width, tokens = lefts[0].shape
    plan = attn_plan(width)
    buf1 = [refs.pop(0) for _ in plan]
    rec1 = [refs.pop(0) for _ in plan]
    rec2 = [refs.pop(0) for _ in plan]
    rec3 = [refs.pop(0) for _ in plan]
    small, small1, small2, small3 = [refs.pop(0) for _ in range(4)]
    (load_sem, s1_send, s1_recv, s2_send, s2_recv, s3_send, s3_recv,
     m_send, m_recv, f_send, f_recv) = refs[:11]

    section, dp, seq, core = place()
    y = dp // 2
    sibling = (section, dp + 1 - 2 * core, seq)
    across_y = (section, dp + 2 - 4 * y, seq)
    along = [(section, dp, lax.rem(seq + t, 4)) for t in range(1, 4)]
    count = len(plan)
    loads = [[pltpu.make_async_copy(lefts[t], left_buf[t], load_sem.at[0, t]),
              pltpu.make_async_copy(rights[t], right_buf[t], load_sem.at[1, t])] for t in range(2)]
    for pair in loads:
        for load in pair:
            load.start()
    greet(across_y, *column_mates(section, dp, seq, core))
    blocks = Blocks(dx, dx_out, False, refs[11:14], section, dp, seq, core)
    blocks.start()

    def ffn_sent(n):
        size = ffn_in[n].shape[0] // 2
        return remote(ffn_in[n].at[span((1 - y) * size, size)], ffn_rec[n], f_send.at[n], f_recv.at[n], across_y)


    size = width // 16

    def half(yy):
        return span(yy * 4 * size, 4 * size)

    def first(p, yy):
        return remote(buf1[p].at[core_rows(size, yy, 1 - core)], rec1[p].at[half(yy)],
                      s1_send.at[p, yy], s1_recv.at[p, yy], sibling)

    def second(p):
        return remote(rec1[p].at[half(1 - y)], rec2[p], s2_send.at[p], s2_recv.at[p], across_y)

    def third(p, t):
        rows = span(y * 4 * size + lax.rem(seq + t, 4) * size, size)
        return remote(rec1[p].at[rows], rec3[p].at[seq], s3_send.at[p, t - 1], s3_recv.at[p, t - 1], along[t - 1])

    def third_got(p, t):
        rows = span(y * 4 * size + seq * size, size)
        return remote(rec1[p].at[rows], rec3[p].at[lax.rem(seq + 4 - t, 4)],
                      s3_send.at[p, t - 1], s3_recv.at[p, t - 1], along[t - 1])

    def reduce_core(p):
        for yy in range(2):
            first(p, yy).wait_recv()
            total = buf1[p][core_rows(size, yy, core), :].astype(F32) + rec1[p][half(yy), :].astype(F32)
            rec1[p][half(yy), :] = total.astype(BF16)
        second(p).start()

    def reduce_y(p):
        second(p).wait_recv()
        mine = half(y)
        rec1[p][mine, :] = (rec1[p][mine, :].astype(F32) + rec2[p][...].astype(F32)).astype(BF16)
        for t in range(1, 4):
            third(p, t).start()

    def reduce_z(p):
        rows, cols, t_out, at = plan[p]
        total = rec1[p][span(y * 4 * size + seq * size, size), :].astype(F32)
        for t in range(1, 4):
            third_got(p, t).wait_recv()
            total = total + rec3[p][lax.rem(seq + 4 - t, 4)].astype(F32)
        outs[t_out][:, at:at + cols] = total

    line = 0
    for s in sums:
        row = jnp.sum(s[...], axis=0, keepdims=True)
        for t in range(s.shape[1] // 128):
            small[line:line + 1, :] = row[:, t * 128:(t + 1) * 128]
            line += 1
    v1 = remote(small, small1, m_send.at[0], m_recv.at[0], sibling)
    v2 = remote(small, small2, m_send.at[1], m_recv.at[1], across_y)

    def v3(t):
        return remote(small, small3.at[t - 1], m_send.at[1 + t], m_recv.at[1 + t], along[t - 1])

    v1.start()
    v1.wait()
    small[...] += small1[...]
    v2.start()
    ready = set()
    for p, (rows, cols, t, at) in enumerate(plan):
        if t not in ready:
            ready.add(t)
            for load in loads[t]:
                load.wait()
        piece(left_buf[t], right_buf[t], at, cols, buf1[p])
        for yy in range(2):
            first(p, yy).start()
        if p > 0:
            reduce_core(p - 1)
        if p == 1:
            v2.wait()
            small[...] += small2[...]
            for t in range(1, 4):
                v3(t).start()
    reduce_core(count - 1)
    for n in range(2):
        ffn_sent(n).start()
    for p in range(count):
        reduce_y(p)
    for n in range(2):
        ffn_sent(n).wait_recv()
        rows = ffn_in[n].shape[0] // 2
        ffn_out[n][...] = ffn_in[n][span(y * rows, rows), :].astype(F32) + ffn_rec[n][...].astype(F32)
    for t in range(1, 4):
        v3(t).wait()
    small_out[...] = small[...] + small3[0] + small3[1] + small3[2]
    for p in range(count):
        reduce_z(p)

    for p in range(count):
        for yy in range(2):
            first(p, yy).wait_send()
        second(p).wait_send()
        for t in range(1, 4):
            third(p, t).wait_send()
    for n in range(2):
        ffn_sent(n).wait_send()
    blocks.wait()


def grads_call(att_t, norm_t, d_proj, d_joined, ffn, dx, sums, each):
    width, tokens = att_t.shape
    plan = attn_plan(width)
    count = len(plan)
    lines = sum(s.shape[1] for s in sums) // 128
    vec = pltpu.VMEM((lines, 128), F32)
    halves = [(f.shape[0] // 2, f.shape[1]) for f in ffn]
    return pl.pallas_call(
        partial(grads_kernel, len(sums)),
        in_specs=[ANY] * 4 + [VMEM] * 2 + [ANY] + [VMEM] * len(sums),
        out_specs=[VMEM] * 5 + [ANY],
        out_shape=[sds((width // 16, width), F32), sds((width // 16, 3 * width), F32)]
        + [sds(h, F32) for h in halves]
        + [sds((lines, 128), F32), sds((each, tokens // each, width), BF16)],
        scratch_shapes=(
            [pltpu.VMEM(a.shape, BF16) for a in (att_t, norm_t, d_proj, d_joined)]
            + [pltpu.VMEM(h, BF16) for h in halves]
            + [pltpu.VMEM((r, c), BF16) for r, c, *_ in plan]
            + [pltpu.VMEM((r // 2, c), BF16) for r, c, *_ in plan]
            + [pltpu.VMEM((r // 4, c), BF16) for r, c, *_ in plan]
            + [pltpu.VMEM((4, r // 16, c), BF16) for r, c, *_ in plan]
            + [vec, vec, vec, pltpu.VMEM((3, lines, 128), F32)]
            + [DMA((2, 2)), DMA((count, 2)), DMA((count, 2)), DMA((count,)), DMA((count,)),
               DMA((count, 3)), DMA((count, 3)), DMA((5,)), DMA((5,)), DMA((2,)), DMA((2,))]
            + block_sems(each)),
        compiler_params=pltpu.CompilerParams(collective_id=8, has_side_effects=True, vmem_limit_bytes=62 * MIB),
        name="weight_grads",
    )(att_t, norm_t, d_proj, d_joined, *ffn, dx, *sums)


def swap_cores(x):
    size = lax.axis_size("dp")
    return lax.ppermute(x, "dp", [(i, i ^ 1) for i in range(size)])


def on_device_rows(cell_tokens, cell_lengths, out_grad, *raw_weights):
    (gain1, bias1, wqkv, qb, vb, wo, bo, gain2, bias2, win, bi, wback, bb) = tuple(
        (w if w.ndim == 2 else w[0] for w in raw_weights)
    )
    each, local, width = cell_tokens.shape
    row_length = local * lax.axis_size("seq")
    core = lax.axis_index("dp") % 2
    z = lax.axis_index("seq")

    lengths = jnp.where(z // each == core, cell_lengths, swap_cores(cell_lengths))
    lengths = lax.dynamic_index_in_dim(lengths, z % each, 0, keepdims=False)
    fq, fk, lo, hi = segment_terms(lengths, row_length)

    x, q, k, v = first_call(cell_tokens, wqkv, gain1, bias1, qb, vb)
    o, _ = attn_fwd(lo, hi, q, k, v, fq, fk)
    x, g, norm_t, q, k, v = pass_call(
        o, x, out_grad, wo, win, wback, wqkv, (bo, gain2, bias2, bi, bb, gain1, bias1, qb, vb))
    o, lse = attn_fwd(lo, hi, q, k, v, fq, fk)
    y, resid, slope, att_t, c_t, act_t, dr, do = turn_call(o, x, g, wo, win, wback, (bo, gain2, bias2, bi, bb))

    dq, dk, dv = attn_bwd(lo, hi, q, k, v, do, o, lse, fq, fk)
    outputs, g, di, dr, dp, do, s_gain2, s_bias2, s_out, s_in, s_back = back_call(
        dq, dk, dv, dr, x, y, g, slope, resid, wqkv, wo, win, wback, gain1, gain2, each)
    ffn = [ffn_grads_call(6, c_t, di), ffn_grads_call(7, act_t, g)]
    ffn = [lax.psum_scatter(w, "seq", scatter_dimension=0, tiled=True) for w in ffn]
    dq, dk, dv = attn_bwd(lo, hi, q, k, v, do, o, lse, fq, fk)
    dj, dx, s_gain1, s_bias1, s_q, s_v = last_call(dq, dk, dv, dr, x, wqkv, gain1)
    sums = (s_gain1, s_bias1, s_q, s_v, s_out, s_gain2, s_bias2, s_in, s_back)
    g_out, g_qkv, g_in, g_back, small, in_grads = grads_call(att_t, norm_t, dp, dj, ffn, dx, sums, each)

    flat = small.reshape(-1)
    parts = lax.axis_size("dp") * lax.axis_size("seq")
    owner = lax.axis_index("dp") * lax.axis_size("seq") + z
    shares, at = [], 0
    for s in sums:
        size = s.shape[1] // parts
        shares.append(lax.dynamic_slice_in_dim(flat, at + owner * size, size))
        at += s.shape[1]
    return (
        outputs[None],
        in_grads.astype(F32)[None],
        shares[0][None],
        shares[1][None],
        g_qkv[None],
        shares[2][None],
        shares[3][None],
        g_out[None],
        shares[4][None],
        shares[5][None],
        shares[6][None],
        g_in[None],
        shares[7][None],
        g_back[None],
        shares[8][None],
    )


def either_plan(cell_tokens, *others):
    one_chip = lax.axis_size("dp") % 2 == 0 and lax.axis_size("seq") == 2 * cell_tokens.shape[0] and lax.axis_size("section") == 2 and lax.axis_size("dp") == lax.axis_size("seq") == 4
    return (on_device_rows if one_chip else on_device)(cell_tokens, *others)


def solution(mesh):
    in_specs = (
        P("dp", "seq", None),
        P("dp", None),
        P("dp", "seq", None),
        P("section", None),
        P("section", None),
        P("section", None, None),
        P("section", None),
        P("section", None),
        P("section", None, None),
        P("section", None),
        P("section", None),
        P("section", None),
        P("section", None, None),
        P("section", None),
        P("section", None, None),
        P("section", None),
    )
    out_specs = (
        P("section", "dp", "seq", None),
        P("section", "dp", "seq", None),
        P("section", ("dp", "seq")),
        P("section", ("dp", "seq")),
        P("section", ("dp", "seq"), None),
        P("section", ("dp", "seq")),
        P("section", ("dp", "seq")),
        P("section", ("dp", "seq"), None),
        P("section", ("dp", "seq")),
        P("section", ("dp", "seq")),
        P("section", ("dp", "seq")),
        P("section", ("dp", "seq"), None),
        P("section", ("dp", "seq")),
        P("section", ("dp", "seq"), None),
        P("section", ("dp", "seq")),
    )
    return jax.shard_map(
        either_plan, mesh=mesh, in_specs=in_specs, out_specs=out_specs, check_vma=False
    )
```

```python
from functools import partial

import jax
import jax.numpy as jnp
from jax import lax
from jax.experimental import pallas as pl
from jax.experimental.pallas import tpu as pltpu
from jax.sharding import PartitionSpec as P

HEADS = 12


SCALE = 0.125
EPS = 1e-05
MASKED = -1e30


def from_behind(x, axis, by):
    peers = lax.axis_size(axis)
    pairs = [(i, i + by) for i in range(peers) if 0 <= i + by < peers]
    return lax.ppermute(x, axis, pairs)


def norm_rows(values, gain_vec, bias_vec):
    centre = jnp.mean(values, axis=-1, keepdims=True)
    offset = values - centre
    spread = jnp.mean(offset * offset, axis=-1, keepdims=True)
    return offset * lax.rsqrt(spread + EPS) * gain_vec + bias_vec


def row_segments(lengths, row_length):
    limits = jnp.cumsum(lengths, axis=-1)
    places = jnp.arange(row_length, dtype=jnp.int32)
    return jnp.sum((places[None, :, None] >= limits[:, None, :]).astype(jnp.int32), axis=-1)


def split_heads(values):
    return values.reshape(values.shape[0], HEADS, values.shape[1] // HEADS)


def masked_scores(queries, keys_in, seg_query, seg_keys):
    scores = (
        jnp.einsum(
            "qhe,khe->hqk",
            split_heads(queries),
            split_heads(keys_in),
            preferred_element_type=jnp.float32,
        )
        * SCALE
    )
    return jnp.where((seg_query[:, None] == seg_keys[None, :])[None], scores, MASKED)


def softmax_parts(scores):
    highest = jnp.max(scores, axis=-1)
    raised = jnp.exp(scores - highest[..., None])
    summed = jnp.sum(raised, axis=-1)
    return (raised / summed[..., None], highest, summed)


def project_in(inputs, weights):
    normed = norm_rows(inputs, weights[0], weights[1]).astype(jnp.bfloat16)
    joined = jnp.dot(normed, weights[2], preferred_element_type=jnp.float32)
    model_width = inputs.shape[1]
    queries = (joined[:, :model_width] + weights[3]).astype(jnp.bfloat16)
    keys_out = joined[:, model_width : 2 * model_width].astype(jnp.bfloat16)
    values_out = (joined[:, 2 * model_width :] + weights[4]).astype(jnp.bfloat16)
    return (normed, queries, keys_out, values_out)


def attend(queries, keys_all, values_all, seg_own, seg_row):
    soft_probs, highest, summed = softmax_parts(masked_scores(queries, keys_all, seg_own, seg_row))
    low_probs = soft_probs.astype(jnp.bfloat16)
    combined = jnp.einsum(
        "hqk,khe->qhe", low_probs, split_heads(values_all), preferred_element_type=jnp.float32
    )
    return (
        combined.reshape(queries.shape).astype(jnp.bfloat16),
        soft_probs,
        low_probs,
        highest,
        summed,
    )


def finish(inputs, attended, weights):
    resid_sum = (
        inputs + jnp.dot(attended, weights[5], preferred_element_type=jnp.float32) + weights[6]
    )
    normed = norm_rows(resid_sum, weights[7], weights[8]).astype(jnp.bfloat16)
    hidden_pre = jnp.dot(normed, weights[9], preferred_element_type=jnp.float32) + weights[10]
    active = jax.nn.gelu(hidden_pre, approximate=False).astype(jnp.bfloat16)
    result = (
        resid_sum + jnp.dot(active, weights[11], preferred_element_type=jnp.float32) + weights[12]
    )
    return (result, resid_sum, normed, hidden_pre, active)


def store_slot(buffer, item_new, slot_idx, is_valid):
    current = lax.dynamic_index_in_dim(buffer, slot_idx, 0, keepdims=False)
    return lax.dynamic_update_index_in_dim(
        buffer, jnp.where(is_valid, item_new, current), slot_idx, 0
    )


def token_sum(values):
    return jnp.sum(values.astype(jnp.float32), axis=0)


def on_device(
    cell_tokens,
    cell_lengths,
    out_grad,
    norm1_gain,
    norm1_bias,
    qkv_weight,
    query_bias,
    value_bias,
    out_weight,
    out_bias,
    norm2_gain,
    norm2_bias,
    in_weight,
    in_bias,
    back_weight,
    back_bias,
):
    raw_weights = (
        norm1_gain,
        norm1_bias,
        qkv_weight,
        query_bias,
        value_bias,
        out_weight,
        out_bias,
        norm2_gain,
        norm2_bias,
        in_weight,
        in_bias,
        back_weight,
        back_bias,
    )
    weights = tuple(
        (weight[0].astype(jnp.float32) if weight.ndim == 2 else weight[0] for weight in raw_weights)
    )
    sections = lax.axis_size("section")
    section_rank = lax.axis_index("section")
    micro_count, local_len, model_width = cell_tokens.shape
    row_length = local_len * lax.axis_size("seq")
    own_start = lax.axis_index("seq") * local_len
    segments = row_segments(cell_lengths, row_length)
    tick_count = micro_count + sections - 1
    kept_depth = 1

    def row_segs(slot_idx):
        seg_row = lax.dynamic_index_in_dim(segments, slot_idx, 0, keepdims=False)
        return (seg_row, lax.dynamic_slice_in_dim(seg_row, own_start, local_len))

    def forward_tick(tick_now, state_now):
        incoming, kept_in, outputs, kept_keys, kept_values = state_now
        index_now = tick_now - section_rank
        is_valid = (index_now >= 0) & (index_now < micro_count)
        slot_idx = jnp.clip(index_now, 0, micro_count - 1)
        first_in = lax.dynamic_index_in_dim(cell_tokens, slot_idx, 0, keepdims=False)
        layer_in = jnp.where(section_rank == 0, first_in, incoming)
        seg_row, seg_own = row_segs(slot_idx)
        inputs = layer_in.astype(jnp.float32)
        normed, queries, keys_out, values_out = project_in(inputs, weights)
        keys_all, values_all = (
            lax.all_gather(keys_out, "seq", axis=0, tiled=True),
            lax.all_gather(values_out, "seq", axis=0, tiled=True),
        )
        attended = attend(queries, keys_all, values_all, seg_own, seg_row)[0]
        result = finish(inputs, attended, weights)[0].astype(jnp.bfloat16)
        kept_in = store_slot(kept_in, layer_in, slot_idx, is_valid)
        outputs = store_slot(outputs, result, slot_idx, is_valid)
        passed = from_behind(result, "section", 1)
        return (passed, kept_in, outputs, kept_keys, kept_values)

    start_state = (
        jnp.zeros((local_len, model_width), jnp.bfloat16),
        jnp.zeros((micro_count, local_len, model_width), jnp.bfloat16),
        jnp.zeros((micro_count, local_len, model_width), jnp.bfloat16),
        jnp.zeros((kept_depth, row_length, model_width), jnp.bfloat16),
        jnp.zeros((kept_depth, row_length, model_width), jnp.bfloat16),
    )
    ignored, kept_in, outputs, kept_keys, kept_values = lax.fori_loop(
        0, tick_count, forward_tick, start_state
    )

    def backward_tick(tick_now, state_now):
        incoming, in_grads, totals = state_now
        index_now = tick_now - (sections - 1 - section_rank)
        is_valid = (index_now >= 0) & (index_now < micro_count)
        slot_idx = jnp.clip(index_now, 0, micro_count - 1)
        from_out = lax.dynamic_index_in_dim(out_grad, slot_idx, 0, keepdims=False)
        grad_out = jnp.where(section_rank == sections - 1, from_out, incoming).astype(jnp.float32)
        inputs = lax.dynamic_index_in_dim(kept_in, slot_idx, 0, keepdims=False).astype(jnp.float32)
        seg_row, seg_own = row_segs(slot_idx)
        normed_one, queries, keys_out, values_out = project_in(inputs, weights)
        keys_all, values_all = (
            lax.all_gather(keys_out, "seq", axis=0, tiled=True),
            lax.all_gather(values_out, "seq", axis=0, tiled=True),
        )
        attended, soft_probs, low_probs, highest, summed = attend(
            queries, keys_all, values_all, seg_own, seg_row
        )
        result, resid_sum, normed_two, hidden_pre, active = finish(inputs, attended, weights)
        d_result = grad_out.astype(jnp.bfloat16)
        g_back_w = jnp.einsum("tf,td->fd", active, d_result, preferred_element_type=jnp.float32)
        g_back_b = token_sum(d_result)
        d_active = jnp.einsum(
            "td,fd->tf", d_result, weights[11], preferred_element_type=jnp.float32
        )
        gelu_value, gelu_back = jax.vjp(partial(jax.nn.gelu, approximate=False), hidden_pre)
        d_hidden = gelu_back(d_active)[0].astype(jnp.bfloat16)
        g_in_w = jnp.einsum("td,tf->df", normed_two, d_hidden, preferred_element_type=jnp.float32)
        g_in_b = token_sum(d_hidden)
        d_normed_two = jnp.einsum(
            "tf,df->td", d_hidden, weights[9], preferred_element_type=jnp.float32
        )
        norm_value, norm_two_back = jax.vjp(norm_rows, resid_sum, weights[7], weights[8])
        d_resid_norm, g_gain_two, g_bias_two = norm_two_back(d_normed_two)
        d_resid = grad_out + d_resid_norm
        d_proj = d_resid.astype(jnp.bfloat16)
        g_out_w = jnp.einsum("td,te->de", attended, d_proj, preferred_element_type=jnp.float32)
        g_out_b = token_sum(d_proj)
        d_attended = jnp.einsum(
            "te,de->td", d_proj, weights[5], preferred_element_type=jnp.float32
        ).astype(jnp.bfloat16)
        dout_heads = split_heads(d_attended)
        d_probs = jnp.einsum(
            "qhe,khe->hqk", dout_heads, split_heads(values_all), preferred_element_type=jnp.float32
        )
        delta_rows = jnp.sum(soft_probs * d_probs, axis=-1)
        d_scores = (soft_probs * (d_probs - delta_rows[..., None])).astype(jnp.bfloat16)
        d_query = (
            (
                jnp.einsum(
                    "hqk,khe->qhe",
                    d_scores,
                    split_heads(keys_all),
                    preferred_element_type=jnp.float32,
                )
                * SCALE
            )
            .reshape(local_len, model_width)
            .astype(jnp.bfloat16)
        )
        key_part = (
            jnp.einsum(
                "hqk,qhe->khe", d_scores, split_heads(queries), preferred_element_type=jnp.float32
            )
            * SCALE
        ).reshape(row_length, model_width)
        value_part = jnp.einsum(
            "hqk,qhe->khe", low_probs, dout_heads, preferred_element_type=jnp.float32
        ).reshape(row_length, model_width)
        d_keys, d_values = (
            lax.psum_scatter(
                key_part.astype(jnp.bfloat16), "seq", scatter_dimension=0, tiled=True
            ).astype(jnp.float32),
            lax.psum_scatter(
                value_part.astype(jnp.bfloat16), "seq", scatter_dimension=0, tiled=True
            ).astype(jnp.float32),
        )
        d_values_low = d_values.astype(jnp.bfloat16)
        d_joined = jnp.concatenate([d_query, d_keys.astype(jnp.bfloat16), d_values_low], axis=1)
        g_qkv_w = jnp.einsum("td,tf->df", normed_one, d_joined, preferred_element_type=jnp.float32)
        g_q_b = token_sum(d_query)
        g_v_b = token_sum(d_values_low)
        d_normed_one = jnp.einsum(
            "tf,df->td", d_joined, weights[2], preferred_element_type=jnp.float32
        )
        norm_value_one, norm_one_back = jax.vjp(norm_rows, inputs, weights[0], weights[1])
        d_inputs_norm, g_gain_one, g_bias_one = norm_one_back(d_normed_one)
        d_inputs = d_resid + d_inputs_norm
        new_grads = (
            g_gain_one,
            g_bias_one,
            g_qkv_w,
            g_q_b,
            g_v_b,
            g_out_w,
            g_out_b,
            g_gain_two,
            g_bias_two,
            g_in_w,
            g_in_b,
            g_back_w,
            g_back_b,
        )
        totals = tuple(
            (
                running + jnp.where(is_valid, grad_new, 0.0)
                for running, grad_new in zip(totals, new_grads)
            )
        )
        shown = jnp.where(
            section_rank == 0, d_inputs, d_inputs.astype(jnp.bfloat16).astype(jnp.float32)
        )
        in_grads = store_slot(in_grads, shown, slot_idx, is_valid)
        passed = from_behind(d_inputs.astype(jnp.bfloat16), "section", -1)
        return (passed, in_grads, totals)

    back_state = (
        jnp.zeros((local_len, model_width), jnp.bfloat16),
        jnp.zeros((micro_count, local_len, model_width), jnp.float32),
        tuple((jnp.zeros(weight.shape, jnp.float32) for weight in weights)),
    )
    ignored_grad, in_grads, totals = lax.fori_loop(0, tick_count, backward_tick, back_state)
    reduced = lax.psum_scatter(totals, ("dp", "seq"), scatter_dimension=0, tiled=True)
    return (
        outputs[None],
        in_grads[None],
        reduced[0][None],
        reduced[1][None],
        reduced[2][None],
        reduced[3][None],
        reduced[4][None],
        reduced[5][None],
        reduced[6][None],
        reduced[7][None],
        reduced[8][None],
        reduced[9][None],
        reduced[10][None],
        reduced[11][None],
        reduced[12][None],
    )


HEAD = 64
BIG = 1e30
NT = (((1,), (1,)), ((), ()))
F32 = jnp.float32
BF16 = jnp.bfloat16
BLK = 256
CH = 256
FINE = 128
PIECE = 512
UN = 8

def lane_mask(shape, h):
    lane = lax.broadcasted_iota(jnp.int32, shape, len(shape) - 1)
    return (lane < HEAD) if h == 0 else (lane >= HEAD)

def only(x, h):
    return jnp.where(lane_mask(x.shape, h), x, jnp.zeros_like(x))

def fwd_kernel(lo_ref, hi_ref, q_ref, k_ref, v_ref, fq_ref, fk_ref, o_ref, lse_ref):
    i = pl.program_id(0)
    n, w = k_ref.shape
    pairs = w // 128
    lo = lo_ref[i]
    count = hi_ref[i] - lo

    def run(lo, c):
        fq = fq_ref[...]
        at = pl.multiple_of(lo * FINE, FINE)
        pieces = []
        done = 0
        while done < c * FINE:
            size = min(PIECE, c * FINE - done)
            pieces.append(pl.ds(pl.multiple_of(at + done, FINE), size))
            done += size

        def scores(u, rows):
            p, h = divmod(u, 2)
            cols = slice(p * 128, (p + 1) * 128)
            q = q_ref[:, cols] * jnp.asarray(SCALE, BF16)
            qa = jnp.concatenate([only(q, h), fq], axis=1)
            kb = jnp.concatenate([k_ref[rows, cols], fk_ref[rows, :]], axis=1)
            return lax.dot_general(qa, kb, NT, preferred_element_type=F32)

        now = [scores(0, rows) for rows in pieces]
        outs, lses = [], []
        for u in range(2 * pairs):
            p, h = divmod(u, 2)
            cols = slice(p * 128, (p + 1) * 128)
            m = jnp.max(now[0], axis=1, keepdims=True)
            for s in now[1:]:
                m = jnp.maximum(m, jnp.max(s, axis=1, keepdims=True))
            r = None
            later = []
            for s, rows in zip(now, pieces):
                if u + 1 < 2 * pairs:
                    later.append(scores(u + 1, rows))
                pr = jnp.exp(s - m).astype(BF16)
                vb = jnp.concatenate([v_ref[rows, cols], jnp.ones((s.shape[1], 128), BF16)], axis=1)
                part = jnp.dot(pr, vb, preferred_element_type=F32)
                r = part if r is None else r + part
            now = later
            l = r[:, 128:]
            outs.append(r[:, :128] / l)
            lses.append(m + jnp.log(l))
            if h == 1:
                mask = lane_mask((BLK, 128), 0)
                o_ref[:, cols] = jnp.where(mask, outs[0], outs[1]).astype(BF16)
                both = jnp.where(mask, lses[0], lses[1]).T
                lse_ref[p, 0:1, :] = both[0:1, :]
                lse_ref[p, 1:2, :] = both[HEAD:HEAD + 1, :]
                outs, lses = [], []

    most = n // FINE
    below = 0
    for c in sorted({max(BLK // FINE, most * e // 16) for e in (2, 4, 6, 8, 11, 13, 14, 16)}):
        @pl.when((count > below) & (count <= c))
        def _(c=c):
            run(jnp.minimum(lo, most - c), c)
        below = c

def attn_fwd(lo, hi, q, k, v, fq, fk):
    n, w = q.shape
    pairs = w // 128
    blk = lambda i, lo, hi: (i, 0)
    full = lambda i, lo, hi: (0, 0)
    return pl.pallas_call(
        fwd_kernel,
        grid_spec=pltpu.PrefetchScalarGridSpec(
            num_scalar_prefetch=2,
            grid=(n // BLK,),
            in_specs=[pl.BlockSpec((BLK, w), blk), pl.BlockSpec((n, w), full), pl.BlockSpec((n, w), full),
                      pl.BlockSpec((BLK, 128), blk), pl.BlockSpec((n, 128), full)],
            out_specs=[pl.BlockSpec((BLK, w), blk), pl.BlockSpec((pairs, 8, BLK), lambda i, lo, hi: (0, 0, i))],
        ),
        out_shape=[jax.ShapeDtypeStruct((n, w), BF16), jax.ShapeDtypeStruct((pairs, 8, n), F32)],
        compiler_params=pltpu.CompilerParams(vmem_limit_bytes=62 * 2 ** 20),
        name="attn_fwd",
    )(lo, hi, q, k, v, fq, fk)

def bwd_kernel(lo_ref, hi_ref, q_ref, k_ref, v_ref, do_ref, o_ref, lse_ref, fq_ref, fk_ref,
               dq_ref, dk_ref, dv_ref, delta, dqt, dk_acc, dv_acc):
    j = pl.program_id(0)
    nb = pl.num_programs(0)
    n, w = q_ref.shape
    pairs = w // 128

    @pl.when(j == 0)
    def _():
        head = lax.broadcasted_iota(jnp.int32, (16, 128), 0)
        lane = lax.broadcasted_iota(jnp.int32, (16, 128), 1)
        sel = jnp.where(lane // HEAD == head, 1.0, 0.0).astype(BF16)

        def prep(b, c):
            rows = pl.ds(pl.multiple_of(b * CH, CH), CH)
            for p in range(pairs):
                cols = slice(p * 128, (p + 1) * 128)
                prod = do_ref[rows, cols].astype(F32) * o_ref[rows, cols].astype(F32)
                hi = prod.astype(BF16)
                lo = (prod - hi.astype(F32)).astype(BF16)
                d = lax.dot_general(sel, hi, NT, preferred_element_type=F32) + lax.dot_general(sel, lo, NT, preferred_element_type=F32)
                delta[p, :, rows] = d[0:8, :]
                dqt[p, :, rows] = jnp.zeros((128, CH), F32)
            return c
        lax.fori_loop(0, n // CH, prep, 0)

    lo = lo_ref[j]
    count = hi_ref[j] - lo
    dk_acc[...] = jnp.zeros_like(dk_acc)
    dv_acc[...] = jnp.zeros_like(dv_acc)

    def run(first, c):
        rows = pl.ds(pl.multiple_of(first * FINE, FINE), c * FINE)
        units = 2 * pairs

        def scores(u):
            p, h = divmod(u, 2)
            cols = slice(p * 128, (p + 1) * 128)
            kb = jnp.concatenate([only(k_ref[:, cols] * jnp.asarray(SCALE, BF16), h), fk_ref[...]], axis=1)
            qa = jnp.concatenate([q_ref[rows, cols], fq_ref[rows, :]], axis=1)
            s = lax.dot_general(kb, qa, NT, preferred_element_type=F32)
            dp = lax.dot_general(only(v_ref[:, cols], h), do_ref[rows, cols], NT, preferred_element_type=F32)
            return s, dp

        now = scores(0)
        dk, dv = [], []
        for u in range(units):
            p, h = divmod(u, 2)
            cols = slice(p * 128, (p + 1) * 128)
            later = scores(u + 1) if u + 1 < units else None
            s, dp = now
            pr = jnp.exp(s - lse_ref[p, h:h + 1, rows])
            ds = (pr * (dp - delta[p, h:h + 1, rows])).astype(BF16)
            dv.append(jnp.dot(pr.astype(BF16), do_ref[rows, cols], preferred_element_type=F32))
            dk.append(jnp.dot(ds, q_ref[rows, cols], preferred_element_type=F32))
            kt = (k_ref[:, cols] * jnp.asarray(SCALE, BF16)).T
            dqt[p, h * HEAD:(h + 1) * HEAD, rows] += jnp.dot(kt[h * HEAD:(h + 1) * HEAD, :], ds, preferred_element_type=F32)
            now = later
            if h == 1:
                mask = lane_mask((BLK, 128), 0)
                dk_acc[:, cols] += jnp.where(mask, dk[0], dk[1])
                dv_acc[:, cols] += jnp.where(mask, dv[0], dv[1])
                dk, dv = [], []

    @pl.loop(0, count // UN)
    def _(t):
        run(lo + t * UN, UN)

    left = count % UN
    for c in range(1, UN):
        @pl.when(left == c)
        def _(c=c):
            run(lo + (count - left), c)
    dk_ref[...] = (dk_acc[...] * SCALE).astype(BF16)
    dv_ref[...] = dv_acc[...].astype(BF16)

    @pl.when(j == nb - 1)
    def _():
        def fin(b, c):
            rows = pl.ds(pl.multiple_of(b * CH, CH), CH)
            for p in range(pairs):
                dq_ref[rows, p * 128:(p + 1) * 128] = dqt[p, :, rows].T.astype(BF16)
            return c
        lax.fori_loop(0, n // CH, fin, 0)

def attn_bwd(lo, hi, q, k, v, do, o, lse, fq, fk):
    n, w = q.shape
    pairs = w // 128
    full = lambda j, lo, hi: (0, 0)
    blk = lambda j, lo, hi: (j, 0)
    sh = jax.ShapeDtypeStruct((n, w), BF16)
    big = pl.BlockSpec((n, w), full, pipeline_mode=pl.Buffered(1))
    return pl.pallas_call(
        bwd_kernel,
        grid_spec=pltpu.PrefetchScalarGridSpec(
            num_scalar_prefetch=2,
            grid=(n // BLK,),
            in_specs=[big, pl.BlockSpec((BLK, w), blk), pl.BlockSpec((BLK, w), blk), big, big, pl.BlockSpec((pairs, 8, n), lambda j, lo, hi: (0, 0, 0)),
                      pl.BlockSpec((n, 128), full), pl.BlockSpec((BLK, 128), blk)],
            out_specs=[pl.BlockSpec((n, w), full), pl.BlockSpec((BLK, w), blk), pl.BlockSpec((BLK, w), blk)],
            scratch_shapes=[
                pltpu.VMEM((pairs, 8, n), F32),
                pltpu.VMEM((pairs, 128, n), F32),
                pltpu.VMEM((BLK, w), F32),
                pltpu.VMEM((BLK, w), F32),
            ],
        ),
        out_shape=[sh, sh, sh],
        compiler_params=pltpu.CompilerParams(vmem_limit_bytes=62 * 2 ** 20),
        name="attn_bwd",
    )(lo, hi, q, k, v, do, o, lse, fq, fk)

def segment_terms(lengths, n):
    cells = lengths.shape[0]
    place_of = jnp.arange(cells)
    ends = jnp.sum(jnp.where(place_of[:, None] <= place_of[None, :], lengths[:, None], 0), axis=0)
    starts = ends - lengths
    pos = jnp.arange(n, dtype=jnp.int32)[:, None]
    pad = lambda v: jnp.pad(v, (0, 128 - cells))[None, :]
    hot = (pos >= pad(starts)) & (pos < pad(ends))
    used = (jnp.arange(128) < cells)[None, :]
    fq = jnp.where(hot, -BIG, 0.0).astype(BF16)
    fk = jnp.where(used & ~hot, 1.0, 0.0).astype(BF16)
    first = jnp.arange(n // BLK, dtype=jnp.int32)[:, None] * BLK
    lo = jnp.max(jnp.where(starts[None, :] <= first, starts[None, :], 0), axis=1) // FINE
    hi = (jnp.min(jnp.where(ends[None, :] > first + BLK - 1, ends[None, :], n), axis=1) + FINE - 1) // FINE
    return fq, fk, lo.astype(jnp.int32), hi.astype(jnp.int32)


MIB = 2 ** 20
MESH = pl.DeviceIdType.MESH
ANY = pl.BlockSpec(memory_space=pl.ANY)
VMEM = pl.BlockSpec(memory_space=pltpu.VMEM)
DMA = pltpu.SemaphoreType.DMA
TOK = 256
COLS = 768


def sds(shape, dtype):
    return jax.ShapeDtypeStruct(shape, dtype)


def place():
    section, dp, seq = lax.axis_index("section"), lax.axis_index("dp"), lax.axis_index("seq")
    core = lax.rem(dp, 2)
    return section, dp, seq, core


def greet(*devices):
    barrier = pltpu.get_barrier_semaphore()
    for device in devices:
        pl.semaphore_signal(barrier, 1, device_id=device, device_id_type=MESH)
    pl.semaphore_wait(barrier, len(devices))


def column_mates(section, dp, seq, core):
    mates = [(section, dp, lax.rem(seq + t, 4)) for t in range(1, 4)]
    mates += [(section, dp + 1 - 2 * core, lax.rem(seq + t, 4)) for t in range(4)]
    return mates


def remote(src, dst, send_sem, recv_sem, device):
    return pltpu.make_async_remote_copy(
        src_ref=src, dst_ref=dst, send_sem=send_sem, recv_sem=recv_sem,
        device_id=device, device_id_type=MESH,
    )


def span(start, size):
    return pl.ds(pl.multiple_of(start, size), size)


def chunk(i):
    return span(i * TOK, TOK)


def row_norm(values):
    centre = jnp.mean(values, axis=-1, keepdims=True)
    offset = values - centre
    spread = jnp.mean(offset * offset, axis=-1, keepdims=True)
    rstd = lax.rsqrt(spread + EPS)
    return offset * rstd, rstd


def row_norm_back(grad, hat, rstd, gain):
    d_hat = grad * gain
    mean_d = jnp.mean(d_hat, axis=-1, keepdims=True)
    mean_dh = jnp.mean(d_hat * hat, axis=-1, keepdims=True)
    return rstd * (d_hat - mean_d - hat * mean_dh)


def fold(values):
    return jnp.sum(values.reshape(values.shape[0] // 8, 8, values.shape[1]), axis=0)


def up(ref):
    return ref[...].astype(F32)


def gelu_parts(x):
    size = jnp.abs(x)
    d = 1.0 + 0.2316418882 * size
    t = pl.reciprocal(d, approx=True)
    t = t * (2.0 - d * t)
    density = jnp.exp(-0.5 * (x * x)) * 0.3989422804014327
    poly = ((((1.330274429 * t - 1.821255978) * t + 1.781477937) * t - 0.356563782) * t + 0.319381530) * t
    tail = density * poly
    phi = jnp.where(x >= 0.0, 1.0 - tail, tail)
    return x * phi, phi + x * density


def ffn_loads(wo_in, win_in, wback_in, wo, win, wback, sem):
    pairs = [(wo_in, wo)]
    for f in range(win.shape[1] // COLS):
        cols = pl.ds(f * COLS, COLS)
        pairs += [(win_in.at[:, cols], win.at[:, cols]), (wback_in.at[cols], wback.at[cols])]
    return [pltpu.make_async_copy(a, b, sem.at[n]) for n, (a, b) in enumerate(pairs)]


class ToHeads:
    def __init__(self, buf, outs, tokens, width, sems, core, sibling):
        self.buf, self.outs, self.tokens, self.width = buf, outs, tokens, width
        self.own_sem, self.send_sem, self.recv_sem = sems
        self.core, self.sibling = core, sibling

    def _cols(self, part, core):
        return span(part * self.width + core * (self.width // 2), self.width // 2)

    def _sent(self, i, part, owner):
        rows = span(owner * self.tokens + i * TOK, TOK)
        return remote(self.buf.at[chunk(i), self._cols(part, 1 - self.core)], self.outs[part].at[rows],
                      self.send_sem.at[part, i], self.recv_sem.at[part, i], self.sibling)

    def _own(self, i, part):
        rows = span(self.core * self.tokens + i * TOK, TOK)
        return pltpu.make_async_copy(self.buf.at[chunk(i), self._cols(part, self.core)],
                                     self.outs[part].at[rows], self.own_sem.at[part, i])

    def start(self, i):
        for part in range(len(self.outs)):
            self._own(i, part).start()
            self._sent(i, part, self.core).start()

    def wait(self, i):
        for part in range(len(self.outs)):
            self._own(i, part).wait()
            self._sent(i, part, self.core).wait_send()
            self._sent(i, part, 1 - self.core).wait_recv()


class ToTokens:
    def __init__(self, ins, buf, tokens, width, sems, core, sibling):
        self.ins, self.buf, self.tokens, self.width = ins, buf, tokens, width
        self.own_sem, self.send_sem, self.recv_sem = sems
        self.core, self.sibling = core, sibling

    def _cols(self, part, core):
        return span(part * self.width + core * (self.width // 2), self.width // 2)

    def _sent(self, i, part, owner):
        rows = span((1 - self.core) * self.tokens + i * TOK, TOK)
        return remote(self.ins[part].at[rows], self.buf.at[chunk(i), self._cols(part, owner)],
                      self.send_sem.at[part, i], self.recv_sem.at[part, i], self.sibling)

    def _own(self, i, part):
        rows = span(self.core * self.tokens + i * TOK, TOK)
        return pltpu.make_async_copy(self.ins[part].at[rows], self.buf.at[chunk(i), self._cols(part, self.core)],
                                     self.own_sem.at[part, i])

    def start(self, i):
        for part in range(len(self.ins)):
            self._own(i, part).start()
            self._sent(i, part, self.core).start()

    def wait(self, i):
        for part in range(len(self.ins)):
            self._own(i, part).wait()
            self._sent(i, part, 1 - self.core).wait_recv()

    def wait_sent(self, i):
        for part in range(len(self.ins)):
            self._sent(i, part, self.core).wait_send()


def swap_sems(parts, steps):
    return [DMA((parts, steps))] * 3


class Blocks:
    def __init__(self, rows_ref, blocks_ref, gather, sems, section, dp, seq, core):
        self.rows, self.blocks, self.gather = rows_ref, blocks_ref, gather
        self.bounce, self.own_sem, self.send_sem, self.recv_sem = sems
        self.section, self.seq, self.core, self.column = section, seq, core, dp - core
        self.each, self.local, _ = blocks_ref.shape

    def _move(self, j):
        target_core, target_seq = self.seq // self.each, self.core * self.each + j
        slot = lax.rem(self.seq, self.each)
        here = (target_core == self.core) & (target_seq == self.seq)
        if self.gather:
            src, dst = self.blocks.at[j], self.rows.at[span(slot * self.local, self.local)]
        else:
            src, dst = self.rows.at[pl.ds(j * self.local, self.local)], self.blocks.at[slot]
        target = (self.section, self.column + target_core, target_seq)
        return here, src, dst, slot, target

    def start(self, *which):
        for j in which or range(self.each):
            here, src, dst, slot, target = self._move(j)

            @pl.when(here)
            def _():
                pltpu.make_async_copy(src, dst if self.bounce is None else self.bounce, self.own_sem).start()

            @pl.when(jnp.logical_not(here))
            def _():
                remote(src, dst, self.send_sem.at[j], self.recv_sem.at[slot], target).start()

    def wait(self):
        for j in range(self.each):
            here, src, dst, slot, target = self._move(j)

            @pl.when(here)
            def _():
                pltpu.make_async_copy(src, dst if self.bounce is None else self.bounce, self.own_sem).wait()
                if self.bounce is not None:
                    out = pltpu.make_async_copy(self.bounce, dst, self.own_sem)
                    out.start()
                    out.wait()

            @pl.when(jnp.logical_not(here))
            def _():
                remote(src, dst, self.send_sem.at[j], self.recv_sem.at[slot], target).wait_send()
        for j in range(self.each):
            here = (self.seq // self.each == self.core) & (self.core * self.each + j == self.seq)
            mate = (self.section, self.column + 1 - self.core, self.seq)
            if self.gather:
                dst = self.rows.at[pl.ds(j * self.local, self.local)]
                src = self.blocks.at[0]
            else:
                dst = self.blocks.at[j]
                src = self.rows.at[pl.ds(0, self.local)]

            @pl.when(jnp.logical_not(here))
            def _():
                remote(src, dst, self.send_sem.at[0], self.recv_sem.at[j], mate).wait_recv()


def block_scratch(each, local, width):
    return [pltpu.VMEM((local, width), BF16), DMA, DMA((each,)), DMA((each,))]


def project(x, gain, bias, w, qb, vb, buf, rows):
    width = x.shape[1]
    hat, _ = row_norm(x)
    a = (hat * up(gain) + up(bias)).astype(BF16)
    for part in range(3):
        cols = slice(part * width, (part + 1) * width)
        m = jnp.dot(a, w[:, cols], preferred_element_type=F32)
        if part == 0:
            m = m + up(qb)
        if part == 2:
            m = m + up(vb)
        buf[rows, cols] = m.astype(BF16)
    return a


def first_kernel(x_ref, w_in, gain, bias, qb, vb, x_out, q_ref, k_ref, v_ref,
                 xb, w, buf, w_sem, out_sem, own_sem, send_sem, recv_sem, *sems):
    section, dp, seq, core = place()
    sibling = (section, dp + 1 - 2 * core, seq)
    each, local, width = x_ref.shape
    part = local // 2
    column = dp - core
    load = pltpu.make_async_copy(w_in, w, w_sem)
    load.start()
    greet(*[(s, column + c, z) for s in range(2) for c in range(2) for z in range(2 * each)])

    def move(m):
        target_core, target_seq = seq // each, core * each + m
        slot = lax.rem(seq, each)
        here = (section == 0) & (target_core == core) & (target_seq == seq)
        src = x_ref.at[m, span(section * part, part)]
        dst = xb.at[span(slot * local + section * part, part)]
        return here, src, dst, slot, (0, column + target_core, target_seq)

    for m in range(each):
        here, src, dst, slot, target = move(m)

        @pl.when(here)
        def _():
            pltpu.make_async_copy(src, dst, own_sem).start()

        @pl.when(jnp.logical_not(here))
        def _():
            remote(src, dst, send_sem.at[m], recv_sem.at[section, slot], target).start()
    load.wait()

    @pl.when(section == 0)
    def _():
        swap = ToHeads(buf, (q_ref, k_ref, v_ref), each * local, width, sems, core, sibling)

        def out(i):
            return pltpu.make_async_copy(xb.at[chunk(i)], x_out.at[chunk(i)], out_sem.at[i])

        for h in range(2):
            for j in range(each):
                here = (seq // each == core) & (core * each + j == seq) & (h == 0)
                dst = xb.at[pl.ds(j * local + h * part, part)]

                @pl.when(here)
                def _():
                    pltpu.make_async_copy(x_ref.at[0, pl.ds(0, part)], dst, own_sem).wait()

                @pl.when(jnp.logical_not(here))
                def _():
                    remote(x_ref.at[0, pl.ds(0, part)], dst, send_sem.at[0], recv_sem.at[h, j], sibling).wait_recv()

                for i in range((j * local + h * part) // TOK, (j * local + (h + 1) * part) // TOK):
                    rows = slice(i * TOK, (i + 1) * TOK)
                    project(xb[rows, :].astype(F32), gain, bias, w, qb, vb, buf, rows)
                    out(i).start()
                    swap.start(i)
        for i in range(each * local // TOK):
            out(i).wait()
            swap.wait(i)

    for m in range(each):
        here, src, dst, slot, target = move(m)

        @pl.when(jnp.logical_not(here))
        def _():
            remote(src, dst, send_sem.at[m], recv_sem.at[section, slot], target).wait_send()


def first_call(x, w, gain, bias, qb, vb):
    each, local, width = x.shape
    tokens = each * local
    steps = tokens // TOK
    out = sds((2 * tokens, width // 2), BF16)
    return pl.pallas_call(
        first_kernel,
        in_specs=[ANY, ANY] + [VMEM] * 4,
        out_specs=[ANY] * 4,
        out_shape=[sds((tokens, width), BF16), out, out, out],
        scratch_shapes=[
            pltpu.VMEM((tokens, width), BF16), pltpu.VMEM(w.shape, BF16), pltpu.VMEM((tokens, 3 * width), BF16),
            DMA, DMA((steps,)), DMA, DMA((each,)), DMA((2, each))] + swap_sems(3, steps),
        compiler_params=pltpu.CompilerParams(collective_id=1, has_side_effects=True, vmem_limit_bytes=62 * MIB),
        name="rows_qkv",
    )(x, w, gain, bias, qb, vb)


def feed(i, out, att, x, wo, win, wback, bo, g2, b2, bi, bb, keep=None, ready=None):
    rows = chunk(i)
    hidden = win.shape[1]
    if ready:
        ready[0].wait()
    resid = x[rows, :].astype(F32) + up(bo) + jnp.dot(att[rows, :], wo[...], preferred_element_type=F32)
    hat, rstd = row_norm(resid)
    c = (hat * up(g2) + up(b2)).astype(BF16)
    if keep is not None:
        resid_b, slope_b, att_t, c_t, act_t = keep
        resid_b[rows, :] = resid
        att_t[:, rows] = att[rows, :].T
        c_t[:, rows] = c.T
    total = resid + up(bb)
    yield
    for f in range(hidden // COLS):
        cols = slice(f * COLS, (f + 1) * COLS)
        if ready:
            ready[1 + 2 * f].wait()
            ready[2 + 2 * f].wait()
        inner = jnp.dot(c, win[:, cols], preferred_element_type=F32) + bi[:, cols].astype(F32)
        yield
        active, slope = gelu_parts(inner)
        active = active.astype(BF16)
        if keep is not None:
            slope_b[rows, cols] = slope.astype(BF16)
            act_t[cols, rows] = active.T
        total = total + jnp.dot(active, wback[cols, :], preferred_element_type=F32)
        yield
    out[rows, :] = total.astype(BF16)


def feed_back(i, dy, slope_b, resid_b, wo, win, wback, g2, di_b, dr_b, dp_b, da_b, sums):
    rows = chunk(i)
    hidden = win.shape[1]
    g = dy.astype(F32)
    d_c = jnp.zeros(dy.shape, F32)
    yield
    for f in range(hidden // COLS):
        cols = slice(f * COLS, (f + 1) * COLS)
        d_active = lax.dot_general(dy, wback[cols, :], NT, preferred_element_type=F32)
        yield
        d_inner = d_active * slope_b[rows, cols].astype(F32)
        if sums:
            sums[3][:, cols] += fold(d_inner)
        d_inner = d_inner.astype(BF16)
        if di_b is not None:
            di_b[rows, cols] = d_inner
        d_c = d_c + lax.dot_general(d_inner, win[:, cols], NT, preferred_element_type=F32)
        yield
    hat, rstd = row_norm(resid_b[rows, :])
    d_resid = g + row_norm_back(d_c, hat, rstd, up(g2))
    d_proj = d_resid.astype(BF16)
    dr_b[rows, :] = d_resid
    if sums:
        s_gain, s_bias, s_out, _, s_back = sums
        s_gain[...] += fold(d_c * hat)
        s_bias[...] += fold(d_c)
        s_out[...] += fold(d_resid)
        s_back[...] += fold(g)
    if dp_b is not None:
        dp_b[rows, :] = d_proj
    da_b[rows, :] = lax.dot_general(d_proj, wo[...], NT, preferred_element_type=F32).astype(BF16)


def in_turns(*parts):
    parts = list(parts)
    while parts:
        for part in list(parts):
            if next(part, part) is part:
                parts.remove(part)


def pass_kernel(o_ref, x_ref, g_ref, wo_in, win_in, wback_in, wqkv_in, bo, g2, b2, bi, bb, g1, b1, qb, vb,
                x_out, g_out, n_out, q_ref, k_ref, v_ref,
                wo, win, wback, wqkv, att, yb, xn, buf, w_sem, x_send, x_recv, x_sem, *sems):
    section, dp, seq, core = place()
    sibling = (section, dp + 1 - 2 * core, seq)
    across = (1 - section, dp, seq)
    tokens, width = x_ref.shape
    steps = tokens // TOK
    loads = ffn_loads(wo_in, win_in, wback_in, wo, win, wback, w_sem)
    load_qkv = pltpu.make_async_copy(wqkv_in, wqkv, w_sem.at[len(loads)])
    loads[0].start()
    greet(across, *column_mates(section, dp, seq, core))
    to_tokens = ToTokens((o_ref,), att, tokens, width, sems[:3], core, sibling)
    to_heads = ToHeads(buf, (q_ref, k_ref, v_ref), tokens, width, sems[3:6], core, sibling)
    blocks = Blocks(g_out, g_ref, True, sems[6:10], section, dp, seq, core)
    to_tokens.start(0)
    for load in loads[1:]:
        load.start()

    @pl.loop(1, steps)
    def _(i):
        to_tokens.start(i)

    load_qkv.start()

    @pl.when(section == 1)
    def _():
        blocks.start()

    def passed(i):
        return remote(yb.at[chunk(i)], xn.at[chunk(i)], x_send.at[i], x_recv.at[i], across)

    def kept(i):
        return pltpu.make_async_copy(xn.at[chunk(i)], x_out.at[chunk(i)], x_sem.at[i])

    def send_chunk(i, ready=None):
        in_turns(feed(i, yb, att, x_ref, wo, win, wback, bo, g2, b2, bi, bb, ready=ready))
        passed(i).start()
        xn[chunk(i), :] = x_ref[chunk(i), :]

    to_tokens.wait(0)

    @pl.when(section == 0)
    def _():
        send_chunk(0, loads)

    @pl.when(section == 1)
    def _():
        for load in loads:
            load.wait()

    @pl.loop(1, steps)
    def _(i):
        to_tokens.wait(i)

        @pl.when(section == 0)
        def _():
            send_chunk(i)

    load_qkv.wait()

    @pl.loop(0, steps)
    def _(i):
        @pl.when(section == 1)
        def _():
            passed(i).wait_recv()

        kept(i).start()
        a = project(xn[chunk(i), :].astype(F32), g1, b1, wqkv, qb, vb, buf, chunk(i))
        n_out[:, chunk(i)] = a.T
        to_heads.start(i)

    @pl.loop(0, steps)
    def _(i):
        to_tokens.wait_sent(i)
        to_heads.wait(i)
        kept(i).wait()

        @pl.when(section == 0)
        def _():
            passed(i).wait_send()

    @pl.when(section == 1)
    def _():
        blocks.wait()


def pass_call(o, x, g, wo, win, wback, wqkv, vectors):
    tokens, width = x.shape
    steps = tokens // TOK
    each = g.shape[0]
    out = sds((2 * tokens, width // 2), BF16)
    low = sds(x.shape, BF16)
    low_buf = pltpu.VMEM(x.shape, BF16)
    return pl.pallas_call(
        pass_kernel,
        in_specs=[ANY, VMEM, ANY, ANY, ANY, ANY, ANY] + [VMEM] * len(vectors),
        out_specs=[ANY, ANY, VMEM, ANY, ANY, ANY],
        out_shape=[low, low, sds((width, tokens), BF16), out, out, out],
        scratch_shapes=[pltpu.VMEM(w.shape, BF16) for w in (wo, win, wback, wqkv)]
        + [low_buf, low_buf, low_buf, pltpu.VMEM((tokens, 3 * width), BF16),
           DMA((2 + 2 * (win.shape[1] // COLS),)), DMA((steps,)), DMA((steps,)), DMA((steps,))]
        + swap_sems(1, steps) + swap_sems(3, steps) + block_scratch(each, tokens // each, width),
        compiler_params=pltpu.CompilerParams(collective_id=2, has_side_effects=True, vmem_limit_bytes=62 * MIB),
        name="ffn_pass_qkv",
    )(o, x, g, wo, win, wback, wqkv, *vectors)


def turn_kernel(o_ref, x_ref, g_ref, wo_in, win_in, wback_in, bo, g2, b2, bi, bb,
                y_out, resid_out, slope_out, att_out, c_out, act_out, dr_out, da_ref,
                wo, win, wback, att, yb, resid_b, slope_b, att_t, c_t, act_t, dr_b, da_b,
                w_sem, out_sem, *sems):
    section, dp, seq, core = place()
    sibling = (section, dp + 1 - 2 * core, seq)
    tokens, width = x_ref.shape
    steps = tokens // TOK
    loads = ffn_loads(wo_in, win_in, wback_in, wo, win, wback, w_sem)
    loads[0].start()
    greet(sibling)
    to_tokens = ToTokens((o_ref,), att, tokens, width, sems[:3], core, sibling)
    to_heads = ToHeads(da_b, (da_ref,), tokens, width, sems[3:6], core, sibling)
    to_tokens.start(0)
    for load in loads[1:]:
        load.start()

    @pl.loop(1, steps)
    def _(i):
        to_tokens.start(i)

    def copies(i, which, at, turned=False):
        where = (slice(None), chunk(i)) if turned else (chunk(i),)
        return [pltpu.make_async_copy(b.at[where], o.at[where], out_sem.at[at + n, i]) for n, (b, o) in enumerate(which)]

    def results(i):
        return copies(i, ((yb, y_out), (resid_b, resid_out), (slope_b, slope_out)), 0) + copies(
            i, ((att_t, att_out), (c_t, c_out), (act_t, act_out)), 3, True)

    def back_results(i):
        return copies(i, ((dr_b, dr_out),), 6)

    def forward(i, ready=None):
        return feed(i, yb, att, x_ref, wo, win, wback, bo, g2, b2, bi, bb, (resid_b, slope_b, att_t, c_t, act_t), ready)

    def backward(i):
        return feed_back(i, g_ref[chunk(i), :], slope_b, resid_b, wo, win, wback, g2, None, dr_b, None, da_b, None)

    to_tokens.wait(0)
    in_turns(forward(0, loads))
    for copy in results(0):
        copy.start()

    @pl.loop(1, steps)
    def _(i):
        to_tokens.wait(i)
        in_turns(forward(i))
        in_turns(backward(i - 1))
        to_heads.start(i - 1)
        for copy in results(i) + back_results(i - 1):
            copy.start()

    in_turns(backward(steps - 1))
    to_heads.start(steps - 1)
    for copy in back_results(steps - 1):
        copy.start()

    @pl.loop(0, steps)
    def _(i):
        to_tokens.wait_sent(i)
        to_heads.wait(i)
        for copy in results(i) + back_results(i):
            copy.wait()


def turn_call(o, x, g, wo, win, wback, vectors):
    tokens, width = x.shape
    hidden = win.shape[1]
    steps = tokens // TOK
    low, full = sds(x.shape, BF16), sds(x.shape, F32)
    turned = sds((width, tokens), BF16)
    outs = [low, full, sds((tokens, hidden), BF16), turned, turned, sds((hidden, tokens), BF16), full]
    buf = lambda s: pltpu.VMEM(s.shape, s.dtype)
    return pl.pallas_call(
        turn_kernel,
        in_specs=[ANY, VMEM, VMEM, ANY, ANY, ANY] + [VMEM] * len(vectors),
        out_specs=[ANY] * 8,
        out_shape=outs + [sds((2 * tokens, width // 2), BF16)],
        scratch_shapes=[buf(wo), buf(win), buf(wback), buf(low)] + [buf(s) for s in outs] + [buf(low)]
        + [DMA((1 + 2 * (hidden // COLS),)), DMA((7, steps))] + swap_sems(1, steps) + swap_sems(1, steps),
        compiler_params=pltpu.CompilerParams(collective_id=3, has_side_effects=True, vmem_limit_bytes=62 * MIB),
        name="ffn_turn",
    )(o, x, g, wo, win, wback, *vectors)


def input_back(i, dj, dr, x, w, gain, sums):
    rows = chunk(i)
    width = x.shape[1]
    d_a = lax.dot_general(dj[rows, :], w[...], NT, preferred_element_type=F32)
    hat, rstd = row_norm(x[rows, :].astype(F32))
    if sums:
        s_gain, s_bias, s_q, s_v = sums
        s_q[...] += fold(dj[rows, :width].astype(F32))
        s_v[...] += fold(dj[rows, 2 * width:].astype(F32))
        s_gain[...] += fold(d_a * hat)
        s_bias[...] += fold(d_a)
    return (dr[rows, :] + row_norm_back(d_a, hat, rstd, up(gain))).astype(BF16)


def back_kernel(dq_ref, dk_ref, dv_ref, dr_ref, x_ref, y_ref, g_in, slope_in, resid_in, c_in, act_in,
                wqkv_in, wo_in, win_in, wback_in, g1, g2,
                y_out, dr_out, dp_out, da_ref, *rest):
    rest = list(rest)
    shares = [rest.pop(0) for _ in range(4)]
    y_shares = [rest.pop(0) for _ in range(2)]
    s_gain, s_bias, s_out, s_in, s_back = [rest.pop(0) for _ in range(5)]
    wqkv, wo, win, wback, dj, dx, gb, di, dr, dp, da_b, c_t, act_t, grad_in, grad_back = [rest.pop(0) for _ in range(15)]
    (w_sem, in_sem, a_sem, t_sem, out_sem, g_sem, x_send, x_recv, ready, r_send, r_recv, r_out) = rest[:12]
    sems = rest[12:]
    section, dp_index, seq, core = place()
    sibling = (section, dp_index + 1 - 2 * core, seq)
    across = (1 - section, dp_index, seq)
    tokens, width = gb.shape
    hidden = win.shape[1]
    steps = tokens // TOK
    blocks_of = hidden // COLS
    x_b, dr_in = da_b, grad_back
    loads = [pltpu.make_async_copy(a, b, w_sem.at[n]) for n, (a, b) in enumerate(
        ((wqkv_in, wqkv), (wback_in, wback), (win_in, win), (wo_in, wo), (c_in, c_t)))]

    def kept(i):
        return [pltpu.make_async_copy(a.at[chunk(i)], b.at[chunk(i)], in_sem.at[n, i])
                for n, (a, b) in enumerate(((slope_in, di), (resid_in, dr)))]

    def turned(i):
        return pltpu.make_async_copy(act_in.at[:, chunk(i)], act_t.at[lax.rem(i, 2)], t_sem.at[i])

    def given(i):
        return [pltpu.make_async_copy(a.at[chunk(i)], b.at[chunk(i)], a_sem.at[n, i])
                for n, (a, b) in enumerate(((x_ref, x_b), (dr_ref, dr_in)))]

    def last(i):
        return pltpu.make_async_copy(g_in.at[chunk(i)], gb.at[chunk(i)], g_sem.at[i])

    def passed(i):
        return remote(dx.at[chunk(i)], gb.at[chunk(i)], x_send.at[i], x_recv.at[i], across)

    def results(i):
        return [pltpu.make_async_copy(b.at[chunk(i)], o.at[chunk(i)], out_sem.at[n, i])
                for n, (b, o) in enumerate(((dr, dr_out), (dp, dp_out)))]

    @pl.when(section == 1)
    def _():
        loads[0].start()

    greet(across, *column_mates(section, dp_index, seq, core))
    to_tokens = ToTokens((dq_ref, dk_ref, dv_ref), dj, tokens, width, sems[:3], core, sibling)
    to_heads = ToHeads(da_b, (da_ref,), tokens, width, sems[3:6], core, sibling)
    blocks = Blocks(y_ref, y_out, False, sems[6:10], section, dp_index, seq, core)

    @pl.when(section == 1)
    def _():
        @pl.loop(0, steps)
        def _(i):
            to_tokens.start(i)
            for copy in given(i):
                copy.start()

        loads[0].wait()

        @pl.loop(0, steps)
        def _(i):
            to_tokens.wait(i)
            for copy in given(i):
                copy.wait()
            last(i).start()
            dx[chunk(i), :] = input_back(i, dj, dr_in, x_b, wqkv, g1, None)
            passed(i).start()

    for load in loads[1:]:
        load.start()

    @pl.loop(0, steps)
    def _(i):
        for copy in kept(i):
            copy.start()

    for i in range(2):
        turned(i).start()
    blocks.start()
    sums = (s_gain, s_bias, s_out, s_in, s_back)
    for s in sums + (grad_in, grad_back):
        s[...] = jnp.zeros_like(s)
    for load in loads[1:]:
        load.wait()

    def grad_block(i, n):
        part = span(n % blocks_of * COLS, COLS) if not isinstance(n, int) else pl.ds(n % blocks_of * COLS, COLS)
        if n < blocks_of:
            grad_in[:, part] += jnp.dot(c_t[:, chunk(i)], di[chunk(i), part], preferred_element_type=F32)
        else:
            grad_back[part, :] += jnp.dot(act_t[lax.rem(i, 2), part, :], gb[chunk(i), :], preferred_element_type=F32)

    def feed_step(i):
        for copy in kept(i):
            copy.wait()

        @pl.when(section == 0)
        def _():
            passed(i).wait_recv()

        @pl.when(section == 1)
        def _():
            last(i).wait()

        in_turns(feed_back(i, gb[chunk(i), :], di, dr, wo, win, wback, g2, di, dr, dp, da_b, sums))
        to_heads.start(i)
        for copy in results(i):
            copy.start()

    @pl.loop(0, steps - 1)
    def _(i):
        feed_step(i)
        turned(i).wait()
        for n in range(2 * blocks_of):
            grad_block(i, n)

        @pl.when(i + 2 < steps)
        def _():
            turned(i + 2).start()

    end = steps - 1
    feed_step(end)
    pl.semaphore_signal(ready, 1, device_id=sibling, device_id_type=MESH)
    turned(end).wait()
    pl.semaphore_wait(ready, 1)

    size_in, size_back = width // 16, hidden // 16

    def sent_in(n, yy):
        cols = pl.ds(n * COLS, COLS)
        return remote(win.at[pl.ds(yy * 4 * size_in, 4 * size_in), cols],
                      win.at[pl.ds((2 + yy) * 4 * size_in, 4 * size_in), cols],
                      r_send.at[2 * n + yy], r_recv.at[2 * n + yy], sibling)

    def sent_back(n):
        yy = n // 2
        return remote(wback.at[pl.ds(yy * COLS, COLS)], wback.at[pl.ds((2 + yy) * COLS, COLS)],
                      r_send.at[2 * blocks_of + yy], r_recv.at[2 * blocks_of + yy], sibling)

    def write_in(t, yy):
        rows = span((2 + yy) * 4 * size_in + lax.rem(seq + t, 4) * size_in, size_in)
        return pltpu.make_async_copy(win.at[rows], shares[t].at[pl.ds(yy * size_in, size_in)], r_out.at[t, yy])

    def write_back(t):
        yy = (dp_index // 2 + t) % 2
        return pltpu.make_async_copy(wback.at[span((2 + yy) * COLS, COLS)], y_shares[t], r_out.at[4, t])

    for n in range(blocks_of):
        grad_block(end, n)
        cols = slice(n * COLS, (n + 1) * COLS)
        for yy in range(2):
            win[yy * 4 * size_in:(yy + 1) * 4 * size_in, cols] = grad_in[core_rows(size_in, yy, 1 - core), cols].astype(BF16)
            sent_in(n, yy).start()
    for n in range(blocks_of):
        grad_block(end, blocks_of + n)
        if n % 2 == 1:
            yy = n // 2
            wback[yy * COLS:(yy + 1) * COLS, :] = grad_back[core_rows(size_back, yy, 1 - core), :].astype(BF16)
            sent_back(n).start()
    for n in range(blocks_of):
        cols = slice(n * COLS, (n + 1) * COLS)
        for yy in range(2):
            sent_in(n, yy).wait_recv()
            rows = slice((2 + yy) * 4 * size_in, (3 + yy) * 4 * size_in)
            win[rows, cols] = (grad_in[core_rows(size_in, yy, core), cols] + win[rows, cols].astype(F32)).astype(BF16)
    for yy in range(2):
        for t in range(4):
            write_in(t, yy).start()
    for yy in range(2):
        sent_back(2 * yy).wait_recv()
        rows = slice((2 + yy) * COLS, (3 + yy) * COLS)
        wback[rows, :] = (grad_back[core_rows(size_back, yy, core), :] + wback[rows, :].astype(F32)).astype(BF16)
    for t in range(2):
        write_back(t).start()

    @pl.loop(0, steps)
    def _(i):
        to_heads.wait(i)
        for copy in results(i):
            copy.wait()

        @pl.when(section == 1)
        def _():
            to_tokens.wait_sent(i)
            passed(i).wait_send()

    for yy in range(2):
        for n in range(blocks_of):
            sent_in(n, yy).wait_send()
        sent_back(2 * yy).wait_send()
        write_back(yy).wait()
        for t in range(4):
            write_in(t, yy).wait()
    blocks.wait()


def back_call(dq, dk, dv, dr, x, y, g, slope, resid, c_t, act_t, wqkv, wo, win, wback, g1, g2, each):
    tokens, width = x.shape
    hidden = win.shape[1]
    steps = tokens // TOK
    blocks_of = hidden // COLS
    low, full, wide = sds(x.shape, BF16), sds(x.shape, F32), sds((tokens, hidden), BF16)
    one = sds((8, width), F32)
    buf = lambda s: pltpu.VMEM(s.shape, s.dtype)
    shares = [sds((width // 8, hidden), BF16)] * 4 + [sds((hidden // 4, width), BF16)] * 2
    return pl.pallas_call(
        back_kernel,
        in_specs=[ANY] * 15 + [VMEM, VMEM],
        out_specs=[ANY] * 10 + [VMEM] * 5,
        out_shape=[sds((each, tokens // each, width), BF16), full, low, sds((2 * tokens, width // 2), BF16)]
        + shares + [one, one, one, sds((8, hidden), F32), one],
        scratch_shapes=[buf(wqkv), buf(wo), buf(win), buf(wback), pltpu.VMEM((tokens, 3 * width), BF16),
                        buf(low), buf(low), buf(wide), buf(full), buf(low), buf(low), buf(c_t),
                        pltpu.VMEM((2, hidden, TOK), BF16), pltpu.VMEM((width, hidden), F32), pltpu.VMEM((hidden, width), F32),
                        DMA((5,)), DMA((2, steps)), DMA((2, steps)), DMA((steps,)), DMA((2, steps)), DMA((steps,)),
                        DMA((steps,)), DMA((steps,)), pltpu.SemaphoreType.REGULAR,
                        DMA((2 * blocks_of + 2,)), DMA((2 * blocks_of + 2,)), DMA((5, 2))]
        + swap_sems(3, steps) + swap_sems(1, steps) + block_scratch(each, tokens // each, width),
        compiler_params=pltpu.CompilerParams(collective_id=4, has_side_effects=True, vmem_limit_bytes=62 * MIB),
        name="qkv_back_pass",
    )(dq, dk, dv, dr, x, y, g, slope, resid, c_t, act_t, wqkv, wo, win, wback, g1, g2)


def core_rows(size, yy, core):
    return span((2 * yy + core) * 4 * size, 4 * size)


def attn_plan(width):
    return [(width, width, 0, 0)] + [(width, width, 1, i * width) for i in range(3)]


def piece(left, right, at, cols, out):
    step = min(left.shape[0], 1024)

    @pl.loop(0, left.shape[0] // step)
    def _(r):
        block = span(r * step, step)
        out[block, :] = jnp.dot(left[block, :], right[:, at:at + cols], preferred_element_type=F32).astype(BF16)


def grads_kernel(n_small, *refs):
    refs = list(refs)
    d_parts = [refs.pop(0) for _ in range(3)]
    dr_ref, x_ref, w_in, g1 = [refs.pop(0) for _ in range(4)]
    lefts = [refs.pop(0) for _ in range(2)]
    rights = [refs.pop(0)]
    ffn_in = [refs.pop(0) for _ in range(4)]
    back_in = [refs.pop(0) for _ in range(2)]
    sums = [refs.pop(0) for _ in range(n_small)]
    outs = [refs.pop(0) for _ in range(2)]
    ffn_out, back_out = refs.pop(0), refs.pop(0)
    small_out, dx_out = refs.pop(0), refs.pop(0)
    left_buf = [refs.pop(0) for _ in range(2)]
    right_buf = [refs.pop(0) for _ in range(2)]
    w, dr, x, dxb = [refs.pop(0) for _ in range(4)]
    own_sums = [refs.pop(0) for _ in range(4)]
    dj = right_buf[1]
    ffn_buf, ffn_rec, back_buf, back_rec = [refs.pop(0) for _ in range(4)]
    width, tokens = lefts[0].shape
    plan = attn_plan(width)
    buf1 = [refs.pop(0) for _ in plan]
    rec1 = [refs.pop(0) for _ in plan]
    rec2 = [refs.pop(0) for _ in plan]
    rec3 = [refs.pop(0) for _ in plan]
    small, small1, small2, small3 = [refs.pop(0) for _ in range(4)]
    (load_sem, s1_send, s1_recv, s2_send, s2_recv, s3_send, s3_recv,
     m_send, m_recv, f_send, f_recv, f_load, b_load, b_send, b_recv, in_sem) = refs[:16]

    section, dp, seq, core = place()
    y = dp // 2
    sibling = (section, dp + 1 - 2 * core, seq)
    across_y = (section, dp + 2 - 4 * y, seq)
    along = [(section, dp, lax.rem(seq + t, 4)) for t in range(1, 4)]
    count = len(plan)
    steps = tokens // TOK
    load_w = pltpu.make_async_copy(w_in, w, load_sem.at[1, 1])
    loads = [[pltpu.make_async_copy(lefts[0], left_buf[0], load_sem.at[0, 0]),
              pltpu.make_async_copy(rights[0], right_buf[0], load_sem.at[1, 0])],
             [pltpu.make_async_copy(lefts[1], left_buf[1], load_sem.at[0, 1])]]

    def given(i):
        return [pltpu.make_async_copy(a.at[chunk(i)], b.at[chunk(i)], in_sem.at[n, i])
                for n, (a, b) in enumerate(((x_ref, x), (dr_ref, dr)))]

    greet(across_y, *column_mates(section, dp, seq, core))
    to_tokens = ToTokens(d_parts, dj, tokens, width, refs[16:19], core, sibling)
    blocks = Blocks(dxb, dx_out, False, [None] + refs[19:22], section, dp, seq, core)
    ffn_loads = [pltpu.make_async_copy(ffn_in[t], ffn_buf.at[t], f_load.at[t]) for t in range(4)]
    back_loads = [pltpu.make_async_copy(back_in[t], back_buf.at[t], b_load.at[t]) for t in range(2)]
    for load in back_loads:
        load.start()

    @pl.loop(0, steps)
    def _(i):
        to_tokens.start(i)
        for copy in given(i):
            copy.start()

    load_w.start()
    for pair in loads:
        for load in pair:
            load.start()
    for load in ffn_loads:
        load.start()

    def ffn_half(yy):
        rows = ffn_rec.shape[0]
        return span(yy * rows, rows)

    def ffn_sent():
        return remote(ffn_buf.at[0, ffn_half(1 - y)], ffn_rec, f_send, f_recv, across_y)

    def ffn_sum(yy):
        rows = ffn_half(yy)
        total = ffn_buf[0, rows, :].astype(F32)
        for t in range(1, 4):
            total = total + ffn_buf[t, rows, :].astype(F32)
        return total

    next_z = seq + 1 - 2 * lax.rem(seq, 2)
    far_z = lax.rem(seq + 2, 4)

    def back_rows(zz):
        rows = back_rec.shape[1]
        return span(zz * rows, rows)

    def back_near(t):
        return remote(back_buf.at[0, back_rows(lax.rem(next_z + 2 * t, 4))], back_rec.at[t],
                      b_send.at[t], b_recv.at[t], (section, dp, next_z))

    def back_far():
        return remote(back_buf.at[0, back_rows(far_z)], back_rec.at[2], b_send.at[2], b_recv.at[2], (section, dp, far_z))

    def back_add(rows, other):
        back_buf[0, rows, :] = (back_buf[0, rows, :].astype(F32) + other.astype(F32)).astype(BF16)

    size = width // 16

    def half(yy):
        return span(yy * 4 * size, 4 * size)

    def first(p, yy):
        return remote(buf1[p].at[core_rows(size, yy, 1 - core)], rec1[p].at[half(yy)],
                      s1_send.at[p, yy], s1_recv.at[p, yy], sibling)

    def second(p):
        return remote(rec1[p].at[half(1 - y)], rec2[p], s2_send.at[p], s2_recv.at[p], across_y)

    def shard(zz):
        return span(y * 4 * size + zz * size, size)

    def third(p, t):
        target = (section, dp, next_z)
        return remote(rec1[p].at[shard(lax.rem(next_z + 2 * t, 4))], rec3[p].at[t],
                      s3_send.at[p, t], s3_recv.at[p, t], target)

    def fourth(p):
        return remote(rec1[p].at[shard(far_z)], rec3[p].at[2], s3_send.at[p, 2], s3_recv.at[p, 2], (section, dp, far_z))

    def reduce_core(p):
        for yy in range(2):
            first(p, yy).wait_recv()
            total = buf1[p][core_rows(size, yy, core), :].astype(F32) + rec1[p][half(yy), :].astype(F32)
            rec1[p][half(yy), :] = total.astype(BF16)
        second(p).start()

    def reduce_y(p):
        second(p).wait_recv()
        mine = half(y)
        rec1[p][mine, :] = (rec1[p][mine, :].astype(F32) + rec2[p][...].astype(F32)).astype(BF16)
        for t in range(2):
            third(p, t).start()

    def reduce_next(p):
        for t, zz in enumerate((seq, far_z)):
            third(p, t).wait_recv()
            rec1[p][shard(zz), :] = (rec1[p][shard(zz), :].astype(F32) + rec3[p][t].astype(F32)).astype(BF16)
        fourth(p).start()

    def reduce_far(p):
        rows, cols, t_out, at = plan[p]
        fourth(p).wait_recv()
        outs[t_out][:, at:at + cols] = rec1[p][shard(seq), :].astype(F32) + rec3[p][2].astype(F32)

    for load in back_loads:
        load.wait()
    back_buf[0] = (back_buf[0].astype(F32) + back_buf[1].astype(F32)).astype(BF16)
    for t in range(2):
        back_near(t).start()

    for s in own_sums:
        s[...] = jnp.zeros_like(s)
    load_w.wait()
    per = steps // dx_out.shape[0]
    for j in range(dx_out.shape[0]):
        @pl.loop(j * per, (j + 1) * per)
        def _(i):
            to_tokens.wait(i)
            for copy in given(i):
                copy.wait()
            dxb[chunk(i), :] = input_back(i, dj, dr, x, w, g1, own_sums)

        blocks.start(j)

    line = 0
    for s in own_sums + sums:
        row = jnp.sum(s[...], axis=0, keepdims=True)
        for t in range(s.shape[1] // 128):
            small[line:line + 1, :] = row[:, t * 128:(t + 1) * 128]
            line += 1
    v1 = remote(small, small1, m_send.at[0], m_recv.at[0], sibling)
    v2 = remote(small, small2, m_send.at[1], m_recv.at[1], across_y)

    def v3(t):
        return remote(small, small3.at[t - 1], m_send.at[1 + t], m_recv.at[1 + t], along[t - 1])

    v1.start()
    v1.wait()
    small[...] += small1[...]
    v2.start()
    ready = set()
    for p, (rows, cols, t, at) in enumerate(plan):
        if t not in ready:
            ready.add(t)
            for load in loads[t]:
                load.wait()
        piece(left_buf[t], right_buf[t], at, cols, buf1[p])
        for yy in range(2):
            first(p, yy).start()
        if p > 0:
            reduce_core(p - 1)
        if p == 1:
            v2.wait()
            small[...] += small2[...]
            for t in range(1, 4):
                v3(t).start()
    reduce_core(count - 1)
    for t, zz in enumerate((seq, far_z)):
        back_near(t).wait_recv()
        back_add(back_rows(zz), back_rec[t])
    back_far().start()
    for load in ffn_loads:
        load.wait()
    ffn_buf[0, ffn_half(1 - y), :] = ffn_sum(1 - y).astype(BF16)
    ffn_sent().start()
    for p in range(count):
        reduce_y(p)
        if p > 0:
            reduce_next(p - 1)
    reduce_next(count - 1)
    own = ffn_sum(y)
    ffn_sent().wait_recv()
    ffn_out[...] = own + ffn_rec[...].astype(F32)
    back_far().wait_recv()
    back_out[...] = back_buf[0, back_rows(seq), :].astype(F32) + back_rec[2].astype(F32)
    for t in range(1, 4):
        v3(t).wait()
    small_out[...] = small[...] + small3[0] + small3[1] + small3[2]
    for p in range(count):
        reduce_far(p)

    for p in range(count):
        for yy in range(2):
            first(p, yy).wait_send()
        second(p).wait_send()
        for t in range(2):
            third(p, t).wait_send()
        fourth(p).wait_send()
    @pl.loop(0, steps)
    def _(i):
        to_tokens.wait_sent(i)

    ffn_sent().wait_send()
    for t in range(2):
        back_near(t).wait_send()
    back_far().wait_send()
    blocks.wait()


def grads_call(d_parts, dr, x, w, g1, att_t, norm_t, d_proj, ffn, back, sums, each):
    width, tokens = att_t.shape
    plan = attn_plan(width)
    count = len(plan)
    steps = tokens // TOK
    one = sds((8, width), F32)
    lines = (4 * width + sum(s.shape[1] for s in sums)) // 128
    vec = pltpu.VMEM((lines, 128), F32)
    buf = lambda s: pltpu.VMEM(s.shape, s.dtype)
    half = (ffn[0].shape[0] // 2, ffn[0].shape[1])
    quarter = (back[0].shape[0] // 4, back[0].shape[1])
    return pl.pallas_call(
        partial(grads_kernel, len(sums)),
        in_specs=[ANY] * 6 + [VMEM] + [ANY] * 9 + [VMEM] * len(sums),
        out_specs=[VMEM] * 5 + [ANY],
        out_shape=[sds((width // 16, width), F32), sds((width // 16, 3 * width), F32)]
        + [sds(half, F32), sds(quarter, F32)]
        + [sds((lines, 128), F32), sds((each, tokens // each, width), BF16)],
        scratch_shapes=(
            [buf(att_t), buf(norm_t), buf(d_proj), pltpu.VMEM((tokens, 3 * width), BF16), buf(w), buf(dr), buf(x), buf(x)]
            + [buf(one)] * 4
            + [pltpu.VMEM((4,) + ffn[0].shape, BF16), pltpu.VMEM(half, BF16),
               pltpu.VMEM((2,) + back[0].shape, BF16), pltpu.VMEM((3,) + quarter, BF16)]
            + [pltpu.VMEM((r, c), BF16) for r, c, *_ in plan]
            + [pltpu.VMEM((r // 2, c), BF16) for r, c, *_ in plan]
            + [pltpu.VMEM((r // 4, c), BF16) for r, c, *_ in plan]
            + [pltpu.VMEM((3, r // 16, c), BF16) for r, c, *_ in plan]
            + [vec, vec, vec, pltpu.VMEM((3, lines, 128), F32)]
            + [DMA((2, 2)), DMA((count, 2)), DMA((count, 2)), DMA((count,)), DMA((count,)),
               DMA((count, 3)), DMA((count, 3)), DMA((5,)), DMA((5,)), DMA, DMA, DMA((4,)), DMA((2,)), DMA((3,)), DMA((3,)),
               DMA((2, steps))]
            + swap_sems(3, steps) + [DMA, DMA((each,)), DMA((each,))]),
        compiler_params=pltpu.CompilerParams(collective_id=8, has_side_effects=True, vmem_limit_bytes=62 * MIB),
        name="weight_grads",
    )(*d_parts, dr, x, w, g1, att_t, norm_t, d_proj, *ffn, *back, *sums)


def finish_kernel(dx_ref, y_ref, *refs):
    count = (len(refs) - 2) // 2
    ins, (dx_out, y_out), outs = refs[:count], refs[count:count + 2], refs[count + 2:]
    dx_out[...] = dx_ref[...].astype(F32)
    y_out[...] = y_ref[...]

    @pl.when(pl.program_id(0) == 0)
    def _():
        for a, b in zip(ins, outs):
            b[...] = a[...]


def finish_call(dx, y, *arrays):
    each, local, width = dx.shape
    block = pl.BlockSpec((1, local // 2, width), lambda i: (i // 2, i % 2, 0))
    whole = [pl.BlockSpec(a.shape, lambda i: (0, 0)) for a in arrays]
    return pl.pallas_call(
        finish_kernel,
        grid=(2 * each,),
        in_specs=[block, block] + whole,
        out_specs=[block, block] + whole,
        out_shape=[sds(dx.shape, F32), sds(y.shape, y.dtype)] + [sds(a.shape, a.dtype) for a in arrays],
        compiler_params=pltpu.CompilerParams(vmem_limit_bytes=62 * MIB),
        name="finish",
    )(dx, y, *arrays)


def swap_cores(x):
    size = lax.axis_size("dp")
    return lax.ppermute(x, "dp", [(i, i ^ 1) for i in range(size)])


def swap_y(x):
    size = lax.axis_size("dp")
    return lax.ppermute(x, "dp", [(i, i ^ 2) for i in range(size)])


def along_seq(x, by):
    size = lax.axis_size("seq")
    return lax.ppermute(x, "seq", [(i, (i + by) % size) for i in range(size)])


def on_device_rows(cell_tokens, cell_lengths, out_grad, *raw_weights):
    (gain1, bias1, wqkv, qb, vb, wo, bo, gain2, bias2, win, bi, wback, bb) = tuple(
        (w if w.ndim == 2 else w[0] for w in raw_weights)
    )
    each, local, width = cell_tokens.shape
    row_length = local * lax.axis_size("seq")
    core = lax.axis_index("dp") % 2
    z = lax.axis_index("seq")

    lengths = jnp.where(z // each == core, cell_lengths, swap_cores(cell_lengths))
    lengths = lax.dynamic_index_in_dim(lengths, z % each, 0, keepdims=False)
    fq, fk, lo, hi = segment_terms(lengths, row_length)

    x, q, k, v = first_call(cell_tokens, wqkv, gain1, bias1, qb, vb)
    o, _ = attn_fwd(lo, hi, q, k, v, fq, fk)
    x, g, norm_t, q, k, v = pass_call(
        o, x, out_grad, wo, win, wback, wqkv, (bo, gain2, bias2, bi, bb, gain1, bias1, qb, vb))
    o, lse = attn_fwd(lo, hi, q, k, v, fq, fk)
    y, resid, slope, att_t, c_t, act_t, dr, do = turn_call(o, x, g, wo, win, wback, (bo, gain2, bias2, bi, bb))

    dq, dk, dv = attn_bwd(lo, hi, q, k, v, do, o, lse, fq, fk)
    outputs, dr, dp, do, *rest = back_call(
        dq, dk, dv, dr, x, y, g, slope, resid, c_t, act_t, wqkv, wo, win, wback, gain1, gain2, each)
    ffn = [w if t == 0 else along_seq(w, t) for t, w in enumerate(rest[:4])]
    back = [rest[4], swap_y(rest[5])]
    s_gain2, s_bias2, s_out, s_in, s_back = rest[6:]
    dq, dk, dv = attn_bwd(lo, hi, q, k, v, do, o, lse, fq, fk)
    sums = (s_out, s_gain2, s_bias2, s_in, s_back)
    g_out, g_qkv, g_in, g_back, small, in_grads = grads_call(
        (dq, dk, dv), dr, x, wqkv, gain1, att_t, norm_t, dp, ffn, back, sums, each)
    in_grads, outputs, g_out, g_qkv, g_in, g_back = finish_call(in_grads, outputs, g_out, g_qkv, g_in, g_back)

    flat = small.reshape(-1)
    parts = lax.axis_size("dp") * lax.axis_size("seq")
    owner = lax.axis_index("dp") * lax.axis_size("seq") + z
    shares, at = [], 0
    for total in [width] * 4 + [s.shape[1] for s in sums]:
        size = total // parts
        shares.append(lax.dynamic_slice_in_dim(flat, at + owner * size, size))
        at += total
    return (
        outputs[None],
        in_grads[None],
        shares[0][None],
        shares[1][None],
        g_qkv[None],
        shares[2][None],
        shares[3][None],
        g_out[None],
        shares[4][None],
        shares[5][None],
        shares[6][None],
        g_in[None],
        shares[7][None],
        g_back[None],
        shares[8][None],
    )


def either_plan(cell_tokens, *others):
    one_chip = lax.axis_size("dp") % 2 == 0 and lax.axis_size("seq") == 2 * cell_tokens.shape[0] and lax.axis_size("section") == 2 and lax.axis_size("dp") == lax.axis_size("seq") == 4
    return (on_device_rows if one_chip else on_device)(cell_tokens, *others)


def solution(mesh):
    in_specs = (
        P("dp", "seq", None),
        P("dp", None),
        P("dp", "seq", None),
        P("section", None),
        P("section", None),
        P("section", None, None),
        P("section", None),
        P("section", None),
        P("section", None, None),
        P("section", None),
        P("section", None),
        P("section", None),
        P("section", None, None),
        P("section", None),
        P("section", None, None),
        P("section", None),
    )
    out_specs = (
        P("section", "dp", "seq", None),
        P("section", "dp", "seq", None),
        P("section", ("dp", "seq")),
        P("section", ("dp", "seq")),
        P("section", ("dp", "seq"), None),
        P("section", ("dp", "seq")),
        P("section", ("dp", "seq")),
        P("section", ("dp", "seq"), None),
        P("section", ("dp", "seq")),
        P("section", ("dp", "seq")),
        P("section", ("dp", "seq")),
        P("section", ("dp", "seq"), None),
        P("section", ("dp", "seq")),
        P("section", ("dp", "seq"), None),
        P("section", ("dp", "seq")),
    )
    return jax.shard_map(
        either_plan, mesh=mesh, in_specs=in_specs, out_specs=out_specs, check_vma=False
    )
```

```python
from functools import partial

import jax
import jax.numpy as jnp
from jax import lax
from jax.experimental import pallas as pl
from jax.experimental.pallas import tpu as pltpu
from jax.sharding import PartitionSpec as P

HEADS = 12


SCALE = 0.125
EPS = 1e-05
MASKED = -1e30


def from_behind(x, axis, by):
    peers = lax.axis_size(axis)
    pairs = [(i, i + by) for i in range(peers) if 0 <= i + by < peers]
    return lax.ppermute(x, axis, pairs)


def norm_rows(values, gain_vec, bias_vec):
    centre = jnp.mean(values, axis=-1, keepdims=True)
    offset = values - centre
    spread = jnp.mean(offset * offset, axis=-1, keepdims=True)
    return offset * lax.rsqrt(spread + EPS) * gain_vec + bias_vec


def row_segments(lengths, row_length):
    limits = jnp.cumsum(lengths, axis=-1)
    places = jnp.arange(row_length, dtype=jnp.int32)
    return jnp.sum((places[None, :, None] >= limits[:, None, :]).astype(jnp.int32), axis=-1)


def split_heads(values):
    return values.reshape(values.shape[0], HEADS, values.shape[1] // HEADS)


def masked_scores(queries, keys_in, seg_query, seg_keys):
    scores = (
        jnp.einsum(
            "qhe,khe->hqk",
            split_heads(queries),
            split_heads(keys_in),
            preferred_element_type=jnp.float32,
        )
        * SCALE
    )
    return jnp.where((seg_query[:, None] == seg_keys[None, :])[None], scores, MASKED)


def softmax_parts(scores):
    highest = jnp.max(scores, axis=-1)
    raised = jnp.exp(scores - highest[..., None])
    summed = jnp.sum(raised, axis=-1)
    return (raised / summed[..., None], highest, summed)


def project_in(inputs, weights):
    normed = norm_rows(inputs, weights[0], weights[1]).astype(jnp.bfloat16)
    joined = jnp.dot(normed, weights[2], preferred_element_type=jnp.float32)
    model_width = inputs.shape[1]
    queries = (joined[:, :model_width] + weights[3]).astype(jnp.bfloat16)
    keys_out = joined[:, model_width : 2 * model_width].astype(jnp.bfloat16)
    values_out = (joined[:, 2 * model_width :] + weights[4]).astype(jnp.bfloat16)
    return (normed, queries, keys_out, values_out)


def attend(queries, keys_all, values_all, seg_own, seg_row):
    soft_probs, highest, summed = softmax_parts(masked_scores(queries, keys_all, seg_own, seg_row))
    low_probs = soft_probs.astype(jnp.bfloat16)
    combined = jnp.einsum(
        "hqk,khe->qhe", low_probs, split_heads(values_all), preferred_element_type=jnp.float32
    )
    return (
        combined.reshape(queries.shape).astype(jnp.bfloat16),
        soft_probs,
        low_probs,
        highest,
        summed,
    )


def finish(inputs, attended, weights):
    resid_sum = (
        inputs + jnp.dot(attended, weights[5], preferred_element_type=jnp.float32) + weights[6]
    )
    normed = norm_rows(resid_sum, weights[7], weights[8]).astype(jnp.bfloat16)
    hidden_pre = jnp.dot(normed, weights[9], preferred_element_type=jnp.float32) + weights[10]
    active = jax.nn.gelu(hidden_pre, approximate=False).astype(jnp.bfloat16)
    result = (
        resid_sum + jnp.dot(active, weights[11], preferred_element_type=jnp.float32) + weights[12]
    )
    return (result, resid_sum, normed, hidden_pre, active)


def store_slot(buffer, item_new, slot_idx, is_valid):
    current = lax.dynamic_index_in_dim(buffer, slot_idx, 0, keepdims=False)
    return lax.dynamic_update_index_in_dim(
        buffer, jnp.where(is_valid, item_new, current), slot_idx, 0
    )


def token_sum(values):
    return jnp.sum(values.astype(jnp.float32), axis=0)


def on_device(
    cell_tokens,
    cell_lengths,
    out_grad,
    norm1_gain,
    norm1_bias,
    qkv_weight,
    query_bias,
    value_bias,
    out_weight,
    out_bias,
    norm2_gain,
    norm2_bias,
    in_weight,
    in_bias,
    back_weight,
    back_bias,
):
    raw_weights = (
        norm1_gain,
        norm1_bias,
        qkv_weight,
        query_bias,
        value_bias,
        out_weight,
        out_bias,
        norm2_gain,
        norm2_bias,
        in_weight,
        in_bias,
        back_weight,
        back_bias,
    )
    weights = tuple(
        (weight[0].astype(jnp.float32) if weight.ndim == 2 else weight[0] for weight in raw_weights)
    )
    sections = lax.axis_size("section")
    section_rank = lax.axis_index("section")
    micro_count, local_len, model_width = cell_tokens.shape
    row_length = local_len * lax.axis_size("seq")
    own_start = lax.axis_index("seq") * local_len
    segments = row_segments(cell_lengths, row_length)
    tick_count = micro_count + sections - 1
    kept_depth = 1

    def row_segs(slot_idx):
        seg_row = lax.dynamic_index_in_dim(segments, slot_idx, 0, keepdims=False)
        return (seg_row, lax.dynamic_slice_in_dim(seg_row, own_start, local_len))

    def forward_tick(tick_now, state_now):
        incoming, kept_in, outputs, kept_keys, kept_values = state_now
        index_now = tick_now - section_rank
        is_valid = (index_now >= 0) & (index_now < micro_count)
        slot_idx = jnp.clip(index_now, 0, micro_count - 1)
        first_in = lax.dynamic_index_in_dim(cell_tokens, slot_idx, 0, keepdims=False)
        layer_in = jnp.where(section_rank == 0, first_in, incoming)
        seg_row, seg_own = row_segs(slot_idx)
        inputs = layer_in.astype(jnp.float32)
        normed, queries, keys_out, values_out = project_in(inputs, weights)
        keys_all, values_all = (
            lax.all_gather(keys_out, "seq", axis=0, tiled=True),
            lax.all_gather(values_out, "seq", axis=0, tiled=True),
        )
        attended = attend(queries, keys_all, values_all, seg_own, seg_row)[0]
        result = finish(inputs, attended, weights)[0].astype(jnp.bfloat16)
        kept_in = store_slot(kept_in, layer_in, slot_idx, is_valid)
        outputs = store_slot(outputs, result, slot_idx, is_valid)
        passed = from_behind(result, "section", 1)
        return (passed, kept_in, outputs, kept_keys, kept_values)

    start_state = (
        jnp.zeros((local_len, model_width), jnp.bfloat16),
        jnp.zeros((micro_count, local_len, model_width), jnp.bfloat16),
        jnp.zeros((micro_count, local_len, model_width), jnp.bfloat16),
        jnp.zeros((kept_depth, row_length, model_width), jnp.bfloat16),
        jnp.zeros((kept_depth, row_length, model_width), jnp.bfloat16),
    )
    ignored, kept_in, outputs, kept_keys, kept_values = lax.fori_loop(
        0, tick_count, forward_tick, start_state
    )

    def backward_tick(tick_now, state_now):
        incoming, in_grads, totals = state_now
        index_now = tick_now - (sections - 1 - section_rank)
        is_valid = (index_now >= 0) & (index_now < micro_count)
        slot_idx = jnp.clip(index_now, 0, micro_count - 1)
        from_out = lax.dynamic_index_in_dim(out_grad, slot_idx, 0, keepdims=False)
        grad_out = jnp.where(section_rank == sections - 1, from_out, incoming).astype(jnp.float32)
        inputs = lax.dynamic_index_in_dim(kept_in, slot_idx, 0, keepdims=False).astype(jnp.float32)
        seg_row, seg_own = row_segs(slot_idx)
        normed_one, queries, keys_out, values_out = project_in(inputs, weights)
        keys_all, values_all = (
            lax.all_gather(keys_out, "seq", axis=0, tiled=True),
            lax.all_gather(values_out, "seq", axis=0, tiled=True),
        )
        attended, soft_probs, low_probs, highest, summed = attend(
            queries, keys_all, values_all, seg_own, seg_row
        )
        result, resid_sum, normed_two, hidden_pre, active = finish(inputs, attended, weights)
        d_result = grad_out.astype(jnp.bfloat16)
        g_back_w = jnp.einsum("tf,td->fd", active, d_result, preferred_element_type=jnp.float32)
        g_back_b = token_sum(d_result)
        d_active = jnp.einsum(
            "td,fd->tf", d_result, weights[11], preferred_element_type=jnp.float32
        )
        gelu_value, gelu_back = jax.vjp(partial(jax.nn.gelu, approximate=False), hidden_pre)
        d_hidden = gelu_back(d_active)[0].astype(jnp.bfloat16)
        g_in_w = jnp.einsum("td,tf->df", normed_two, d_hidden, preferred_element_type=jnp.float32)
        g_in_b = token_sum(d_hidden)
        d_normed_two = jnp.einsum(
            "tf,df->td", d_hidden, weights[9], preferred_element_type=jnp.float32
        )
        norm_value, norm_two_back = jax.vjp(norm_rows, resid_sum, weights[7], weights[8])
        d_resid_norm, g_gain_two, g_bias_two = norm_two_back(d_normed_two)
        d_resid = grad_out + d_resid_norm
        d_proj = d_resid.astype(jnp.bfloat16)
        g_out_w = jnp.einsum("td,te->de", attended, d_proj, preferred_element_type=jnp.float32)
        g_out_b = token_sum(d_proj)
        d_attended = jnp.einsum(
            "te,de->td", d_proj, weights[5], preferred_element_type=jnp.float32
        ).astype(jnp.bfloat16)
        dout_heads = split_heads(d_attended)
        d_probs = jnp.einsum(
            "qhe,khe->hqk", dout_heads, split_heads(values_all), preferred_element_type=jnp.float32
        )
        delta_rows = jnp.sum(soft_probs * d_probs, axis=-1)
        d_scores = (soft_probs * (d_probs - delta_rows[..., None])).astype(jnp.bfloat16)
        d_query = (
            (
                jnp.einsum(
                    "hqk,khe->qhe",
                    d_scores,
                    split_heads(keys_all),
                    preferred_element_type=jnp.float32,
                )
                * SCALE
            )
            .reshape(local_len, model_width)
            .astype(jnp.bfloat16)
        )
        key_part = (
            jnp.einsum(
                "hqk,qhe->khe", d_scores, split_heads(queries), preferred_element_type=jnp.float32
            )
            * SCALE
        ).reshape(row_length, model_width)
        value_part = jnp.einsum(
            "hqk,qhe->khe", low_probs, dout_heads, preferred_element_type=jnp.float32
        ).reshape(row_length, model_width)
        d_keys, d_values = (
            lax.psum_scatter(
                key_part.astype(jnp.bfloat16), "seq", scatter_dimension=0, tiled=True
            ).astype(jnp.float32),
            lax.psum_scatter(
                value_part.astype(jnp.bfloat16), "seq", scatter_dimension=0, tiled=True
            ).astype(jnp.float32),
        )
        d_values_low = d_values.astype(jnp.bfloat16)
        d_joined = jnp.concatenate([d_query, d_keys.astype(jnp.bfloat16), d_values_low], axis=1)
        g_qkv_w = jnp.einsum("td,tf->df", normed_one, d_joined, preferred_element_type=jnp.float32)
        g_q_b = token_sum(d_query)
        g_v_b = token_sum(d_values_low)
        d_normed_one = jnp.einsum(
            "tf,df->td", d_joined, weights[2], preferred_element_type=jnp.float32
        )
        norm_value_one, norm_one_back = jax.vjp(norm_rows, inputs, weights[0], weights[1])
        d_inputs_norm, g_gain_one, g_bias_one = norm_one_back(d_normed_one)
        d_inputs = d_resid + d_inputs_norm
        new_grads = (
            g_gain_one,
            g_bias_one,
            g_qkv_w,
            g_q_b,
            g_v_b,
            g_out_w,
            g_out_b,
            g_gain_two,
            g_bias_two,
            g_in_w,
            g_in_b,
            g_back_w,
            g_back_b,
        )
        totals = tuple(
            (
                running + jnp.where(is_valid, grad_new, 0.0)
                for running, grad_new in zip(totals, new_grads)
            )
        )
        shown = jnp.where(
            section_rank == 0, d_inputs, d_inputs.astype(jnp.bfloat16).astype(jnp.float32)
        )
        in_grads = store_slot(in_grads, shown, slot_idx, is_valid)
        passed = from_behind(d_inputs.astype(jnp.bfloat16), "section", -1)
        return (passed, in_grads, totals)

    back_state = (
        jnp.zeros((local_len, model_width), jnp.bfloat16),
        jnp.zeros((micro_count, local_len, model_width), jnp.float32),
        tuple((jnp.zeros(weight.shape, jnp.float32) for weight in weights)),
    )
    ignored_grad, in_grads, totals = lax.fori_loop(0, tick_count, backward_tick, back_state)
    reduced = lax.psum_scatter(totals, ("dp", "seq"), scatter_dimension=0, tiled=True)
    return (
        outputs[None],
        in_grads[None],
        reduced[0][None],
        reduced[1][None],
        reduced[2][None],
        reduced[3][None],
        reduced[4][None],
        reduced[5][None],
        reduced[6][None],
        reduced[7][None],
        reduced[8][None],
        reduced[9][None],
        reduced[10][None],
        reduced[11][None],
        reduced[12][None],
    )


HEAD = 64
BIG = 1e30
NT = (((1,), (1,)), ((), ()))
F32 = jnp.float32
BF16 = jnp.bfloat16
BLK = 256
CH = 256
FINE = 128
PIECE = 512
UN = 8

def lane_mask(shape, h):
    lane = lax.broadcasted_iota(jnp.int32, shape, len(shape) - 1)
    return (lane < HEAD) if h == 0 else (lane >= HEAD)

def only(x, h):
    return jnp.where(lane_mask(x.shape, h), x, jnp.zeros_like(x))

def fwd_kernel(lo_ref, hi_ref, q_ref, k_ref, v_ref, fq_ref, fk_ref, o_ref, lse_ref):
    i = pl.program_id(0)
    n, w = k_ref.shape
    pairs = w // 128
    lo = lo_ref[i]
    count = hi_ref[i] - lo

    def run(lo, c):
        fq = fq_ref[...]
        at = pl.multiple_of(lo * FINE, FINE)
        pieces = []
        done = 0
        while done < c * FINE:
            size = min(PIECE, c * FINE - done)
            pieces.append(pl.ds(pl.multiple_of(at + done, FINE), size))
            done += size

        def scores(u, rows):
            p, h = divmod(u, 2)
            cols = slice(p * 128, (p + 1) * 128)
            q = q_ref[:, cols] * jnp.asarray(SCALE, BF16)
            qa = jnp.concatenate([only(q, h), fq], axis=1)
            kb = jnp.concatenate([k_ref[rows, cols], fk_ref[rows, :]], axis=1)
            return lax.dot_general(qa, kb, NT, preferred_element_type=F32)

        now = [scores(0, rows) for rows in pieces]
        outs, lses = [], []
        for u in range(2 * pairs):
            p, h = divmod(u, 2)
            cols = slice(p * 128, (p + 1) * 128)
            m = jnp.max(now[0], axis=1, keepdims=True)
            for s in now[1:]:
                m = jnp.maximum(m, jnp.max(s, axis=1, keepdims=True))
            r = None
            later = []
            for s, rows in zip(now, pieces):
                if u + 1 < 2 * pairs:
                    later.append(scores(u + 1, rows))
                pr = jnp.exp(s - m).astype(BF16)
                vb = jnp.concatenate([v_ref[rows, cols], jnp.ones((s.shape[1], 128), BF16)], axis=1)
                part = jnp.dot(pr, vb, preferred_element_type=F32)
                r = part if r is None else r + part
            now = later
            l = r[:, 128:]
            outs.append(r[:, :128] / l)
            lses.append(m + jnp.log(l))
            if h == 1:
                mask = lane_mask((BLK, 128), 0)
                o_ref[:, cols] = jnp.where(mask, outs[0], outs[1]).astype(BF16)
                both = jnp.where(mask, lses[0], lses[1]).T
                lse_ref[p, 0:1, :] = both[0:1, :]
                lse_ref[p, 1:2, :] = both[HEAD:HEAD + 1, :]
                outs, lses = [], []

    most = n // FINE
    below = 0
    for c in sorted({max(BLK // FINE, most * e // 16) for e in (2, 4, 8, 13, 14, 16)}):
        @pl.when((count > below) & (count <= c))
        def _(c=c):
            run(jnp.minimum(lo, most - c), c)
        below = c

def attn_fwd(lo, hi, q, k, v, fq, fk):
    n, w = q.shape
    pairs = w // 128
    blk = lambda i, lo, hi: (i, 0)
    full = lambda i, lo, hi: (0, 0)
    return pl.pallas_call(
        fwd_kernel,
        grid_spec=pltpu.PrefetchScalarGridSpec(
            num_scalar_prefetch=2,
            grid=(n // BLK,),
            in_specs=[pl.BlockSpec((BLK, w), blk), pl.BlockSpec((n, w), full), pl.BlockSpec((n, w), full),
                      pl.BlockSpec((BLK, 128), blk), pl.BlockSpec((n, 128), full)],
            out_specs=[pl.BlockSpec((BLK, w), blk), pl.BlockSpec((pairs, 8, BLK), lambda i, lo, hi: (0, 0, i))],
        ),
        out_shape=[jax.ShapeDtypeStruct((n, w), BF16), jax.ShapeDtypeStruct((pairs, 8, n), F32)],
        compiler_params=pltpu.CompilerParams(vmem_limit_bytes=62 * 2 ** 20),
        name="attn_fwd",
    )(lo, hi, q, k, v, fq, fk)

def bwd_kernel(lo_ref, hi_ref, q_ref, k_ref, v_ref, do_ref, o_ref, lse_ref, fq_ref, fk_ref,
               dq_ref, dk_ref, dv_ref, delta, dqt, dk_acc, dv_acc):
    j = pl.program_id(0)
    nb = pl.num_programs(0)
    n, w = q_ref.shape
    pairs = w // 128

    @pl.when(j == 0)
    def _():
        head = lax.broadcasted_iota(jnp.int32, (16, 128), 0)
        lane = lax.broadcasted_iota(jnp.int32, (16, 128), 1)
        sel = jnp.where(lane // HEAD == head, 1.0, 0.0).astype(BF16)

        def prep(b, c):
            rows = pl.ds(pl.multiple_of(b * CH, CH), CH)
            for p in range(pairs):
                cols = slice(p * 128, (p + 1) * 128)
                prod = do_ref[rows, cols].astype(F32) * o_ref[rows, cols].astype(F32)
                hi = prod.astype(BF16)
                lo = (prod - hi.astype(F32)).astype(BF16)
                d = lax.dot_general(sel, hi, NT, preferred_element_type=F32) + lax.dot_general(sel, lo, NT, preferred_element_type=F32)
                delta[p, :, rows] = d[0:8, :]
                dqt[p, :, rows] = jnp.zeros((128, CH), F32)
            return c
        lax.fori_loop(0, n // CH, prep, 0)

    lo = lo_ref[j]
    count = hi_ref[j] - lo
    dk_acc[...] = jnp.zeros_like(dk_acc)
    dv_acc[...] = jnp.zeros_like(dv_acc)

    def run(first, c):
        rows = pl.ds(pl.multiple_of(first * FINE, FINE), c * FINE)
        units = 2 * pairs

        def scores(u):
            p, h = divmod(u, 2)
            cols = slice(p * 128, (p + 1) * 128)
            kb = jnp.concatenate([only(k_ref[:, cols] * jnp.asarray(SCALE, BF16), h), fk_ref[...]], axis=1)
            qa = jnp.concatenate([q_ref[rows, cols], fq_ref[rows, :]], axis=1)
            s = lax.dot_general(kb, qa, NT, preferred_element_type=F32)
            dp = lax.dot_general(only(v_ref[:, cols], h), do_ref[rows, cols], NT, preferred_element_type=F32)
            return s, dp

        now = scores(0)
        dk, dv = [], []
        for u in range(units):
            p, h = divmod(u, 2)
            cols = slice(p * 128, (p + 1) * 128)
            later = scores(u + 1) if u + 1 < units else None
            s, dp = now
            pr = jnp.exp(s - lse_ref[p, h:h + 1, rows])
            ds = (pr * (dp - delta[p, h:h + 1, rows])).astype(BF16)
            dv.append(jnp.dot(pr.astype(BF16), do_ref[rows, cols], preferred_element_type=F32))
            dk.append(jnp.dot(ds, q_ref[rows, cols], preferred_element_type=F32))
            kt = (k_ref[:, cols] * jnp.asarray(SCALE, BF16)).T
            dqt[p, h * HEAD:(h + 1) * HEAD, rows] += jnp.dot(kt[h * HEAD:(h + 1) * HEAD, :], ds, preferred_element_type=F32)
            now = later
            if h == 1:
                mask = lane_mask((BLK, 128), 0)
                dk_acc[:, cols] += jnp.where(mask, dk[0], dk[1])
                dv_acc[:, cols] += jnp.where(mask, dv[0], dv[1])
                dk, dv = [], []

    @pl.loop(0, count // UN)
    def _(t):
        run(lo + t * UN, UN)

    left = count % UN
    for c in range(1, UN):
        @pl.when(left == c)
        def _(c=c):
            run(lo + (count - left), c)
    dk_ref[...] = (dk_acc[...] * SCALE).astype(BF16)
    dv_ref[...] = dv_acc[...].astype(BF16)

    @pl.when(j == nb - 1)
    def _():
        def fin(b, c):
            rows = pl.ds(pl.multiple_of(b * CH, CH), CH)
            for p in range(pairs):
                dq_ref[rows, p * 128:(p + 1) * 128] = dqt[p, :, rows].T.astype(BF16)
            return c
        lax.fori_loop(0, n // CH, fin, 0)

def attn_bwd(lo, hi, q, k, v, do, o, lse, fq, fk):
    n, w = q.shape
    pairs = w // 128
    full = lambda j, lo, hi: (0, 0)
    blk = lambda j, lo, hi: (j, 0)
    sh = jax.ShapeDtypeStruct((n, w), BF16)
    big = pl.BlockSpec((n, w), full, pipeline_mode=pl.Buffered(1))
    return pl.pallas_call(
        bwd_kernel,
        grid_spec=pltpu.PrefetchScalarGridSpec(
            num_scalar_prefetch=2,
            grid=(n // BLK,),
            in_specs=[big, pl.BlockSpec((BLK, w), blk), pl.BlockSpec((BLK, w), blk), big, big, pl.BlockSpec((pairs, 8, n), lambda j, lo, hi: (0, 0, 0)),
                      pl.BlockSpec((n, 128), full), pl.BlockSpec((BLK, 128), blk)],
            out_specs=[pl.BlockSpec((n, w), full), pl.BlockSpec((BLK, w), blk), pl.BlockSpec((BLK, w), blk)],
            scratch_shapes=[
                pltpu.VMEM((pairs, 8, n), F32),
                pltpu.VMEM((pairs, 128, n), F32),
                pltpu.VMEM((BLK, w), F32),
                pltpu.VMEM((BLK, w), F32),
            ],
        ),
        out_shape=[sh, sh, sh],
        compiler_params=pltpu.CompilerParams(vmem_limit_bytes=62 * 2 ** 20),
        name="attn_bwd",
    )(lo, hi, q, k, v, do, o, lse, fq, fk)

def segment_terms(lengths, n):
    cells = lengths.shape[0]
    place_of = jnp.arange(cells)
    ends = jnp.sum(jnp.where(place_of[:, None] <= place_of[None, :], lengths[:, None], 0), axis=0)
    starts = ends - lengths
    pos = jnp.arange(n, dtype=jnp.int32)[:, None]
    pad = lambda v: jnp.pad(v, (0, 128 - cells))[None, :]
    hot = (pos >= pad(starts)) & (pos < pad(ends))
    used = (jnp.arange(128) < cells)[None, :]
    fq = jnp.where(hot, -BIG, 0.0).astype(BF16)
    fk = jnp.where(used & ~hot, 1.0, 0.0).astype(BF16)
    first = jnp.arange(n // BLK, dtype=jnp.int32)[:, None] * BLK
    lo = jnp.max(jnp.where(starts[None, :] <= first, starts[None, :], 0), axis=1) // FINE
    hi = (jnp.min(jnp.where(ends[None, :] > first + BLK - 1, ends[None, :], n), axis=1) + FINE - 1) // FINE
    return fq, fk, lo.astype(jnp.int32), hi.astype(jnp.int32)


MIB = 2 ** 20
MESH = pl.DeviceIdType.MESH
ANY = pl.BlockSpec(memory_space=pl.ANY)
VMEM = pl.BlockSpec(memory_space=pltpu.VMEM)
DMA = pltpu.SemaphoreType.DMA
TOK = 256
COLS = 768


def sds(shape, dtype):
    return jax.ShapeDtypeStruct(shape, dtype)


def place():
    section, dp, seq = lax.axis_index("section"), lax.axis_index("dp"), lax.axis_index("seq")
    core = lax.rem(dp, 2)
    return section, dp, seq, core


def greet(*devices):
    barrier = pltpu.get_barrier_semaphore()
    for device in devices:
        pl.semaphore_signal(barrier, 1, device_id=device, device_id_type=MESH)
    pl.semaphore_wait(barrier, len(devices))


def column_mates(section, dp, seq, core):
    mates = [(section, dp, lax.rem(seq + t, 4)) for t in range(1, 4)]
    mates += [(section, dp + 1 - 2 * core, lax.rem(seq + t, 4)) for t in range(4)]
    return mates


def remote(src, dst, send_sem, recv_sem, device):
    return pltpu.make_async_remote_copy(
        src_ref=src, dst_ref=dst, send_sem=send_sem, recv_sem=recv_sem,
        device_id=device, device_id_type=MESH,
    )


def span(start, size):
    return pl.ds(pl.multiple_of(start, size), size)


def chunk(i):
    return span(i * TOK, TOK)


def row_norm(values):
    centre = jnp.mean(values, axis=-1, keepdims=True)
    offset = values - centre
    spread = jnp.mean(offset * offset, axis=-1, keepdims=True)
    rstd = lax.rsqrt(spread + EPS)
    return offset * rstd, rstd


def row_norm_back(grad, hat, rstd, gain):
    d_hat = grad * gain
    mean_d = jnp.mean(d_hat, axis=-1, keepdims=True)
    mean_dh = jnp.mean(d_hat * hat, axis=-1, keepdims=True)
    return rstd * (d_hat - mean_d - hat * mean_dh)


def fold(values):
    return jnp.sum(values.reshape(values.shape[0] // 8, 8, values.shape[1]), axis=0)


def up(ref):
    return ref[...].astype(F32)


def gelu_parts(x):
    size = jnp.abs(x)
    d = 1.0 + 0.2316418882 * size
    t = pl.reciprocal(d, approx=True)
    t = t * (2.0 - d * t)
    density = jnp.exp(-0.5 * (x * x)) * 0.3989422804014327
    poly = ((((1.330274429 * t - 1.821255978) * t + 1.781477937) * t - 0.356563782) * t + 0.319381530) * t
    tail = density * poly
    phi = jnp.where(x >= 0.0, 1.0 - tail, tail)
    return x * phi, phi + x * density


def ffn_loads(wo_in, win_in, wback_in, wo, win, wback, sem):
    pairs = [(wo_in, wo)]
    for f in range(win.shape[1] // COLS):
        cols = pl.ds(f * COLS, COLS)
        pairs += [(win_in.at[:, cols], win.at[:, cols]), (wback_in.at[cols], wback.at[cols])]
    return [pltpu.make_async_copy(a, b, sem.at[n]) for n, (a, b) in enumerate(pairs)]


class ToHeads:
    def __init__(self, buf, outs, tokens, width, sems, core, sibling):
        self.buf, self.outs, self.tokens, self.width = buf, outs, tokens, width
        self.own_sem, self.send_sem, self.recv_sem = sems
        self.core, self.sibling = core, sibling

    def _cols(self, part, core):
        return span(part * self.width + core * (self.width // 2), self.width // 2)

    def _sent(self, i, part, owner):
        rows = span(owner * self.tokens + i * TOK, TOK)
        return remote(self.buf.at[chunk(i), self._cols(part, 1 - self.core)], self.outs[part].at[rows],
                      self.send_sem.at[part, i], self.recv_sem.at[part, i], self.sibling)

    def _own(self, i, part):
        rows = span(self.core * self.tokens + i * TOK, TOK)
        return pltpu.make_async_copy(self.buf.at[chunk(i), self._cols(part, self.core)],
                                     self.outs[part].at[rows], self.own_sem.at[part, i])

    def start(self, i):
        for part in range(len(self.outs)):
            self._own(i, part).start()
            self._sent(i, part, self.core).start()

    def wait(self, i):
        for part in range(len(self.outs)):
            self._own(i, part).wait()
            self._sent(i, part, self.core).wait_send()
            self._sent(i, part, 1 - self.core).wait_recv()


class ToTokens:
    def __init__(self, ins, buf, tokens, width, sems, core, sibling):
        self.ins, self.buf, self.tokens, self.width = ins, buf, tokens, width
        self.own_sem, self.send_sem, self.recv_sem = sems
        self.core, self.sibling = core, sibling

    def _cols(self, part, core):
        return span(part * self.width + core * (self.width // 2), self.width // 2)

    def _sent(self, i, part, owner):
        rows = span((1 - self.core) * self.tokens + i * TOK, TOK)
        return remote(self.ins[part].at[rows], self.buf.at[chunk(i), self._cols(part, owner)],
                      self.send_sem.at[part, i], self.recv_sem.at[part, i], self.sibling)

    def _own(self, i, part):
        rows = span(self.core * self.tokens + i * TOK, TOK)
        return pltpu.make_async_copy(self.ins[part].at[rows], self.buf.at[chunk(i), self._cols(part, self.core)],
                                     self.own_sem.at[part, i])

    def start(self, i):
        for part in range(len(self.ins)):
            self._own(i, part).start()
            self._sent(i, part, self.core).start()

    def wait(self, i):
        for part in range(len(self.ins)):
            self._own(i, part).wait()
            self._sent(i, part, 1 - self.core).wait_recv()

    def wait_sent(self, i):
        for part in range(len(self.ins)):
            self._sent(i, part, self.core).wait_send()


def swap_sems(parts, steps):
    return [DMA((parts, steps))] * 3


class Blocks:
    def __init__(self, rows_ref, blocks_ref, gather, sems, section, dp, seq, core):
        self.rows, self.blocks, self.gather = rows_ref, blocks_ref, gather
        self.bounce, self.own_sem, self.send_sem, self.recv_sem = sems
        self.section, self.seq, self.core, self.column = section, seq, core, dp - core
        self.each, self.local, _ = blocks_ref.shape

    def _move(self, j):
        target_core, target_seq = self.seq // self.each, self.core * self.each + j
        slot = lax.rem(self.seq, self.each)
        here = (target_core == self.core) & (target_seq == self.seq)
        if self.gather:
            src, dst = self.blocks.at[j], self.rows.at[span(slot * self.local, self.local)]
        else:
            src, dst = self.rows.at[pl.ds(j * self.local, self.local)], self.blocks.at[slot]
        target = (self.section, self.column + target_core, target_seq)
        return here, src, dst, slot, target

    def start(self, *which):
        for j in which or range(self.each):
            here, src, dst, slot, target = self._move(j)

            @pl.when(here)
            def _():
                pltpu.make_async_copy(src, dst if self.bounce is None else self.bounce, self.own_sem).start()

            @pl.when(jnp.logical_not(here))
            def _():
                remote(src, dst, self.send_sem.at[j], self.recv_sem.at[slot], target).start()

    def wait(self):
        for j in range(self.each):
            here, src, dst, slot, target = self._move(j)

            @pl.when(here)
            def _():
                pltpu.make_async_copy(src, dst if self.bounce is None else self.bounce, self.own_sem).wait()
                if self.bounce is not None:
                    out = pltpu.make_async_copy(self.bounce, dst, self.own_sem)
                    out.start()
                    out.wait()

            @pl.when(jnp.logical_not(here))
            def _():
                remote(src, dst, self.send_sem.at[j], self.recv_sem.at[slot], target).wait_send()
        for j in range(self.each):
            here = (self.seq // self.each == self.core) & (self.core * self.each + j == self.seq)
            mate = (self.section, self.column + 1 - self.core, self.seq)
            if self.gather:
                dst = self.rows.at[pl.ds(j * self.local, self.local)]
                src = self.blocks.at[0]
            else:
                dst = self.blocks.at[j]
                src = self.rows.at[pl.ds(0, self.local)]

            @pl.when(jnp.logical_not(here))
            def _():
                remote(src, dst, self.send_sem.at[0], self.recv_sem.at[j], mate).wait_recv()


def block_scratch(each, local, width):
    return [pltpu.VMEM((local, width), BF16), DMA, DMA((each,)), DMA((each,))]


def project(x, gain, bias, w, qb, vb, buf, rows):
    width = x.shape[1]
    hat, _ = row_norm(x)
    a = (hat * up(gain) + up(bias)).astype(BF16)
    for part in range(3):
        cols = slice(part * width, (part + 1) * width)
        m = jnp.dot(a, w[:, cols], preferred_element_type=F32)
        if part == 0:
            m = m + up(qb)
        if part == 2:
            m = m + up(vb)
        buf[rows, cols] = m.astype(BF16)
    return a


def first_kernel(x_ref, w_in, gain, bias, qb, vb, x_out, q_ref, k_ref, v_ref,
                 xb, w, buf, w_sem, out_sem, own_sem, send_sem, recv_sem, *sems):
    section, dp, seq, core = place()
    sibling = (section, dp + 1 - 2 * core, seq)
    each, local, width = x_ref.shape
    part = local // 2
    column = dp - core
    load = pltpu.make_async_copy(w_in, w, w_sem)
    load.start()
    greet(*[(s, column + c, z) for s in range(2) for c in range(2) for z in range(2 * each)])

    def move(m):
        target_core, target_seq = seq // each, core * each + m
        slot = lax.rem(seq, each)
        here = (section == 0) & (target_core == core) & (target_seq == seq)
        src = x_ref.at[m, span(section * part, part)]
        dst = xb.at[span(slot * local + section * part, part)]
        return here, src, dst, slot, (0, column + target_core, target_seq)

    for m in range(each):
        here, src, dst, slot, target = move(m)

        @pl.when(here)
        def _():
            pltpu.make_async_copy(src, dst, own_sem).start()

        @pl.when(jnp.logical_not(here))
        def _():
            remote(src, dst, send_sem.at[m], recv_sem.at[section, slot], target).start()
    load.wait()

    @pl.when(section == 0)
    def _():
        swap = ToHeads(buf, (q_ref, k_ref, v_ref), each * local, width, sems, core, sibling)

        def out(i):
            return pltpu.make_async_copy(xb.at[chunk(i)], x_out.at[chunk(i)], out_sem.at[i])

        for h in range(2):
            for j in range(each):
                here = (seq // each == core) & (core * each + j == seq) & (h == 0)
                dst = xb.at[pl.ds(j * local + h * part, part)]

                @pl.when(here)
                def _():
                    pltpu.make_async_copy(x_ref.at[0, pl.ds(0, part)], dst, own_sem).wait()

                @pl.when(jnp.logical_not(here))
                def _():
                    remote(x_ref.at[0, pl.ds(0, part)], dst, send_sem.at[0], recv_sem.at[h, j], sibling).wait_recv()

                for i in range((j * local + h * part) // TOK, (j * local + (h + 1) * part) // TOK):
                    rows = slice(i * TOK, (i + 1) * TOK)
                    project(xb[rows, :].astype(F32), gain, bias, w, qb, vb, buf, rows)
                    out(i).start()
                    swap.start(i)
        for i in range(each * local // TOK):
            out(i).wait()
            swap.wait(i)

    for m in range(each):
        here, src, dst, slot, target = move(m)

        @pl.when(jnp.logical_not(here))
        def _():
            remote(src, dst, send_sem.at[m], recv_sem.at[section, slot], target).wait_send()


def first_call(x, w, gain, bias, qb, vb):
    each, local, width = x.shape
    tokens = each * local
    steps = tokens // TOK
    out = sds((2 * tokens, width // 2), BF16)
    return pl.pallas_call(
        first_kernel,
        in_specs=[ANY, ANY] + [VMEM] * 4,
        out_specs=[ANY] * 4,
        out_shape=[sds((tokens, width), BF16), out, out, out],
        scratch_shapes=[
            pltpu.VMEM((tokens, width), BF16), pltpu.VMEM(w.shape, BF16), pltpu.VMEM((tokens, 3 * width), BF16),
            DMA, DMA((steps,)), DMA, DMA((each,)), DMA((2, each))] + swap_sems(3, steps),
        compiler_params=pltpu.CompilerParams(collective_id=1, has_side_effects=True, vmem_limit_bytes=62 * MIB),
        name="rows_qkv",
    )(x, w, gain, bias, qb, vb)


def feed(i, out, att, x, wo, win, wback, bo, g2, b2, bi, bb, keep=None, ready=None):
    rows = chunk(i)
    hidden = win.shape[1]
    if ready:
        ready[0].wait()
    resid = x[rows, :].astype(F32) + up(bo) + jnp.dot(att[rows, :], wo[...], preferred_element_type=F32)
    hat, rstd = row_norm(resid)
    c = (hat * up(g2) + up(b2)).astype(BF16)
    if keep is not None:
        resid_b, slope_b, att_t, c_t, act_t = keep
        resid_b[rows, :] = resid
        att_t[:, rows] = att[rows, :].T
        c_t[:, rows] = c.T
    total = resid + up(bb)
    yield
    for f in range(hidden // COLS):
        cols = slice(f * COLS, (f + 1) * COLS)
        if ready:
            ready[1 + 2 * f].wait()
            ready[2 + 2 * f].wait()
        inner = jnp.dot(c, win[:, cols], preferred_element_type=F32) + bi[:, cols].astype(F32)
        yield
        active, slope = gelu_parts(inner)
        active = active.astype(BF16)
        if keep is not None:
            slope_b[rows, cols] = slope.astype(BF16)
            act_t[cols, rows] = active.T
        total = total + jnp.dot(active, wback[cols, :], preferred_element_type=F32)
        yield
    out[rows, :] = total.astype(BF16)


def feed_back(i, dy, slope_b, resid_b, wo, win, wback, g2, di_b, dr_b, dp_b, da_b, sums):
    rows = chunk(i)
    hidden = win.shape[1]
    g = dy.astype(F32)
    d_c = jnp.zeros(dy.shape, F32)
    yield
    for f in range(hidden // COLS):
        cols = slice(f * COLS, (f + 1) * COLS)
        d_active = lax.dot_general(dy, wback[cols, :], NT, preferred_element_type=F32)
        yield
        d_inner = d_active * slope_b[rows, cols].astype(F32)
        if sums:
            sums[3][:, cols] += fold(d_inner)
        d_inner = d_inner.astype(BF16)
        if di_b is not None:
            di_b[rows, cols] = d_inner
        d_c = d_c + lax.dot_general(d_inner, win[:, cols], NT, preferred_element_type=F32)
        yield
    hat, rstd = row_norm(resid_b[rows, :])
    d_resid = g + row_norm_back(d_c, hat, rstd, up(g2))
    d_proj = d_resid.astype(BF16)
    dr_b[rows, :] = d_resid
    if sums:
        s_gain, s_bias, s_out, _, s_back = sums
        s_gain[...] += fold(d_c * hat)
        s_bias[...] += fold(d_c)
        s_out[...] += fold(d_resid)
        s_back[...] += fold(g)
    if dp_b is not None:
        dp_b[rows, :] = d_proj
    da_b[rows, :] = lax.dot_general(d_proj, wo[...], NT, preferred_element_type=F32).astype(BF16)


def in_turns(*parts):
    parts = list(parts)
    while parts:
        for part in list(parts):
            if next(part, part) is part:
                parts.remove(part)


def pass_kernel(o_ref, x_ref, g_ref, wo_in, win_in, wback_in, wqkv_in, bo, g2, b2, bi, bb, g1, b1, qb, vb,
                x_out, g_out, n_out, q_ref, k_ref, v_ref,
                wo, win, wback, wqkv, att, yb, xn, buf, w_sem, x_send, x_recv, x_sem, *sems):
    section, dp, seq, core = place()
    sibling = (section, dp + 1 - 2 * core, seq)
    across = (1 - section, dp, seq)
    tokens, width = x_ref.shape
    steps = tokens // TOK
    loads = ffn_loads(wo_in, win_in, wback_in, wo, win, wback, w_sem)
    load_qkv = pltpu.make_async_copy(wqkv_in, wqkv, w_sem.at[len(loads)])
    loads[0].start()
    greet(across, *column_mates(section, dp, seq, core))
    to_tokens = ToTokens((o_ref,), att, tokens, width, sems[:3], core, sibling)
    to_heads = ToHeads(buf, (q_ref, k_ref, v_ref), tokens, width, sems[3:6], core, sibling)
    blocks = Blocks(g_out, g_ref, True, sems[6:10], section, dp, seq, core)
    to_tokens.start(0)
    for load in loads[1:]:
        load.start()

    @pl.loop(1, steps)
    def _(i):
        to_tokens.start(i)

    load_qkv.start()

    @pl.when(section == 1)
    def _():
        blocks.start()

    def passed(i):
        return remote(yb.at[chunk(i)], xn.at[chunk(i)], x_send.at[i], x_recv.at[i], across)

    def kept(i):
        return pltpu.make_async_copy(xn.at[chunk(i)], x_out.at[chunk(i)], x_sem.at[i])

    def send_chunk(i, ready=None):
        in_turns(feed(i, yb, att, x_ref, wo, win, wback, bo, g2, b2, bi, bb, ready=ready))
        passed(i).start()
        xn[chunk(i), :] = x_ref[chunk(i), :]

    to_tokens.wait(0)

    @pl.when(section == 0)
    def _():
        send_chunk(0, loads)

    @pl.when(section == 1)
    def _():
        for load in loads:
            load.wait()

    @pl.loop(1, steps)
    def _(i):
        to_tokens.wait(i)

        @pl.when(section == 0)
        def _():
            send_chunk(i)

    load_qkv.wait()

    @pl.loop(0, steps)
    def _(i):
        @pl.when(section == 1)
        def _():
            passed(i).wait_recv()

        kept(i).start()
        a = project(xn[chunk(i), :].astype(F32), g1, b1, wqkv, qb, vb, buf, chunk(i))
        n_out[:, chunk(i)] = a.T
        to_heads.start(i)

    @pl.loop(0, steps)
    def _(i):
        to_tokens.wait_sent(i)
        to_heads.wait(i)
        kept(i).wait()

        @pl.when(section == 0)
        def _():
            passed(i).wait_send()

    @pl.when(section == 1)
    def _():
        blocks.wait()


def pass_call(o, x, g, wo, win, wback, wqkv, vectors):
    tokens, width = x.shape
    steps = tokens // TOK
    each = g.shape[0]
    out = sds((2 * tokens, width // 2), BF16)
    low = sds(x.shape, BF16)
    low_buf = pltpu.VMEM(x.shape, BF16)
    return pl.pallas_call(
        pass_kernel,
        in_specs=[ANY, VMEM, ANY, ANY, ANY, ANY, ANY] + [VMEM] * len(vectors),
        out_specs=[ANY, ANY, VMEM, ANY, ANY, ANY],
        out_shape=[low, low, sds((width, tokens), BF16), out, out, out],
        scratch_shapes=[pltpu.VMEM(w.shape, BF16) for w in (wo, win, wback, wqkv)]
        + [low_buf, low_buf, low_buf, pltpu.VMEM((tokens, 3 * width), BF16),
           DMA((2 + 2 * (win.shape[1] // COLS),)), DMA((steps,)), DMA((steps,)), DMA((steps,))]
        + swap_sems(1, steps) + swap_sems(3, steps) + block_scratch(each, tokens // each, width),
        compiler_params=pltpu.CompilerParams(collective_id=2, has_side_effects=True, vmem_limit_bytes=62 * MIB),
        name="ffn_pass_qkv",
    )(o, x, g, wo, win, wback, wqkv, *vectors)


def turn_kernel(o_ref, x_ref, g_ref, wo_in, win_in, wback_in, bo, g2, b2, bi, bb,
                y_out, resid_out, slope_out, att_out, c_out, act_out, dr_out, da_ref,
                wo, win, wback, att, yb, resid_b, slope_b, att_t, c_t, act_t, dr_b, da_b,
                w_sem, out_sem, *sems):
    section, dp, seq, core = place()
    sibling = (section, dp + 1 - 2 * core, seq)
    tokens, width = x_ref.shape
    steps = tokens // TOK
    loads = ffn_loads(wo_in, win_in, wback_in, wo, win, wback, w_sem)
    loads[0].start()
    greet(sibling)
    to_tokens = ToTokens((o_ref,), att, tokens, width, sems[:3], core, sibling)
    to_heads = ToHeads(da_b, (da_ref,), tokens, width, sems[3:6], core, sibling)
    to_tokens.start(0)
    for load in loads[1:]:
        load.start()

    @pl.loop(1, steps)
    def _(i):
        to_tokens.start(i)

    def copies(i, which, at, turned=False):
        where = (slice(None), chunk(i)) if turned else (chunk(i),)
        return [pltpu.make_async_copy(b.at[where], o.at[where], out_sem.at[at + n, i]) for n, (b, o) in enumerate(which)]

    def results(i):
        return copies(i, ((yb, y_out), (resid_b, resid_out), (slope_b, slope_out)), 0) + copies(
            i, ((att_t, att_out), (c_t, c_out), (act_t, act_out)), 3, True)

    def back_results(i):
        return copies(i, ((dr_b, dr_out),), 6)

    def forward(i, ready=None):
        return feed(i, yb, att, x_ref, wo, win, wback, bo, g2, b2, bi, bb, (resid_b, slope_b, att_t, c_t, act_t), ready)

    def backward(i):
        return feed_back(i, g_ref[chunk(i), :], slope_b, resid_b, wo, win, wback, g2, None, dr_b, None, da_b, None)

    to_tokens.wait(0)
    in_turns(forward(0, loads))
    for copy in results(0):
        copy.start()

    @pl.loop(1, steps)
    def _(i):
        to_tokens.wait(i)
        in_turns(forward(i))
        in_turns(backward(i - 1))
        to_heads.start(i - 1)
        for copy in results(i) + back_results(i - 1):
            copy.start()

    in_turns(backward(steps - 1))
    to_heads.start(steps - 1)
    for copy in back_results(steps - 1):
        copy.start()

    @pl.loop(0, steps)
    def _(i):
        to_tokens.wait_sent(i)
        to_heads.wait(i)
        for copy in results(i) + back_results(i):
            copy.wait()


def turn_call(o, x, g, wo, win, wback, vectors):
    tokens, width = x.shape
    hidden = win.shape[1]
    steps = tokens // TOK
    low, full = sds(x.shape, BF16), sds(x.shape, F32)
    turned = sds((width, tokens), BF16)
    outs = [low, full, sds((tokens, hidden), BF16), turned, turned, sds((hidden, tokens), BF16), full]
    buf = lambda s: pltpu.VMEM(s.shape, s.dtype)
    return pl.pallas_call(
        turn_kernel,
        in_specs=[ANY, VMEM, VMEM, ANY, ANY, ANY] + [VMEM] * len(vectors),
        out_specs=[ANY] * 8,
        out_shape=outs + [sds((2 * tokens, width // 2), BF16)],
        scratch_shapes=[buf(wo), buf(win), buf(wback), buf(low)] + [buf(s) for s in outs] + [buf(low)]
        + [DMA((1 + 2 * (hidden // COLS),)), DMA((7, steps))] + swap_sems(1, steps) + swap_sems(1, steps),
        compiler_params=pltpu.CompilerParams(collective_id=3, has_side_effects=True, vmem_limit_bytes=62 * MIB),
        name="ffn_turn",
    )(o, x, g, wo, win, wback, *vectors)


def input_back(i, dj, dr, x, w, gain, sums):
    rows = chunk(i)
    width = x.shape[1]
    d_a = lax.dot_general(dj[rows, :], w[...], NT, preferred_element_type=F32)
    hat, rstd = row_norm(x[rows, :].astype(F32))
    if sums:
        s_gain, s_bias, s_q, s_v = sums
        s_q[...] += fold(dj[rows, :width].astype(F32))
        s_v[...] += fold(dj[rows, 2 * width:].astype(F32))
        s_gain[...] += fold(d_a * hat)
        s_bias[...] += fold(d_a)
    return (dr[rows, :] + row_norm_back(d_a, hat, rstd, up(gain))).astype(BF16)


def back_kernel(dq_ref, dk_ref, dv_ref, dr_ref, x_ref, y_ref, g_in, slope_in, resid_in, c_in, act_in,
                wqkv_in, wo_in, win_in, wback_in, g1, g2,
                y_out, dr_out, dp_out, da_ref, *rest):
    rest = list(rest)
    shares = [rest.pop(0) for _ in range(4)]
    y_shares = [rest.pop(0) for _ in range(2)]
    s_gain, s_bias, s_out, s_in, s_back = [rest.pop(0) for _ in range(5)]
    wqkv, wo, win, wback, dj, dx, gb, di, dr, dp, da_b, c_t, act_t, grad_in, grad_back = [rest.pop(0) for _ in range(15)]
    (w_sem, in_sem, a_sem, t_sem, out_sem, g_sem, x_send, x_recv, ready, r_send, r_recv, r_out) = rest[:12]
    sems = rest[12:]
    section, dp_index, seq, core = place()
    sibling = (section, dp_index + 1 - 2 * core, seq)
    across = (1 - section, dp_index, seq)
    tokens, width = gb.shape
    hidden = win.shape[1]
    steps = tokens // TOK
    blocks_of = hidden // COLS
    x_b, dr_in = da_b, grad_back
    loads = [pltpu.make_async_copy(a, b, w_sem.at[n]) for n, (a, b) in enumerate(
        ((wqkv_in, wqkv), (wback_in, wback), (win_in, win), (wo_in, wo), (c_in, c_t)))]

    def kept(i):
        return [pltpu.make_async_copy(a.at[chunk(i)], b.at[chunk(i)], in_sem.at[n, i])
                for n, (a, b) in enumerate(((slope_in, di), (resid_in, dr)))]

    def turned(i):
        return pltpu.make_async_copy(act_in.at[:, chunk(i)], act_t.at[lax.rem(i, 2)], t_sem.at[i])

    def given(i):
        return [pltpu.make_async_copy(a.at[chunk(i)], b.at[chunk(i)], a_sem.at[n, i])
                for n, (a, b) in enumerate(((x_ref, x_b), (dr_ref, dr_in)))]

    def last(i):
        return pltpu.make_async_copy(g_in.at[chunk(i)], gb.at[chunk(i)], g_sem.at[i])

    def passed(i):
        return remote(dx.at[chunk(i)], gb.at[chunk(i)], x_send.at[i], x_recv.at[i], across)

    def results(i):
        return [pltpu.make_async_copy(b.at[chunk(i)], o.at[chunk(i)], out_sem.at[n, i])
                for n, (b, o) in enumerate(((dr, dr_out), (dp, dp_out)))]

    @pl.when(section == 1)
    def _():
        loads[0].start()

    greet(across, *column_mates(section, dp_index, seq, core))
    to_tokens = ToTokens((dq_ref, dk_ref, dv_ref), dj, tokens, width, sems[:3], core, sibling)
    to_heads = ToHeads(da_b, (da_ref,), tokens, width, sems[3:6], core, sibling)
    blocks = Blocks(y_ref, y_out, False, sems[6:10], section, dp_index, seq, core)

    @pl.when(section == 1)
    def _():
        @pl.loop(0, steps)
        def _(i):
            to_tokens.start(i)
            for copy in given(i):
                copy.start()

        loads[0].wait()

        @pl.loop(0, steps)
        def _(i):
            to_tokens.wait(i)
            for copy in given(i):
                copy.wait()
            last(i).start()
            dx[chunk(i), :] = input_back(i, dj, dr_in, x_b, wqkv, g1, None)
            passed(i).start()

    for load in loads[1:]:
        load.start()

    @pl.loop(0, steps)
    def _(i):
        for copy in kept(i):
            copy.start()

    for i in range(2):
        turned(i).start()
    blocks.start()
    sums = (s_gain, s_bias, s_out, s_in, s_back)
    for s in sums + (grad_in, grad_back):
        s[...] = jnp.zeros_like(s)
    for load in loads[1:]:
        load.wait()

    def grad_block(i, n):
        part = span(n % blocks_of * COLS, COLS) if not isinstance(n, int) else pl.ds(n % blocks_of * COLS, COLS)
        if n < blocks_of:
            grad_in[:, part] += jnp.dot(c_t[:, chunk(i)], di[chunk(i), part], preferred_element_type=F32)
        else:
            grad_back[part, :] += jnp.dot(act_t[lax.rem(i, 2), part, :], gb[chunk(i), :], preferred_element_type=F32)

    def feed_step(i):
        for copy in kept(i):
            copy.wait()

        @pl.when(section == 0)
        def _():
            passed(i).wait_recv()

        @pl.when(section == 1)
        def _():
            last(i).wait()

        in_turns(feed_back(i, gb[chunk(i), :], di, dr, wo, win, wback, g2, di, dr, dp, da_b, sums))
        to_heads.start(i)
        for copy in results(i):
            copy.start()

    @pl.loop(0, steps - 1)
    def _(i):
        feed_step(i)
        turned(i).wait()
        for n in range(2 * blocks_of):
            grad_block(i, n)

        @pl.when(i + 2 < steps)
        def _():
            turned(i + 2).start()

    end = steps - 1
    feed_step(end)
    pl.semaphore_signal(ready, 1, device_id=sibling, device_id_type=MESH)
    turned(end).wait()
    pl.semaphore_wait(ready, 1)

    size_in, size_back = width // 16, hidden // 16

    def sent_in(n, yy):
        cols = pl.ds(n * COLS, COLS)
        return remote(win.at[pl.ds(yy * 4 * size_in, 4 * size_in), cols],
                      win.at[pl.ds((2 + yy) * 4 * size_in, 4 * size_in), cols],
                      r_send.at[2 * n + yy], r_recv.at[2 * n + yy], sibling)

    def sent_back(n):
        yy = n // 2
        return remote(wback.at[pl.ds(yy * COLS, COLS)], wback.at[pl.ds((2 + yy) * COLS, COLS)],
                      r_send.at[2 * blocks_of + yy], r_recv.at[2 * blocks_of + yy], sibling)

    def write_in(t, yy):
        rows = span((2 + yy) * 4 * size_in + lax.rem(seq + t, 4) * size_in, size_in)
        return pltpu.make_async_copy(win.at[rows], shares[t].at[pl.ds(yy * size_in, size_in)], r_out.at[t, yy])

    def write_back(t):
        yy = (dp_index // 2 + t) % 2
        return pltpu.make_async_copy(wback.at[span((2 + yy) * COLS, COLS)], y_shares[t], r_out.at[4, t])

    for n in range(blocks_of):
        grad_block(end, n)
        cols = slice(n * COLS, (n + 1) * COLS)
        for yy in range(2):
            win[yy * 4 * size_in:(yy + 1) * 4 * size_in, cols] = grad_in[core_rows(size_in, yy, 1 - core), cols].astype(BF16)
            sent_in(n, yy).start()
    for n in range(blocks_of):
        grad_block(end, blocks_of + n)
        if n % 2 == 1:
            yy = n // 2
            wback[yy * COLS:(yy + 1) * COLS, :] = grad_back[core_rows(size_back, yy, 1 - core), :].astype(BF16)
            sent_back(n).start()
    for n in range(blocks_of):
        cols = slice(n * COLS, (n + 1) * COLS)
        for yy in range(2):
            sent_in(n, yy).wait_recv()
            rows = slice((2 + yy) * 4 * size_in, (3 + yy) * 4 * size_in)
            win[rows, cols] = (grad_in[core_rows(size_in, yy, core), cols] + win[rows, cols].astype(F32)).astype(BF16)
    for yy in range(2):
        for t in range(4):
            write_in(t, yy).start()
    for yy in range(2):
        sent_back(2 * yy).wait_recv()
        rows = slice((2 + yy) * COLS, (3 + yy) * COLS)
        wback[rows, :] = (grad_back[core_rows(size_back, yy, core), :] + wback[rows, :].astype(F32)).astype(BF16)
    for t in range(2):
        write_back(t).start()

    @pl.loop(0, steps)
    def _(i):
        to_heads.wait(i)
        for copy in results(i):
            copy.wait()

        @pl.when(section == 1)
        def _():
            to_tokens.wait_sent(i)
            passed(i).wait_send()

    for yy in range(2):
        for n in range(blocks_of):
            sent_in(n, yy).wait_send()
        sent_back(2 * yy).wait_send()
        write_back(yy).wait()
        for t in range(4):
            write_in(t, yy).wait()
    blocks.wait()


def back_call(dq, dk, dv, dr, x, y, g, slope, resid, c_t, act_t, wqkv, wo, win, wback, g1, g2, each):
    tokens, width = x.shape
    hidden = win.shape[1]
    steps = tokens // TOK
    blocks_of = hidden // COLS
    low, full, wide = sds(x.shape, BF16), sds(x.shape, F32), sds((tokens, hidden), BF16)
    one = sds((8, width), F32)
    buf = lambda s: pltpu.VMEM(s.shape, s.dtype)
    shares = [sds((width // 8, hidden), BF16)] * 4 + [sds((hidden // 4, width), BF16)] * 2
    return pl.pallas_call(
        back_kernel,
        in_specs=[ANY] * 15 + [VMEM, VMEM],
        out_specs=[ANY] * 10 + [VMEM] * 5,
        out_shape=[sds((each, tokens // each, width), BF16), full, low, sds((2 * tokens, width // 2), BF16)]
        + shares + [one, one, one, sds((8, hidden), F32), one],
        scratch_shapes=[buf(wqkv), buf(wo), buf(win), buf(wback), pltpu.VMEM((tokens, 3 * width), BF16),
                        buf(low), buf(low), buf(wide), buf(full), buf(low), buf(low), buf(c_t),
                        pltpu.VMEM((2, hidden, TOK), BF16), pltpu.VMEM((width, hidden), F32), pltpu.VMEM((hidden, width), F32),
                        DMA((5,)), DMA((2, steps)), DMA((2, steps)), DMA((steps,)), DMA((2, steps)), DMA((steps,)),
                        DMA((steps,)), DMA((steps,)), pltpu.SemaphoreType.REGULAR,
                        DMA((2 * blocks_of + 2,)), DMA((2 * blocks_of + 2,)), DMA((5, 2))]
        + swap_sems(3, steps) + swap_sems(1, steps) + block_scratch(each, tokens // each, width),
        compiler_params=pltpu.CompilerParams(collective_id=4, has_side_effects=True, vmem_limit_bytes=62 * MIB),
        name="qkv_back_pass",
    )(dq, dk, dv, dr, x, y, g, slope, resid, c_t, act_t, wqkv, wo, win, wback, g1, g2)


def core_rows(size, yy, core):
    return span((2 * yy + core) * 4 * size, 4 * size)


def attn_plan(width):
    return [(width, width, 0, 0)] + [(width, width, 1, i * width) for i in range(3)]


def piece(left, right, at, cols, out):
    step = min(left.shape[0], 1024)

    @pl.loop(0, left.shape[0] // step)
    def _(r):
        block = span(r * step, step)
        out[block, :] = jnp.dot(left[block, :], right[:, at:at + cols], preferred_element_type=F32).astype(BF16)


def grads_kernel(n_small, *refs):
    refs = list(refs)
    d_parts = [refs.pop(0) for _ in range(3)]
    dr_ref, x_ref, w_in, g1 = [refs.pop(0) for _ in range(4)]
    lefts = [refs.pop(0) for _ in range(2)]
    rights = [refs.pop(0)]
    ffn_in = [refs.pop(0) for _ in range(4)]
    back_in = [refs.pop(0) for _ in range(2)]
    sums = [refs.pop(0) for _ in range(n_small)]
    outs = [refs.pop(0) for _ in range(2)]
    ffn_out, back_out = refs.pop(0), refs.pop(0)
    small_out, dx_out = refs.pop(0), refs.pop(0)
    left_buf = [refs.pop(0) for _ in range(2)]
    right_buf = [refs.pop(0) for _ in range(2)]
    w, dr, x, dxb = [refs.pop(0) for _ in range(4)]
    own_sums = [refs.pop(0) for _ in range(4)]
    dj = right_buf[1]
    ffn_buf, ffn_rec, back_buf, back_rec = [refs.pop(0) for _ in range(4)]
    width, tokens = lefts[0].shape
    plan = attn_plan(width)
    buf1 = [refs.pop(0) for _ in plan]
    rec1 = [refs.pop(0) for _ in plan]
    rec2 = [refs.pop(0) for _ in plan]
    rec3 = [refs.pop(0) for _ in plan]
    small, small1, small2, small3 = [refs.pop(0) for _ in range(4)]
    (load_sem, s1_send, s1_recv, s2_send, s2_recv, s3_send, s3_recv,
     m_send, m_recv, f_send, f_recv, f_load, b_load, b_send, b_recv, in_sem) = refs[:16]

    section, dp, seq, core = place()
    y = dp // 2
    sibling = (section, dp + 1 - 2 * core, seq)
    across_y = (section, dp + 2 - 4 * y, seq)
    along = [(section, dp, lax.rem(seq + t, 4)) for t in range(1, 4)]
    count = len(plan)
    steps = tokens // TOK
    load_w = pltpu.make_async_copy(w_in, w, load_sem.at[1, 1])
    loads = [[pltpu.make_async_copy(lefts[0], left_buf[0], load_sem.at[0, 0]),
              pltpu.make_async_copy(rights[0], right_buf[0], load_sem.at[1, 0])],
             [pltpu.make_async_copy(lefts[1], left_buf[1], load_sem.at[0, 1])]]

    def given(i):
        return [pltpu.make_async_copy(a.at[chunk(i)], b.at[chunk(i)], in_sem.at[n, i])
                for n, (a, b) in enumerate(((x_ref, x), (dr_ref, dr)))]

    greet(across_y, *column_mates(section, dp, seq, core))
    to_tokens = ToTokens(d_parts, dj, tokens, width, refs[16:19], core, sibling)
    blocks = Blocks(dxb, dx_out, False, [None] + refs[19:22], section, dp, seq, core)
    ffn_loads = [pltpu.make_async_copy(ffn_in[t], ffn_buf.at[t], f_load.at[t]) for t in range(4)]
    back_loads = [pltpu.make_async_copy(back_in[t], back_buf.at[t], b_load.at[t]) for t in range(2)]
    for load in back_loads:
        load.start()

    @pl.loop(0, steps)
    def _(i):
        to_tokens.start(i)
        for copy in given(i):
            copy.start()

    load_w.start()
    for pair in loads:
        for load in pair:
            load.start()
    for load in ffn_loads:
        load.start()

    def ffn_half(yy):
        rows = ffn_rec.shape[0]
        return span(yy * rows, rows)

    def ffn_sent():
        return remote(ffn_buf.at[0, ffn_half(1 - y)], ffn_rec, f_send, f_recv, across_y)

    def ffn_sum(yy):
        rows = ffn_half(yy)
        total = ffn_buf[0, rows, :].astype(F32)
        for t in range(1, 4):
            total = total + ffn_buf[t, rows, :].astype(F32)
        return total

    next_z = seq + 1 - 2 * lax.rem(seq, 2)
    far_z = lax.rem(seq + 2, 4)

    def back_rows(zz):
        rows = back_rec.shape[1]
        return span(zz * rows, rows)

    def back_near(t):
        return remote(back_buf.at[0, back_rows(lax.rem(next_z + 2 * t, 4))], back_rec.at[t],
                      b_send.at[t], b_recv.at[t], (section, dp, next_z))

    def back_far():
        return remote(back_buf.at[0, back_rows(far_z)], back_rec.at[2], b_send.at[2], b_recv.at[2], (section, dp, far_z))

    def back_add(rows, other):
        back_buf[0, rows, :] = (back_buf[0, rows, :].astype(F32) + other.astype(F32)).astype(BF16)

    size = width // 16

    def half(yy):
        return span(yy * 4 * size, 4 * size)

    def first(p, yy):
        return remote(buf1[p].at[core_rows(size, yy, 1 - core)], rec1[p].at[half(yy)],
                      s1_send.at[p, yy], s1_recv.at[p, yy], sibling)

    def second(p):
        return remote(rec1[p].at[half(1 - y)], rec2[p], s2_send.at[p], s2_recv.at[p], across_y)

    def shard(zz):
        return span(y * 4 * size + zz * size, size)

    def third(p, t):
        target = (section, dp, next_z)
        return remote(rec1[p].at[shard(lax.rem(next_z + 2 * t, 4))], rec3[p].at[t],
                      s3_send.at[p, t], s3_recv.at[p, t], target)

    def fourth(p):
        return remote(rec1[p].at[shard(far_z)], rec3[p].at[2], s3_send.at[p, 2], s3_recv.at[p, 2], (section, dp, far_z))

    def reduce_core(p):
        for yy in range(2):
            first(p, yy).wait_recv()
            total = buf1[p][core_rows(size, yy, core), :].astype(F32) + rec1[p][half(yy), :].astype(F32)
            rec1[p][half(yy), :] = total.astype(BF16)
        second(p).start()

    def reduce_y(p):
        second(p).wait_recv()
        mine = half(y)
        rec1[p][mine, :] = (rec1[p][mine, :].astype(F32) + rec2[p][...].astype(F32)).astype(BF16)
        for t in range(2):
            third(p, t).start()

    def reduce_next(p):
        for t, zz in enumerate((seq, far_z)):
            third(p, t).wait_recv()
            rec1[p][shard(zz), :] = (rec1[p][shard(zz), :].astype(F32) + rec3[p][t].astype(F32)).astype(BF16)
        fourth(p).start()

    def reduce_far(p):
        rows, cols, t_out, at = plan[p]
        fourth(p).wait_recv()
        outs[t_out][:, at:at + cols] = rec1[p][shard(seq), :].astype(F32) + rec3[p][2].astype(F32)

    for load in back_loads:
        load.wait()
    back_buf[0] = (back_buf[0].astype(F32) + back_buf[1].astype(F32)).astype(BF16)
    for t in range(2):
        back_near(t).start()

    for s in own_sums:
        s[...] = jnp.zeros_like(s)
    load_w.wait()
    per = steps // dx_out.shape[0]
    for j in range(dx_out.shape[0]):
        @pl.loop(j * per, (j + 1) * per)
        def _(i):
            to_tokens.wait(i)
            for copy in given(i):
                copy.wait()
            dxb[chunk(i), :] = input_back(i, dj, dr, x, w, g1, own_sums)

        blocks.start(j)

    line = 0
    for s in own_sums + sums:
        row = jnp.sum(s[...], axis=0, keepdims=True)
        for t in range(s.shape[1] // 128):
            small[line:line + 1, :] = row[:, t * 128:(t + 1) * 128]
            line += 1
    v1 = remote(small, small1, m_send.at[0], m_recv.at[0], sibling)
    v2 = remote(small, small2, m_send.at[1], m_recv.at[1], across_y)

    def v3(t):
        return remote(small, small3.at[t - 1], m_send.at[1 + t], m_recv.at[1 + t], along[t - 1])

    v1.start()
    v1.wait()
    small[...] += small1[...]
    v2.start()
    ready = set()
    for p, (rows, cols, t, at) in enumerate(plan):
        if t not in ready:
            ready.add(t)
            for load in loads[t]:
                load.wait()
        piece(left_buf[t], right_buf[t], at, cols, buf1[p])
        for yy in range(2):
            first(p, yy).start()
        if p > 0:
            reduce_core(p - 1)
        if p == 1:
            v2.wait()
            small[...] += small2[...]
            for t in range(1, 4):
                v3(t).start()
    reduce_core(count - 1)
    for t, zz in enumerate((seq, far_z)):
        back_near(t).wait_recv()
        back_add(back_rows(zz), back_rec[t])
    back_far().start()
    for load in ffn_loads:
        load.wait()
    ffn_buf[0, ffn_half(1 - y), :] = ffn_sum(1 - y).astype(BF16)
    ffn_sent().start()
    for p in range(count):
        reduce_y(p)
        if p > 0:
            reduce_next(p - 1)
    reduce_next(count - 1)
    own = ffn_sum(y)
    ffn_sent().wait_recv()
    ffn_out[...] = own + ffn_rec[...].astype(F32)
    back_far().wait_recv()
    back_out[...] = back_buf[0, back_rows(seq), :].astype(F32) + back_rec[2].astype(F32)
    for t in range(1, 4):
        v3(t).wait()
    small_out[...] = small[...] + small3[0] + small3[1] + small3[2]
    for p in range(count):
        reduce_far(p)

    for p in range(count):
        for yy in range(2):
            first(p, yy).wait_send()
        second(p).wait_send()
        for t in range(2):
            third(p, t).wait_send()
        fourth(p).wait_send()
    @pl.loop(0, steps)
    def _(i):
        to_tokens.wait_sent(i)

    ffn_sent().wait_send()
    for t in range(2):
        back_near(t).wait_send()
    back_far().wait_send()
    blocks.wait()


def grads_call(d_parts, dr, x, w, g1, att_t, norm_t, d_proj, ffn, back, sums, each):
    width, tokens = att_t.shape
    plan = attn_plan(width)
    count = len(plan)
    steps = tokens // TOK
    one = sds((8, width), F32)
    lines = (4 * width + sum(s.shape[1] for s in sums)) // 128
    vec = pltpu.VMEM((lines, 128), F32)
    buf = lambda s: pltpu.VMEM(s.shape, s.dtype)
    half = (ffn[0].shape[0] // 2, ffn[0].shape[1])
    quarter = (back[0].shape[0] // 4, back[0].shape[1])
    return pl.pallas_call(
        partial(grads_kernel, len(sums)),
        in_specs=[ANY] * 6 + [VMEM] + [ANY] * 9 + [VMEM] * len(sums),
        out_specs=[VMEM] * 5 + [ANY],
        out_shape=[sds((width // 16, width), F32), sds((width // 16, 3 * width), F32)]
        + [sds(half, F32), sds(quarter, F32)]
        + [sds((lines, 128), F32), sds((each, tokens // each, width), BF16)],
        scratch_shapes=(
            [buf(att_t), buf(norm_t), buf(d_proj), pltpu.VMEM((tokens, 3 * width), BF16), buf(w), buf(dr), buf(x), buf(x)]
            + [buf(one)] * 4
            + [pltpu.VMEM((4,) + ffn[0].shape, BF16), pltpu.VMEM(half, BF16),
               pltpu.VMEM((2,) + back[0].shape, BF16), pltpu.VMEM((3,) + quarter, BF16)]
            + [pltpu.VMEM((r, c), BF16) for r, c, *_ in plan]
            + [pltpu.VMEM((r // 2, c), BF16) for r, c, *_ in plan]
            + [pltpu.VMEM((r // 4, c), BF16) for r, c, *_ in plan]
            + [pltpu.VMEM((3, r // 16, c), BF16) for r, c, *_ in plan]
            + [vec, vec, vec, pltpu.VMEM((3, lines, 128), F32)]
            + [DMA((2, 2)), DMA((count, 2)), DMA((count, 2)), DMA((count,)), DMA((count,)),
               DMA((count, 3)), DMA((count, 3)), DMA((5,)), DMA((5,)), DMA, DMA, DMA((4,)), DMA((2,)), DMA((3,)), DMA((3,)),
               DMA((2, steps))]
            + swap_sems(3, steps) + [DMA, DMA((each,)), DMA((each,))]),
        compiler_params=pltpu.CompilerParams(collective_id=8, has_side_effects=True, vmem_limit_bytes=62 * MIB),
        name="weight_grads",
    )(*d_parts, dr, x, w, g1, att_t, norm_t, d_proj, *ffn, *back, *sums)


def finish_kernel(dx_ref, y_ref, *refs):
    count = (len(refs) - 2) // 2
    ins, (dx_out, y_out), outs = refs[:count], refs[count:count + 2], refs[count + 2:]
    dx_out[...] = dx_ref[...].astype(F32)
    y_out[...] = y_ref[...]

    @pl.when(pl.program_id(0) == 0)
    def _():
        for a, b in zip(ins, outs):
            b[...] = a[...]


def finish_call(dx, y, *arrays):
    each, local, width = dx.shape
    block = pl.BlockSpec((1, local // 2, width), lambda i: (i // 2, i % 2, 0))
    whole = [pl.BlockSpec(a.shape, lambda i: (0, 0)) for a in arrays]
    return pl.pallas_call(
        finish_kernel,
        grid=(2 * each,),
        in_specs=[block, block] + whole,
        out_specs=[block, block] + whole,
        out_shape=[sds(dx.shape, F32), sds(y.shape, y.dtype)] + [sds(a.shape, a.dtype) for a in arrays],
        compiler_params=pltpu.CompilerParams(vmem_limit_bytes=62 * MIB),
        name="finish",
    )(dx, y, *arrays)


def swap_cores(x):
    size = lax.axis_size("dp")
    return lax.ppermute(x, "dp", [(i, i ^ 1) for i in range(size)])


def swap_y(x):
    size = lax.axis_size("dp")
    return lax.ppermute(x, "dp", [(i, i ^ 2) for i in range(size)])


def along_seq(x, by):
    size = lax.axis_size("seq")
    return lax.ppermute(x, "seq", [(i, (i + by) % size) for i in range(size)])


def on_device_rows(cell_tokens, cell_lengths, out_grad, *raw_weights):
    (gain1, bias1, wqkv, qb, vb, wo, bo, gain2, bias2, win, bi, wback, bb) = tuple(
        (w if w.ndim == 2 else w[0] for w in raw_weights)
    )
    each, local, width = cell_tokens.shape
    row_length = local * lax.axis_size("seq")
    core = lax.axis_index("dp") % 2
    z = lax.axis_index("seq")

    lengths = jnp.where(z // each == core, cell_lengths, swap_cores(cell_lengths))
    lengths = lax.dynamic_index_in_dim(lengths, z % each, 0, keepdims=False)
    fq, fk, lo, hi = segment_terms(lengths, row_length)

    x, q, k, v = first_call(cell_tokens, wqkv, gain1, bias1, qb, vb)
    o, _ = attn_fwd(lo, hi, q, k, v, fq, fk)
    x, g, norm_t, q, k, v = pass_call(
        o, x, out_grad, wo, win, wback, wqkv, (bo, gain2, bias2, bi, bb, gain1, bias1, qb, vb))
    o, lse = attn_fwd(lo, hi, q, k, v, fq, fk)
    y, resid, slope, att_t, c_t, act_t, dr, do = turn_call(o, x, g, wo, win, wback, (bo, gain2, bias2, bi, bb))

    dq, dk, dv = attn_bwd(lo, hi, q, k, v, do, o, lse, fq, fk)
    outputs, dr, dp, do, *rest = back_call(
        dq, dk, dv, dr, x, y, g, slope, resid, c_t, act_t, wqkv, wo, win, wback, gain1, gain2, each)
    ffn = [w if t == 0 else along_seq(w, t) for t, w in enumerate(rest[:4])]
    back = [rest[4], swap_y(rest[5])]
    s_gain2, s_bias2, s_out, s_in, s_back = rest[6:]
    dq, dk, dv = attn_bwd(lo, hi, q, k, v, do, o, lse, fq, fk)
    sums = (s_out, s_gain2, s_bias2, s_in, s_back)
    g_out, g_qkv, g_in, g_back, small, in_grads = grads_call(
        (dq, dk, dv), dr, x, wqkv, gain1, att_t, norm_t, dp, ffn, back, sums, each)
    in_grads, outputs, g_out, g_qkv, g_in, g_back = finish_call(in_grads, outputs, g_out, g_qkv, g_in, g_back)

    flat = small.reshape(-1)
    parts = lax.axis_size("dp") * lax.axis_size("seq")
    owner = lax.axis_index("dp") * lax.axis_size("seq") + z
    shares, at = [], 0
    for total in [width] * 4 + [s.shape[1] for s in sums]:
        size = total // parts
        shares.append(lax.dynamic_slice_in_dim(flat, at + owner * size, size))
        at += total
    return (
        outputs[None],
        in_grads[None],
        shares[0][None],
        shares[1][None],
        g_qkv[None],
        shares[2][None],
        shares[3][None],
        g_out[None],
        shares[4][None],
        shares[5][None],
        shares[6][None],
        g_in[None],
        shares[7][None],
        g_back[None],
        shares[8][None],
    )


def either_plan(cell_tokens, *others):
    one_chip = lax.axis_size("dp") % 2 == 0 and lax.axis_size("seq") == 2 * cell_tokens.shape[0] and lax.axis_size("section") == 2 and lax.axis_size("dp") == lax.axis_size("seq") == 4
    return (on_device_rows if one_chip else on_device)(cell_tokens, *others)


def solution(mesh):
    in_specs = (
        P("dp", "seq", None),
        P("dp", None),
        P("dp", "seq", None),
        P("section", None),
        P("section", None),
        P("section", None, None),
        P("section", None),
        P("section", None),
        P("section", None, None),
        P("section", None),
        P("section", None),
        P("section", None),
        P("section", None, None),
        P("section", None),
        P("section", None, None),
        P("section", None),
    )
    out_specs = (
        P("section", "dp", "seq", None),
        P("section", "dp", "seq", None),
        P("section", ("dp", "seq")),
        P("section", ("dp", "seq")),
        P("section", ("dp", "seq"), None),
        P("section", ("dp", "seq")),
        P("section", ("dp", "seq")),
        P("section", ("dp", "seq"), None),
        P("section", ("dp", "seq")),
        P("section", ("dp", "seq")),
        P("section", ("dp", "seq")),
        P("section", ("dp", "seq"), None),
        P("section", ("dp", "seq")),
        P("section", ("dp", "seq"), None),
        P("section", ("dp", "seq")),
    )
    return jax.shard_map(
        either_plan, mesh=mesh, in_specs=in_specs, out_specs=out_specs, check_vma=False
    )
```

```python
from functools import partial

import jax
import jax.numpy as jnp
from jax import lax
from jax.experimental import pallas as pl
from jax.experimental.pallas import tpu as pltpu
from jax.sharding import PartitionSpec as P

HEADS = 12


SCALE = 0.125
EPS = 1e-05
MASKED = -1e30


def from_behind(x, axis, by):
    peers = lax.axis_size(axis)
    pairs = [(i, i + by) for i in range(peers) if 0 <= i + by < peers]
    return lax.ppermute(x, axis, pairs)


def norm_rows(values, gain_vec, bias_vec):
    centre = jnp.mean(values, axis=-1, keepdims=True)
    offset = values - centre
    spread = jnp.mean(offset * offset, axis=-1, keepdims=True)
    return offset * lax.rsqrt(spread + EPS) * gain_vec + bias_vec


def row_segments(lengths, row_length):
    limits = jnp.cumsum(lengths, axis=-1)
    places = jnp.arange(row_length, dtype=jnp.int32)
    return jnp.sum((places[None, :, None] >= limits[:, None, :]).astype(jnp.int32), axis=-1)


def split_heads(values):
    return values.reshape(values.shape[0], HEADS, values.shape[1] // HEADS)


def masked_scores(queries, keys_in, seg_query, seg_keys):
    scores = (
        jnp.einsum(
            "qhe,khe->hqk",
            split_heads(queries),
            split_heads(keys_in),
            preferred_element_type=jnp.float32,
        )
        * SCALE
    )
    return jnp.where((seg_query[:, None] == seg_keys[None, :])[None], scores, MASKED)


def softmax_parts(scores):
    highest = jnp.max(scores, axis=-1)
    raised = jnp.exp(scores - highest[..., None])
    summed = jnp.sum(raised, axis=-1)
    return (raised / summed[..., None], highest, summed)


def project_in(inputs, weights):
    normed = norm_rows(inputs, weights[0], weights[1]).astype(jnp.bfloat16)
    joined = jnp.dot(normed, weights[2], preferred_element_type=jnp.float32)
    model_width = inputs.shape[1]
    queries = (joined[:, :model_width] + weights[3]).astype(jnp.bfloat16)
    keys_out = joined[:, model_width : 2 * model_width].astype(jnp.bfloat16)
    values_out = (joined[:, 2 * model_width :] + weights[4]).astype(jnp.bfloat16)
    return (normed, queries, keys_out, values_out)


def attend(queries, keys_all, values_all, seg_own, seg_row):
    soft_probs, highest, summed = softmax_parts(masked_scores(queries, keys_all, seg_own, seg_row))
    low_probs = soft_probs.astype(jnp.bfloat16)
    combined = jnp.einsum(
        "hqk,khe->qhe", low_probs, split_heads(values_all), preferred_element_type=jnp.float32
    )
    return (
        combined.reshape(queries.shape).astype(jnp.bfloat16),
        soft_probs,
        low_probs,
        highest,
        summed,
    )


def finish(inputs, attended, weights):
    resid_sum = (
        inputs + jnp.dot(attended, weights[5], preferred_element_type=jnp.float32) + weights[6]
    )
    normed = norm_rows(resid_sum, weights[7], weights[8]).astype(jnp.bfloat16)
    hidden_pre = jnp.dot(normed, weights[9], preferred_element_type=jnp.float32) + weights[10]
    active = jax.nn.gelu(hidden_pre, approximate=False).astype(jnp.bfloat16)
    result = (
        resid_sum + jnp.dot(active, weights[11], preferred_element_type=jnp.float32) + weights[12]
    )
    return (result, resid_sum, normed, hidden_pre, active)


def store_slot(buffer, item_new, slot_idx, is_valid):
    current = lax.dynamic_index_in_dim(buffer, slot_idx, 0, keepdims=False)
    return lax.dynamic_update_index_in_dim(
        buffer, jnp.where(is_valid, item_new, current), slot_idx, 0
    )


def token_sum(values):
    return jnp.sum(values.astype(jnp.float32), axis=0)


def on_device(
    cell_tokens,
    cell_lengths,
    out_grad,
    norm1_gain,
    norm1_bias,
    qkv_weight,
    query_bias,
    value_bias,
    out_weight,
    out_bias,
    norm2_gain,
    norm2_bias,
    in_weight,
    in_bias,
    back_weight,
    back_bias,
):
    raw_weights = (
        norm1_gain,
        norm1_bias,
        qkv_weight,
        query_bias,
        value_bias,
        out_weight,
        out_bias,
        norm2_gain,
        norm2_bias,
        in_weight,
        in_bias,
        back_weight,
        back_bias,
    )
    weights = tuple(
        (weight[0].astype(jnp.float32) if weight.ndim == 2 else weight[0] for weight in raw_weights)
    )
    sections = lax.axis_size("section")
    section_rank = lax.axis_index("section")
    micro_count, local_len, model_width = cell_tokens.shape
    row_length = local_len * lax.axis_size("seq")
    own_start = lax.axis_index("seq") * local_len
    segments = row_segments(cell_lengths, row_length)
    tick_count = micro_count + sections - 1
    kept_depth = 1

    def row_segs(slot_idx):
        seg_row = lax.dynamic_index_in_dim(segments, slot_idx, 0, keepdims=False)
        return (seg_row, lax.dynamic_slice_in_dim(seg_row, own_start, local_len))

    def forward_tick(tick_now, state_now):
        incoming, kept_in, outputs, kept_keys, kept_values = state_now
        index_now = tick_now - section_rank
        is_valid = (index_now >= 0) & (index_now < micro_count)
        slot_idx = jnp.clip(index_now, 0, micro_count - 1)
        first_in = lax.dynamic_index_in_dim(cell_tokens, slot_idx, 0, keepdims=False)
        layer_in = jnp.where(section_rank == 0, first_in, incoming)
        seg_row, seg_own = row_segs(slot_idx)
        inputs = layer_in.astype(jnp.float32)
        normed, queries, keys_out, values_out = project_in(inputs, weights)
        keys_all, values_all = (
            lax.all_gather(keys_out, "seq", axis=0, tiled=True),
            lax.all_gather(values_out, "seq", axis=0, tiled=True),
        )
        attended = attend(queries, keys_all, values_all, seg_own, seg_row)[0]
        result = finish(inputs, attended, weights)[0].astype(jnp.bfloat16)
        kept_in = store_slot(kept_in, layer_in, slot_idx, is_valid)
        outputs = store_slot(outputs, result, slot_idx, is_valid)
        passed = from_behind(result, "section", 1)
        return (passed, kept_in, outputs, kept_keys, kept_values)

    start_state = (
        jnp.zeros((local_len, model_width), jnp.bfloat16),
        jnp.zeros((micro_count, local_len, model_width), jnp.bfloat16),
        jnp.zeros((micro_count, local_len, model_width), jnp.bfloat16),
        jnp.zeros((kept_depth, row_length, model_width), jnp.bfloat16),
        jnp.zeros((kept_depth, row_length, model_width), jnp.bfloat16),
    )
    ignored, kept_in, outputs, kept_keys, kept_values = lax.fori_loop(
        0, tick_count, forward_tick, start_state
    )

    def backward_tick(tick_now, state_now):
        incoming, in_grads, totals = state_now
        index_now = tick_now - (sections - 1 - section_rank)
        is_valid = (index_now >= 0) & (index_now < micro_count)
        slot_idx = jnp.clip(index_now, 0, micro_count - 1)
        from_out = lax.dynamic_index_in_dim(out_grad, slot_idx, 0, keepdims=False)
        grad_out = jnp.where(section_rank == sections - 1, from_out, incoming).astype(jnp.float32)
        inputs = lax.dynamic_index_in_dim(kept_in, slot_idx, 0, keepdims=False).astype(jnp.float32)
        seg_row, seg_own = row_segs(slot_idx)
        normed_one, queries, keys_out, values_out = project_in(inputs, weights)
        keys_all, values_all = (
            lax.all_gather(keys_out, "seq", axis=0, tiled=True),
            lax.all_gather(values_out, "seq", axis=0, tiled=True),
        )
        attended, soft_probs, low_probs, highest, summed = attend(
            queries, keys_all, values_all, seg_own, seg_row
        )
        result, resid_sum, normed_two, hidden_pre, active = finish(inputs, attended, weights)
        d_result = grad_out.astype(jnp.bfloat16)
        g_back_w = jnp.einsum("tf,td->fd", active, d_result, preferred_element_type=jnp.float32)
        g_back_b = token_sum(d_result)
        d_active = jnp.einsum(
            "td,fd->tf", d_result, weights[11], preferred_element_type=jnp.float32
        )
        gelu_value, gelu_back = jax.vjp(partial(jax.nn.gelu, approximate=False), hidden_pre)
        d_hidden = gelu_back(d_active)[0].astype(jnp.bfloat16)
        g_in_w = jnp.einsum("td,tf->df", normed_two, d_hidden, preferred_element_type=jnp.float32)
        g_in_b = token_sum(d_hidden)
        d_normed_two = jnp.einsum(
            "tf,df->td", d_hidden, weights[9], preferred_element_type=jnp.float32
        )
        norm_value, norm_two_back = jax.vjp(norm_rows, resid_sum, weights[7], weights[8])
        d_resid_norm, g_gain_two, g_bias_two = norm_two_back(d_normed_two)
        d_resid = grad_out + d_resid_norm
        d_proj = d_resid.astype(jnp.bfloat16)
        g_out_w = jnp.einsum("td,te->de", attended, d_proj, preferred_element_type=jnp.float32)
        g_out_b = token_sum(d_proj)
        d_attended = jnp.einsum(
            "te,de->td", d_proj, weights[5], preferred_element_type=jnp.float32
        ).astype(jnp.bfloat16)
        dout_heads = split_heads(d_attended)
        d_probs = jnp.einsum(
            "qhe,khe->hqk", dout_heads, split_heads(values_all), preferred_element_type=jnp.float32
        )
        delta_rows = jnp.sum(soft_probs * d_probs, axis=-1)
        d_scores = (soft_probs * (d_probs - delta_rows[..., None])).astype(jnp.bfloat16)
        d_query = (
            (
                jnp.einsum(
                    "hqk,khe->qhe",
                    d_scores,
                    split_heads(keys_all),
                    preferred_element_type=jnp.float32,
                )
                * SCALE
            )
            .reshape(local_len, model_width)
            .astype(jnp.bfloat16)
        )
        key_part = (
            jnp.einsum(
                "hqk,qhe->khe", d_scores, split_heads(queries), preferred_element_type=jnp.float32
            )
            * SCALE
        ).reshape(row_length, model_width)
        value_part = jnp.einsum(
            "hqk,qhe->khe", low_probs, dout_heads, preferred_element_type=jnp.float32
        ).reshape(row_length, model_width)
        d_keys, d_values = (
            lax.psum_scatter(
                key_part.astype(jnp.bfloat16), "seq", scatter_dimension=0, tiled=True
            ).astype(jnp.float32),
            lax.psum_scatter(
                value_part.astype(jnp.bfloat16), "seq", scatter_dimension=0, tiled=True
            ).astype(jnp.float32),
        )
        d_values_low = d_values.astype(jnp.bfloat16)
        d_joined = jnp.concatenate([d_query, d_keys.astype(jnp.bfloat16), d_values_low], axis=1)
        g_qkv_w = jnp.einsum("td,tf->df", normed_one, d_joined, preferred_element_type=jnp.float32)
        g_q_b = token_sum(d_query)
        g_v_b = token_sum(d_values_low)
        d_normed_one = jnp.einsum(
            "tf,df->td", d_joined, weights[2], preferred_element_type=jnp.float32
        )
        norm_value_one, norm_one_back = jax.vjp(norm_rows, inputs, weights[0], weights[1])
        d_inputs_norm, g_gain_one, g_bias_one = norm_one_back(d_normed_one)
        d_inputs = d_resid + d_inputs_norm
        new_grads = (
            g_gain_one,
            g_bias_one,
            g_qkv_w,
            g_q_b,
            g_v_b,
            g_out_w,
            g_out_b,
            g_gain_two,
            g_bias_two,
            g_in_w,
            g_in_b,
            g_back_w,
            g_back_b,
        )
        totals = tuple(
            (
                running + jnp.where(is_valid, grad_new, 0.0)
                for running, grad_new in zip(totals, new_grads)
            )
        )
        shown = jnp.where(
            section_rank == 0, d_inputs, d_inputs.astype(jnp.bfloat16).astype(jnp.float32)
        )
        in_grads = store_slot(in_grads, shown, slot_idx, is_valid)
        passed = from_behind(d_inputs.astype(jnp.bfloat16), "section", -1)
        return (passed, in_grads, totals)

    back_state = (
        jnp.zeros((local_len, model_width), jnp.bfloat16),
        jnp.zeros((micro_count, local_len, model_width), jnp.float32),
        tuple((jnp.zeros(weight.shape, jnp.float32) for weight in weights)),
    )
    ignored_grad, in_grads, totals = lax.fori_loop(0, tick_count, backward_tick, back_state)
    reduced = lax.psum_scatter(totals, ("dp", "seq"), scatter_dimension=0, tiled=True)
    return (
        outputs[None],
        in_grads[None],
        reduced[0][None],
        reduced[1][None],
        reduced[2][None],
        reduced[3][None],
        reduced[4][None],
        reduced[5][None],
        reduced[6][None],
        reduced[7][None],
        reduced[8][None],
        reduced[9][None],
        reduced[10][None],
        reduced[11][None],
        reduced[12][None],
    )


HEAD = 64
BIG = 1e30
NT = (((1,), (1,)), ((), ()))
F32 = jnp.float32
BF16 = jnp.bfloat16
BLK = 256
CH = 256
FINE = 128
PIECE = 512
UN = 8

def lane_mask(shape, h):
    lane = lax.broadcasted_iota(jnp.int32, shape, len(shape) - 1)
    return (lane < HEAD) if h == 0 else (lane >= HEAD)

def only(x, h):
    return jnp.where(lane_mask(x.shape, h), x, jnp.zeros_like(x))

def fwd_kernel(lo_ref, hi_ref, q_ref, k_ref, v_ref, fq_ref, fk_ref, o_ref, lse_ref):
    i = pl.program_id(0)
    n, w = k_ref.shape
    pairs = w // 128
    lo = lo_ref[i]
    count = hi_ref[i] - lo

    def run(lo, c):
        fq = fq_ref[...]
        at = pl.multiple_of(lo * FINE, FINE)
        pieces = []
        done = 0
        while done < c * FINE:
            size = min(PIECE, c * FINE - done)
            pieces.append(pl.ds(pl.multiple_of(at + done, FINE), size))
            done += size

        def scores(u, rows):
            p, h = divmod(u, 2)
            cols = slice(p * 128, (p + 1) * 128)
            q = q_ref[:, cols] * jnp.asarray(SCALE, BF16)
            qa = jnp.concatenate([only(q, h), fq], axis=1)
            kb = jnp.concatenate([k_ref[rows, cols], fk_ref[rows, :]], axis=1)
            return lax.dot_general(qa, kb, NT, preferred_element_type=F32)

        now = [scores(0, rows) for rows in pieces]
        outs, lses = [], []
        for u in range(2 * pairs):
            p, h = divmod(u, 2)
            cols = slice(p * 128, (p + 1) * 128)
            m = jnp.max(now[0], axis=1, keepdims=True)
            for s in now[1:]:
                m = jnp.maximum(m, jnp.max(s, axis=1, keepdims=True))
            r = None
            later = []
            for s, rows in zip(now, pieces):
                if u + 1 < 2 * pairs:
                    later.append(scores(u + 1, rows))
                pr = jnp.exp(s - m).astype(BF16)
                vb = jnp.concatenate([v_ref[rows, cols], jnp.ones((s.shape[1], 128), BF16)], axis=1)
                part = jnp.dot(pr, vb, preferred_element_type=F32)
                r = part if r is None else r + part
            now = later
            l = r[:, 128:]
            outs.append(r[:, :128] / l)
            lses.append(m + jnp.log(l))
            if h == 1:
                mask = lane_mask((BLK, 128), 0)
                o_ref[:, cols] = jnp.where(mask, outs[0], outs[1]).astype(BF16)
                both = jnp.where(mask, lses[0], lses[1]).T
                lse_ref[p, 0:1, :] = both[0:1, :]
                lse_ref[p, 1:2, :] = both[HEAD:HEAD + 1, :]
                outs, lses = [], []

    most = n // FINE
    below = 0
    for c in sorted({max(BLK // FINE, most * e // 16) for e in (2, 4, 8, 13, 14, 16)}):
        @pl.when((count > below) & (count <= c))
        def _(c=c):
            run(jnp.minimum(lo, most - c), c)
        below = c

def attn_fwd(lo, hi, q, k, v, fq, fk):
    n, w = q.shape
    pairs = w // 128
    blk = lambda i, lo, hi: (i, 0)
    full = lambda i, lo, hi: (0, 0)
    return pl.pallas_call(
        fwd_kernel,
        grid_spec=pltpu.PrefetchScalarGridSpec(
            num_scalar_prefetch=2,
            grid=(n // BLK,),
            in_specs=[pl.BlockSpec((BLK, w), blk), pl.BlockSpec((n, w), full), pl.BlockSpec((n, w), full),
                      pl.BlockSpec((BLK, 128), blk), pl.BlockSpec((n, 128), full)],
            out_specs=[pl.BlockSpec((BLK, w), blk), pl.BlockSpec((pairs, 8, BLK), lambda i, lo, hi: (0, 0, i))],
        ),
        out_shape=[jax.ShapeDtypeStruct((n, w), BF16), jax.ShapeDtypeStruct((pairs, 8, n), F32)],
        compiler_params=pltpu.CompilerParams(vmem_limit_bytes=62 * 2 ** 20),
        name="attn_fwd",
    )(lo, hi, q, k, v, fq, fk)

def bwd_kernel(lo_ref, hi_ref, q_ref, k_ref, v_ref, do_ref, o_ref, lse_ref, fq_ref, fk_ref,
               dq_ref, dk_ref, dv_ref, delta, dqt, dk_acc, dv_acc):
    j = pl.program_id(0)
    nb = pl.num_programs(0)
    n, w = q_ref.shape
    pairs = w // 128

    @pl.when(j == 0)
    def _():
        head = lax.broadcasted_iota(jnp.int32, (16, 128), 0)
        lane = lax.broadcasted_iota(jnp.int32, (16, 128), 1)
        sel = jnp.where(lane // HEAD == head, 1.0, 0.0).astype(BF16)

        def prep(b, c):
            rows = pl.ds(pl.multiple_of(b * CH, CH), CH)
            for p in range(pairs):
                cols = slice(p * 128, (p + 1) * 128)
                prod = do_ref[rows, cols].astype(F32) * o_ref[rows, cols].astype(F32)
                hi = prod.astype(BF16)
                lo = (prod - hi.astype(F32)).astype(BF16)
                d = lax.dot_general(sel, hi, NT, preferred_element_type=F32) + lax.dot_general(sel, lo, NT, preferred_element_type=F32)
                delta[p, :, rows] = d[0:8, :]
                dqt[p, :, rows] = jnp.zeros((128, CH), F32)
            return c
        lax.fori_loop(0, n // CH, prep, 0)

    lo = lo_ref[j]
    count = hi_ref[j] - lo
    dk_acc[...] = jnp.zeros_like(dk_acc)
    dv_acc[...] = jnp.zeros_like(dv_acc)

    def run(first, c):
        rows = pl.ds(pl.multiple_of(first * FINE, FINE), c * FINE)
        units = 2 * pairs

        def scores(u):
            p, h = divmod(u, 2)
            cols = slice(p * 128, (p + 1) * 128)
            kb = jnp.concatenate([only(k_ref[:, cols] * jnp.asarray(SCALE, BF16), h), fk_ref[...]], axis=1)
            qa = jnp.concatenate([q_ref[rows, cols], fq_ref[rows, :]], axis=1)
            s = lax.dot_general(kb, qa, NT, preferred_element_type=F32)
            dp = lax.dot_general(only(v_ref[:, cols], h), do_ref[rows, cols], NT, preferred_element_type=F32)
            return s, dp

        now = scores(0)
        dk, dv = [], []
        for u in range(units):
            p, h = divmod(u, 2)
            cols = slice(p * 128, (p + 1) * 128)
            later = scores(u + 1) if u + 1 < units else None
            s, dp = now
            pr = jnp.exp(s - lse_ref[p, h:h + 1, rows])
            ds = (pr * (dp - delta[p, h:h + 1, rows])).astype(BF16)
            dv.append(jnp.dot(pr.astype(BF16), do_ref[rows, cols], preferred_element_type=F32))
            dk.append(jnp.dot(ds, q_ref[rows, cols], preferred_element_type=F32))
            kt = (k_ref[:, cols] * jnp.asarray(SCALE, BF16)).T
            dqt[p, h * HEAD:(h + 1) * HEAD, rows] += jnp.dot(kt[h * HEAD:(h + 1) * HEAD, :], ds, preferred_element_type=F32)
            now = later
            if h == 1:
                mask = lane_mask((BLK, 128), 0)
                dk_acc[:, cols] += jnp.where(mask, dk[0], dk[1])
                dv_acc[:, cols] += jnp.where(mask, dv[0], dv[1])
                dk, dv = [], []

    @pl.loop(0, count // UN)
    def _(t):
        run(lo + t * UN, UN)

    left = count % UN
    for c in range(1, UN):
        @pl.when(left == c)
        def _(c=c):
            run(lo + (count - left), c)
    dk_ref[...] = (dk_acc[...] * SCALE).astype(BF16)
    dv_ref[...] = dv_acc[...].astype(BF16)

    @pl.when(j == nb - 1)
    def _():
        def fin(b, c):
            rows = pl.ds(pl.multiple_of(b * CH, CH), CH)
            for p in range(pairs):
                dq_ref[rows, p * 128:(p + 1) * 128] = dqt[p, :, rows].T.astype(BF16)
            return c
        lax.fori_loop(0, n // CH, fin, 0)

def attn_bwd(lo, hi, q, k, v, do, o, lse, fq, fk):
    n, w = q.shape
    pairs = w // 128
    full = lambda j, lo, hi: (0, 0)
    blk = lambda j, lo, hi: (j, 0)
    sh = jax.ShapeDtypeStruct((n, w), BF16)
    big = pl.BlockSpec((n, w), full, pipeline_mode=pl.Buffered(1))
    return pl.pallas_call(
        bwd_kernel,
        grid_spec=pltpu.PrefetchScalarGridSpec(
            num_scalar_prefetch=2,
            grid=(n // BLK,),
            in_specs=[big, pl.BlockSpec((BLK, w), blk), pl.BlockSpec((BLK, w), blk), big, big, pl.BlockSpec((pairs, 8, n), lambda j, lo, hi: (0, 0, 0)),
                      pl.BlockSpec((n, 128), full), pl.BlockSpec((BLK, 128), blk)],
            out_specs=[pl.BlockSpec((n, w), full), pl.BlockSpec((BLK, w), blk), pl.BlockSpec((BLK, w), blk)],
            scratch_shapes=[
                pltpu.VMEM((pairs, 8, n), F32),
                pltpu.VMEM((pairs, 128, n), F32),
                pltpu.VMEM((BLK, w), F32),
                pltpu.VMEM((BLK, w), F32),
            ],
        ),
        out_shape=[sh, sh, sh],
        compiler_params=pltpu.CompilerParams(vmem_limit_bytes=62 * 2 ** 20),
        name="attn_bwd",
    )(lo, hi, q, k, v, do, o, lse, fq, fk)

def segment_terms(lengths, n):
    cells = lengths.shape[0]
    place_of = jnp.arange(cells)
    ends = jnp.sum(jnp.where(place_of[:, None] <= place_of[None, :], lengths[:, None], 0), axis=0)
    starts = ends - lengths
    pos = jnp.arange(n, dtype=jnp.int32)[:, None]
    pad = lambda v: jnp.pad(v, (0, 128 - cells))[None, :]
    hot = (pos >= pad(starts)) & (pos < pad(ends))
    used = (jnp.arange(128) < cells)[None, :]
    fq = jnp.where(hot, -BIG, 0.0).astype(BF16)
    fk = jnp.where(used & ~hot, 1.0, 0.0).astype(BF16)
    first = jnp.arange(n // BLK, dtype=jnp.int32)[:, None] * BLK
    lo = jnp.max(jnp.where(starts[None, :] <= first, starts[None, :], 0), axis=1) // FINE
    hi = (jnp.min(jnp.where(ends[None, :] > first + BLK - 1, ends[None, :], n), axis=1) + FINE - 1) // FINE
    return fq, fk, lo.astype(jnp.int32), hi.astype(jnp.int32)


MIB = 2 ** 20
MESH = pl.DeviceIdType.MESH
ANY = pl.BlockSpec(memory_space=pl.ANY)
VMEM = pl.BlockSpec(memory_space=pltpu.VMEM)
DMA = pltpu.SemaphoreType.DMA
TOK = 256
COLS = 768


def sds(shape, dtype):
    return jax.ShapeDtypeStruct(shape, dtype)


def place():
    section, dp, seq = lax.axis_index("section"), lax.axis_index("dp"), lax.axis_index("seq")
    core = lax.rem(dp, 2)
    return section, dp, seq, core


def greet(*devices):
    barrier = pltpu.get_barrier_semaphore()
    for device in devices:
        pl.semaphore_signal(barrier, 1, device_id=device, device_id_type=MESH)
    pl.semaphore_wait(barrier, len(devices))


def column_mates(section, dp, seq, core):
    mates = [(section, dp, lax.rem(seq + t, 4)) for t in range(1, 4)]
    mates += [(section, dp + 1 - 2 * core, lax.rem(seq + t, 4)) for t in range(4)]
    return mates


def remote(src, dst, send_sem, recv_sem, device):
    return pltpu.make_async_remote_copy(
        src_ref=src, dst_ref=dst, send_sem=send_sem, recv_sem=recv_sem,
        device_id=device, device_id_type=MESH,
    )


def span(start, size):
    return pl.ds(pl.multiple_of(start, size), size)


def chunk(i):
    return span(i * TOK, TOK)


def row_norm(values):
    centre = jnp.mean(values, axis=-1, keepdims=True)
    offset = values - centre
    spread = jnp.mean(offset * offset, axis=-1, keepdims=True)
    rstd = lax.rsqrt(spread + EPS)
    return offset * rstd, rstd


def row_norm_back(grad, hat, rstd, gain):
    d_hat = grad * gain
    mean_d = jnp.mean(d_hat, axis=-1, keepdims=True)
    mean_dh = jnp.mean(d_hat * hat, axis=-1, keepdims=True)
    return rstd * (d_hat - mean_d - hat * mean_dh)


def fold(values):
    return jnp.sum(values.reshape(values.shape[0] // 8, 8, values.shape[1]), axis=0)


def up(ref):
    return ref[...].astype(F32)


def gelu_parts(x):
    size = jnp.abs(x)
    d = 1.0 + 0.2316418882 * size
    t = pl.reciprocal(d, approx=True)
    t = t * (2.0 - d * t)
    density = jnp.exp(-0.5 * (x * x)) * 0.3989422804014327
    poly = ((((1.330274429 * t - 1.821255978) * t + 1.781477937) * t - 0.356563782) * t + 0.319381530) * t
    tail = density * poly
    phi = jnp.where(x >= 0.0, 1.0 - tail, tail)
    return x * phi, phi + x * density


def ffn_loads(wo_in, win_in, wback_in, wo, win, wback, sem):
    pairs = [(wo_in, wo)]
    for f in range(win.shape[1] // COLS):
        cols = pl.ds(f * COLS, COLS)
        pairs += [(win_in.at[:, cols], win.at[:, cols]), (wback_in.at[cols], wback.at[cols])]
    return [pltpu.make_async_copy(a, b, sem.at[n]) for n, (a, b) in enumerate(pairs)]


class ToHeads:
    def __init__(self, buf, outs, tokens, width, sems, core, sibling):
        self.buf, self.outs, self.tokens, self.width = buf, outs, tokens, width
        self.own_sem, self.send_sem, self.recv_sem = sems
        self.core, self.sibling = core, sibling

    def _cols(self, part, core):
        return span(part * self.width + core * (self.width // 2), self.width // 2)

    def _sent(self, i, part, owner):
        rows = span(owner * self.tokens + i * TOK, TOK)
        return remote(self.buf.at[chunk(i), self._cols(part, 1 - self.core)], self.outs[part].at[rows],
                      self.send_sem.at[part, i], self.recv_sem.at[part, i], self.sibling)

    def _own(self, i, part):
        rows = span(self.core * self.tokens + i * TOK, TOK)
        return pltpu.make_async_copy(self.buf.at[chunk(i), self._cols(part, self.core)],
                                     self.outs[part].at[rows], self.own_sem.at[part, i])

    def start(self, i):
        for part in range(len(self.outs)):
            self._own(i, part).start()
            self._sent(i, part, self.core).start()

    def wait(self, i):
        for part in range(len(self.outs)):
            self._own(i, part).wait()
            self._sent(i, part, self.core).wait_send()
            self._sent(i, part, 1 - self.core).wait_recv()


class ToTokens:
    def __init__(self, ins, buf, tokens, width, sems, core, sibling):
        self.ins, self.buf, self.tokens, self.width = ins, buf, tokens, width
        self.own_sem, self.send_sem, self.recv_sem = sems
        self.core, self.sibling = core, sibling

    def _cols(self, part, core):
        return span(part * self.width + core * (self.width // 2), self.width // 2)

    def _sent(self, i, part, owner):
        rows = span((1 - self.core) * self.tokens + i * TOK, TOK)
        return remote(self.ins[part].at[rows], self.buf.at[chunk(i), self._cols(part, owner)],
                      self.send_sem.at[part, i], self.recv_sem.at[part, i], self.sibling)

    def _own(self, i, part):
        rows = span(self.core * self.tokens + i * TOK, TOK)
        return pltpu.make_async_copy(self.ins[part].at[rows], self.buf.at[chunk(i), self._cols(part, self.core)],
                                     self.own_sem.at[part, i])

    def start(self, i):
        for part in range(len(self.ins)):
            self._own(i, part).start()
            self._sent(i, part, self.core).start()

    def wait(self, i):
        for part in range(len(self.ins)):
            self._own(i, part).wait()
            self._sent(i, part, 1 - self.core).wait_recv()

    def wait_sent(self, i):
        for part in range(len(self.ins)):
            self._sent(i, part, self.core).wait_send()


def swap_sems(parts, steps):
    return [DMA((parts, steps))] * 3


class Blocks:
    def __init__(self, rows_ref, blocks_ref, gather, sems, section, dp, seq, core):
        self.rows, self.blocks, self.gather = rows_ref, blocks_ref, gather
        self.bounce, self.own_sem, self.send_sem, self.recv_sem = sems
        self.section, self.seq, self.core, self.column = section, seq, core, dp - core
        self.each, self.local, _ = blocks_ref.shape

    def _move(self, j):
        target_core, target_seq = self.seq // self.each, self.core * self.each + j
        slot = lax.rem(self.seq, self.each)
        here = (target_core == self.core) & (target_seq == self.seq)
        if self.gather:
            src, dst = self.blocks.at[j], self.rows.at[span(slot * self.local, self.local)]
        else:
            src, dst = self.rows.at[pl.ds(j * self.local, self.local)], self.blocks.at[slot]
        target = (self.section, self.column + target_core, target_seq)
        return here, src, dst, slot, target

    def start(self, *which):
        for j in which or range(self.each):
            here, src, dst, slot, target = self._move(j)

            @pl.when(here)
            def _():
                pltpu.make_async_copy(src, dst if self.bounce is None else self.bounce, self.own_sem).start()

            @pl.when(jnp.logical_not(here))
            def _():
                remote(src, dst, self.send_sem.at[j], self.recv_sem.at[slot], target).start()

    def wait(self):
        for j in range(self.each):
            here, src, dst, slot, target = self._move(j)

            @pl.when(here)
            def _():
                pltpu.make_async_copy(src, dst if self.bounce is None else self.bounce, self.own_sem).wait()
                if self.bounce is not None:
                    out = pltpu.make_async_copy(self.bounce, dst, self.own_sem)
                    out.start()
                    out.wait()

            @pl.when(jnp.logical_not(here))
            def _():
                remote(src, dst, self.send_sem.at[j], self.recv_sem.at[slot], target).wait_send()
        for j in range(self.each):
            here = (self.seq // self.each == self.core) & (self.core * self.each + j == self.seq)
            mate = (self.section, self.column + 1 - self.core, self.seq)
            if self.gather:
                dst = self.rows.at[pl.ds(j * self.local, self.local)]
                src = self.blocks.at[0]
            else:
                dst = self.blocks.at[j]
                src = self.rows.at[pl.ds(0, self.local)]

            @pl.when(jnp.logical_not(here))
            def _():
                remote(src, dst, self.send_sem.at[0], self.recv_sem.at[j], mate).wait_recv()


def block_scratch(each, local, width):
    return [pltpu.VMEM((local, width), BF16), DMA, DMA((each,)), DMA((each,))]


def project(x, gain, bias, w, qb, vb, buf, rows):
    width = x.shape[1]
    hat, _ = row_norm(x)
    a = (hat * up(gain) + up(bias)).astype(BF16)
    for part in range(3):
        cols = slice(part * width, (part + 1) * width)
        m = jnp.dot(a, w[:, cols], preferred_element_type=F32)
        if part == 0:
            m = m + up(qb)
        if part == 2:
            m = m + up(vb)
        buf[rows, cols] = m.astype(BF16)
    return a


def first_kernel(x_ref, w_in, gain, bias, qb, vb, x_out, q_ref, k_ref, v_ref,
                 xb, w, buf, w_sem, out_sem, own_sem, send_sem, recv_sem, *sems):
    section, dp, seq, core = place()
    sibling = (section, dp + 1 - 2 * core, seq)
    each, local, width = x_ref.shape
    part = local // 2
    column = dp - core
    load = pltpu.make_async_copy(w_in, w, w_sem)
    load.start()
    greet(*[(s, column + c, z) for s in range(2) for c in range(2) for z in range(2 * each)])

    def move(m):
        target_core, target_seq = seq // each, core * each + m
        slot = lax.rem(seq, each)
        here = (section == 0) & (target_core == core) & (target_seq == seq)
        src = x_ref.at[m, span(section * part, part)]
        dst = xb.at[span(slot * local + section * part, part)]
        return here, src, dst, slot, (0, column + target_core, target_seq)

    for m in range(each):
        here, src, dst, slot, target = move(m)

        @pl.when(here)
        def _():
            pltpu.make_async_copy(src, dst, own_sem).start()

        @pl.when(jnp.logical_not(here))
        def _():
            remote(src, dst, send_sem.at[m], recv_sem.at[section, slot], target).start()
    load.wait()

    @pl.when(section == 0)
    def _():
        swap = ToHeads(buf, (q_ref, k_ref, v_ref), each * local, width, sems, core, sibling)

        def out(i):
            return pltpu.make_async_copy(xb.at[chunk(i)], x_out.at[chunk(i)], out_sem.at[i])

        for h in range(2):
            for j in range(each):
                here = (seq // each == core) & (core * each + j == seq) & (h == 0)
                dst = xb.at[pl.ds(j * local + h * part, part)]

                @pl.when(here)
                def _():
                    pltpu.make_async_copy(x_ref.at[0, pl.ds(0, part)], dst, own_sem).wait()

                @pl.when(jnp.logical_not(here))
                def _():
                    remote(x_ref.at[0, pl.ds(0, part)], dst, send_sem.at[0], recv_sem.at[h, j], sibling).wait_recv()

                for i in range((j * local + h * part) // TOK, (j * local + (h + 1) * part) // TOK):
                    rows = slice(i * TOK, (i + 1) * TOK)
                    project(xb[rows, :].astype(F32), gain, bias, w, qb, vb, buf, rows)
                    out(i).start()
                    swap.start(i)
        for i in range(each * local // TOK):
            out(i).wait()
            swap.wait(i)

    for m in range(each):
        here, src, dst, slot, target = move(m)

        @pl.when(jnp.logical_not(here))
        def _():
            remote(src, dst, send_sem.at[m], recv_sem.at[section, slot], target).wait_send()


def first_call(x, w, gain, bias, qb, vb):
    each, local, width = x.shape
    tokens = each * local
    steps = tokens // TOK
    out = sds((2 * tokens, width // 2), BF16)
    return pl.pallas_call(
        first_kernel,
        in_specs=[ANY, ANY] + [VMEM] * 4,
        out_specs=[ANY] * 4,
        out_shape=[sds((tokens, width), BF16), out, out, out],
        scratch_shapes=[
            pltpu.VMEM((tokens, width), BF16), pltpu.VMEM(w.shape, BF16), pltpu.VMEM((tokens, 3 * width), BF16),
            DMA, DMA((steps,)), DMA, DMA((each,)), DMA((2, each))] + swap_sems(3, steps),
        compiler_params=pltpu.CompilerParams(collective_id=1, has_side_effects=True, vmem_limit_bytes=62 * MIB),
        name="rows_qkv",
    )(x, w, gain, bias, qb, vb)


def feed(i, out, att, x, wo, win, wback, bo, g2, b2, bi, bb, keep=None, ready=None):
    rows = chunk(i)
    hidden = win.shape[1]
    if ready:
        ready[0].wait()
    resid = x[rows, :].astype(F32) + up(bo) + jnp.dot(att[rows, :], wo[...], preferred_element_type=F32)
    hat, rstd = row_norm(resid)
    c = (hat * up(g2) + up(b2)).astype(BF16)
    if keep is not None:
        resid_b, slope_b, att_t, c_t, act_t = keep
        resid_b[rows, :] = resid
        att_t[:, rows] = att[rows, :].T
        c_t[:, rows] = c.T
    total = resid + up(bb)
    yield
    for f in range(hidden // COLS):
        cols = slice(f * COLS, (f + 1) * COLS)
        if ready:
            ready[1 + 2 * f].wait()
            ready[2 + 2 * f].wait()
        inner = jnp.dot(c, win[:, cols], preferred_element_type=F32) + bi[:, cols].astype(F32)
        yield
        active, slope = gelu_parts(inner)
        active = active.astype(BF16)
        if keep is not None:
            slope_b[rows, cols] = slope.astype(BF16)
            act_t[cols, rows] = active.T
        total = total + jnp.dot(active, wback[cols, :], preferred_element_type=F32)
        yield
    out[rows, :] = total.astype(BF16)


def feed_back(i, dy, slope_b, resid_b, wo, win, wback, g2, di_b, dr_b, dp_b, da_b, sums):
    rows = chunk(i)
    hidden = win.shape[1]
    g = dy.astype(F32)
    d_c = jnp.zeros(dy.shape, F32)
    yield
    for f in range(hidden // COLS):
        cols = slice(f * COLS, (f + 1) * COLS)
        d_active = lax.dot_general(dy, wback[cols, :], NT, preferred_element_type=F32)
        yield
        d_inner = d_active * slope_b[rows, cols].astype(F32)
        if sums:
            sums[3][:, cols] += fold(d_inner)
        d_inner = d_inner.astype(BF16)
        if di_b is not None:
            di_b[rows, cols] = d_inner
        d_c = d_c + lax.dot_general(d_inner, win[:, cols], NT, preferred_element_type=F32)
        yield
    hat, rstd = row_norm(resid_b[rows, :])
    d_resid = g + row_norm_back(d_c, hat, rstd, up(g2))
    d_proj = d_resid.astype(BF16)
    dr_b[rows, :] = d_resid
    if sums:
        s_gain, s_bias, s_out, _, s_back = sums
        s_gain[...] += fold(d_c * hat)
        s_bias[...] += fold(d_c)
        s_out[...] += fold(d_resid)
        s_back[...] += fold(g)
    if dp_b is not None:
        dp_b[rows, :] = d_proj
    da_b[rows, :] = lax.dot_general(d_proj, wo[...], NT, preferred_element_type=F32).astype(BF16)


def in_turns(*parts):
    parts = list(parts)
    while parts:
        for part in list(parts):
            if next(part, part) is part:
                parts.remove(part)


def pass_kernel(o_ref, x_ref, g_ref, wo_in, win_in, wback_in, wqkv_in, bo, g2, b2, bi, bb, g1, b1, qb, vb,
                x_out, g_out, n_out, q_ref, k_ref, v_ref,
                wo, win, wback, wqkv, att, yb, xn, buf, w_sem, x_send, x_recv, x_sem, *sems):
    section, dp, seq, core = place()
    sibling = (section, dp + 1 - 2 * core, seq)
    across = (1 - section, dp, seq)
    tokens, width = x_ref.shape
    steps = tokens // TOK
    loads = ffn_loads(wo_in, win_in, wback_in, wo, win, wback, w_sem)
    load_qkv = pltpu.make_async_copy(wqkv_in, wqkv, w_sem.at[len(loads)])
    loads[0].start()
    greet(across, *column_mates(section, dp, seq, core))
    to_tokens = ToTokens((o_ref,), att, tokens, width, sems[:3], core, sibling)
    to_heads = ToHeads(buf, (q_ref, k_ref, v_ref), tokens, width, sems[3:6], core, sibling)
    blocks = Blocks(g_out, g_ref, True, sems[6:10], section, dp, seq, core)
    to_tokens.start(0)
    for load in loads[1:]:
        load.start()

    @pl.loop(1, steps)
    def _(i):
        to_tokens.start(i)

    load_qkv.start()

    @pl.when(section == 1)
    def _():
        blocks.start()

    def passed(i):
        return remote(yb.at[chunk(i)], xn.at[chunk(i)], x_send.at[i], x_recv.at[i], across)

    def kept(i):
        return pltpu.make_async_copy(xn.at[chunk(i)], x_out.at[chunk(i)], x_sem.at[i])

    def send_chunk(i, ready=None):
        in_turns(feed(i, yb, att, x_ref, wo, win, wback, bo, g2, b2, bi, bb, ready=ready))
        passed(i).start()
        xn[chunk(i), :] = x_ref[chunk(i), :]

    to_tokens.wait(0)

    @pl.when(section == 0)
    def _():
        send_chunk(0, loads)

    @pl.when(section == 1)
    def _():
        for load in loads:
            load.wait()

    @pl.loop(1, steps)
    def _(i):
        to_tokens.wait(i)

        @pl.when(section == 0)
        def _():
            send_chunk(i)

    load_qkv.wait()

    @pl.loop(0, steps)
    def _(i):
        @pl.when(section == 1)
        def _():
            passed(i).wait_recv()

        kept(i).start()
        a = project(xn[chunk(i), :].astype(F32), g1, b1, wqkv, qb, vb, buf, chunk(i))
        n_out[:, chunk(i)] = a.T
        to_heads.start(i)

    @pl.loop(0, steps)
    def _(i):
        to_tokens.wait_sent(i)
        to_heads.wait(i)
        kept(i).wait()

        @pl.when(section == 0)
        def _():
            passed(i).wait_send()

    @pl.when(section == 1)
    def _():
        blocks.wait()


def pass_call(o, x, g, wo, win, wback, wqkv, vectors):
    tokens, width = x.shape
    steps = tokens // TOK
    each = g.shape[0]
    out = sds((2 * tokens, width // 2), BF16)
    low = sds(x.shape, BF16)
    low_buf = pltpu.VMEM(x.shape, BF16)
    return pl.pallas_call(
        pass_kernel,
        in_specs=[ANY, VMEM, ANY, ANY, ANY, ANY, ANY] + [VMEM] * len(vectors),
        out_specs=[ANY, ANY, VMEM, ANY, ANY, ANY],
        out_shape=[low, low, sds((width, tokens), BF16), out, out, out],
        scratch_shapes=[pltpu.VMEM(w.shape, BF16) for w in (wo, win, wback, wqkv)]
        + [low_buf, low_buf, low_buf, pltpu.VMEM((tokens, 3 * width), BF16),
           DMA((2 + 2 * (win.shape[1] // COLS),)), DMA((steps,)), DMA((steps,)), DMA((steps,))]
        + swap_sems(1, steps) + swap_sems(3, steps) + block_scratch(each, tokens // each, width),
        compiler_params=pltpu.CompilerParams(collective_id=2, has_side_effects=True, vmem_limit_bytes=62 * MIB),
        name="ffn_pass_qkv",
    )(o, x, g, wo, win, wback, wqkv, *vectors)


def turn_kernel(each, o_ref, x_ref, g_ref, wo_in, win_in, wback_in, bo, g2, b2, bi, bb, *refs):
    y_outs, refs = refs[:each], refs[each:]
    turn_body(each, y_outs, o_ref, x_ref, g_ref, wo_in, win_in, wback_in, bo, g2, b2, bi, bb, *refs)


def turn_body(each, y_outs, o_ref, x_ref, g_ref, wo_in, win_in, wback_in, bo, g2, b2, bi, bb,
                resid_out, slope_out, att_out, c_out, act_out, dr_out, da_ref,
                wo, win, wback, att, yb, resid_b, slope_b, att_t, c_t, act_t, dr_b, da_b,
                w_sem, out_sem, *sems):
    section, dp, seq, core = place()
    sibling = (section, dp + 1 - 2 * core, seq)
    tokens, width = x_ref.shape
    steps = tokens // TOK
    loads = ffn_loads(wo_in, win_in, wback_in, wo, win, wback, w_sem)
    loads[0].start()
    greet(sibling)
    to_tokens = ToTokens((o_ref,), att, tokens, width, sems[:3], core, sibling)
    to_heads = ToHeads(da_b, (da_ref,), tokens, width, sems[3:6], core, sibling)
    to_tokens.start(0)
    for load in loads[1:]:
        load.start()

    @pl.loop(1, steps)
    def _(i):
        to_tokens.start(i)

    def copies(i, which, at, turned=False):
        where = (slice(None), chunk(i)) if turned else (chunk(i),)
        return [pltpu.make_async_copy(b.at[where], o.at[where], out_sem.at[at + n, i]) for n, (b, o) in enumerate(which)]

    def y_moves(i, act):
        per = tokens // each // TOK
        step = lax.rem(seq - i // per + each, each)
        for n in range(each):
            @pl.when(step == n)
            def _():
                act(pltpu.make_async_copy(yb.at[chunk(i)], y_outs[n].at[chunk(lax.rem(i, per))], out_sem.at[0, i]))

    def results(i):
        return copies(i, ((resid_b, resid_out), (slope_b, slope_out)), 1) + copies(
            i, ((att_t, att_out), (c_t, c_out), (act_t, act_out)), 3, True)

    def back_results(i):
        return copies(i, ((dr_b, dr_out),), 6)

    def forward(i, ready=None):
        return feed(i, yb, att, x_ref, wo, win, wback, bo, g2, b2, bi, bb, (resid_b, slope_b, att_t, c_t, act_t), ready)

    def backward(i):
        return feed_back(i, g_ref[chunk(i), :], slope_b, resid_b, wo, win, wback, g2, None, dr_b, None, da_b, None)

    to_tokens.wait(0)
    in_turns(forward(0, loads))
    y_moves(jnp.int32(0), lambda copy: copy.start())
    for copy in results(0):
        copy.start()

    @pl.loop(1, steps)
    def _(i):
        to_tokens.wait(i)
        in_turns(forward(i))
        in_turns(backward(i - 1))
        to_heads.start(i - 1)
        y_moves(i, lambda copy: copy.start())
        for copy in results(i) + back_results(i - 1):
            copy.start()

    in_turns(backward(steps - 1))
    to_heads.start(steps - 1)
    for copy in back_results(steps - 1):
        copy.start()

    @pl.loop(0, steps)
    def _(i):
        to_tokens.wait_sent(i)
        to_heads.wait(i)
        y_moves(i, lambda copy: copy.wait())
        for copy in results(i) + back_results(i):
            copy.wait()


def turn_call(o, x, g, wo, win, wback, vectors, each):
    tokens, width = x.shape
    hidden = win.shape[1]
    steps = tokens // TOK
    low, full = sds(x.shape, BF16), sds(x.shape, F32)
    turned = sds((width, tokens), BF16)
    outs = [full, sds((tokens, hidden), BF16), turned, turned, sds((hidden, tokens), BF16), full]
    buf = lambda s: pltpu.VMEM(s.shape, s.dtype)
    return pl.pallas_call(
        partial(turn_kernel, each),
        in_specs=[ANY, VMEM, VMEM, ANY, ANY, ANY] + [VMEM] * len(vectors),
        out_specs=[ANY] * (each + 7),
        out_shape=[sds((tokens // each, width), BF16)] * each + outs + [sds((2 * tokens, width // 2), BF16)],
        scratch_shapes=[buf(wo), buf(win), buf(wback), buf(low), buf(low)] + [buf(s) for s in outs] + [buf(low)]
        + [DMA((1 + 2 * (hidden // COLS),)), DMA((7, steps))] + swap_sems(1, steps) + swap_sems(1, steps),
        compiler_params=pltpu.CompilerParams(collective_id=3, has_side_effects=True, vmem_limit_bytes=62 * MIB),
        name="ffn_turn",
    )(o, x, g, wo, win, wback, *vectors)


def input_back(i, dj, dr, x, w, gain, sums):
    rows = chunk(i)
    width = x.shape[1]
    d_a = lax.dot_general(dj[rows, :], w[...], NT, preferred_element_type=F32)
    hat, rstd = row_norm(x[rows, :].astype(F32))
    if sums:
        s_gain, s_bias, s_q, s_v = sums
        s_q[...] += fold(dj[rows, :width].astype(F32))
        s_v[...] += fold(dj[rows, 2 * width:].astype(F32))
        s_gain[...] += fold(d_a * hat)
        s_bias[...] += fold(d_a)
    return (dr[rows, :] + row_norm_back(d_a, hat, rstd, up(gain))).astype(BF16)


def back_kernel(dq_ref, dk_ref, dv_ref, dr_ref, x_ref, g_in, slope_in, resid_in, c_in, act_in,
                wqkv_in, wo_in, win_in, wback_in, g1, g2,
                dx_out, dr_out, dp_out, da_ref, *rest):
    rest = list(rest)
    shares = [rest.pop(0) for _ in range(4)]
    y_shares = [rest.pop(0) for _ in range(2)]
    s_gain, s_bias, s_out, s_in, s_back = [rest.pop(0) for _ in range(5)]
    wqkv, wo, win, wback, dj, dx, gb, di, dr, dp, da_b, c_t, act_t, grad_in, grad_back = [rest.pop(0) for _ in range(15)]
    (w_sem, in_sem, a_sem, t_sem, out_sem, g_sem, x_send, x_recv, ready, r_send, r_recv, r_out) = rest[:12]
    sems = rest[12:]
    section, dp_index, seq, core = place()
    sibling = (section, dp_index + 1 - 2 * core, seq)
    across = (1 - section, dp_index, seq)
    tokens, width = gb.shape
    hidden = win.shape[1]
    steps = tokens // TOK
    blocks_of = hidden // COLS
    x_b, dr_in = da_b, grad_back
    loads = [pltpu.make_async_copy(a, b, w_sem.at[n]) for n, (a, b) in enumerate(
        ((wqkv_in, wqkv), (wback_in, wback), (win_in, win), (wo_in, wo), (c_in, c_t)))]

    def kept(i):
        return [pltpu.make_async_copy(a.at[chunk(i)], b.at[chunk(i)], in_sem.at[n, i])
                for n, (a, b) in enumerate(((slope_in, di), (resid_in, dr)))]

    def turned(i):
        return pltpu.make_async_copy(act_in.at[:, chunk(i)], act_t.at[lax.rem(i, 2)], t_sem.at[i])

    def given(i):
        return [pltpu.make_async_copy(a.at[chunk(i)], b.at[chunk(i)], a_sem.at[n, i])
                for n, (a, b) in enumerate(((x_ref, x_b), (dr_ref, dr_in)))]

    def last(i):
        return pltpu.make_async_copy(g_in.at[chunk(i)], gb.at[chunk(i)], g_sem.at[i])

    def passed(i):
        return remote(dx.at[chunk(i)], gb.at[chunk(i)], x_send.at[i], x_recv.at[i], across)

    def results(i):
        return [pltpu.make_async_copy(b.at[chunk(i)], o.at[chunk(i)], out_sem.at[n, i])
                for n, (b, o) in enumerate(((dr, dr_out), (dp, dp_out)))]

    @pl.when(section == 1)
    def _():
        loads[0].start()

    greet(across, *column_mates(section, dp_index, seq, core))
    to_tokens = ToTokens((dq_ref, dk_ref, dv_ref), dj, tokens, width, sems[:3], core, sibling)
    to_heads = ToHeads(da_b, (da_ref,), tokens, width, sems[3:6], core, sibling)
    own_blocks = Blocks(dx, dx_out, False, [None] + sems[6:9], section, dp_index, seq, core)

    @pl.when(section == 1)
    def _():
        @pl.loop(0, steps)
        def _(i):
            to_tokens.start(i)
            for copy in given(i):
                copy.start()

        loads[0].wait()

        @pl.loop(0, steps)
        def _(i):
            to_tokens.wait(i)
            for copy in given(i):
                copy.wait()
            last(i).start()
            dx[chunk(i), :] = input_back(i, dj, dr_in, x_b, wqkv, g1, None)
            passed(i).start()

        own_blocks.start()

    for load in loads[1:]:
        load.start()

    @pl.loop(0, steps)
    def _(i):
        for copy in kept(i):
            copy.start()

    for i in range(2):
        turned(i).start()
    sums = (s_gain, s_bias, s_out, s_in, s_back)
    for s in sums + (grad_in, grad_back):
        s[...] = jnp.zeros_like(s)
    for load in loads[1:]:
        load.wait()

    def grad_block(i, n):
        part = span(n % blocks_of * COLS, COLS) if not isinstance(n, int) else pl.ds(n % blocks_of * COLS, COLS)
        if n < blocks_of:
            grad_in[:, part] += jnp.dot(c_t[:, chunk(i)], di[chunk(i), part], preferred_element_type=F32)
        else:
            grad_back[part, :] += jnp.dot(act_t[lax.rem(i, 2), part, :], gb[chunk(i), :], preferred_element_type=F32)

    def feed_step(i):
        for copy in kept(i):
            copy.wait()

        @pl.when(section == 0)
        def _():
            passed(i).wait_recv()

        @pl.when(section == 1)
        def _():
            last(i).wait()

        in_turns(feed_back(i, gb[chunk(i), :], di, dr, wo, win, wback, g2, di, dr, dp, da_b, sums))
        to_heads.start(i)
        for copy in results(i):
            copy.start()

    @pl.loop(0, steps - 1)
    def _(i):
        feed_step(i)
        turned(i).wait()
        for n in range(2 * blocks_of):
            grad_block(i, n)

        @pl.when(i + 2 < steps)
        def _():
            turned(i + 2).start()

    end = steps - 1
    feed_step(end)
    pl.semaphore_signal(ready, 1, device_id=sibling, device_id_type=MESH)
    turned(end).wait()
    pl.semaphore_wait(ready, 1)

    size_in, size_back = width // 16, hidden // 16

    def sent_in(n, yy):
        cols = pl.ds(n * COLS, COLS)
        return remote(win.at[pl.ds(yy * 4 * size_in, 4 * size_in), cols],
                      win.at[pl.ds((2 + yy) * 4 * size_in, 4 * size_in), cols],
                      r_send.at[2 * n + yy], r_recv.at[2 * n + yy], sibling)

    def sent_back(n):
        yy = n // 2
        return remote(wback.at[pl.ds(yy * COLS, COLS)], wback.at[pl.ds((2 + yy) * COLS, COLS)],
                      r_send.at[2 * blocks_of + yy], r_recv.at[2 * blocks_of + yy], sibling)

    def write_in(t, yy):
        rows = span((2 + yy) * 4 * size_in + lax.rem(seq + t, 4) * size_in, size_in)
        return pltpu.make_async_copy(win.at[rows], shares[t].at[pl.ds(yy * size_in, size_in)], r_out.at[t, yy])

    def write_back(t):
        yy = (dp_index // 2 + t) % 2
        return pltpu.make_async_copy(wback.at[span((2 + yy) * COLS, COLS)], y_shares[t], r_out.at[4, t])

    for n in range(blocks_of):
        grad_block(end, n)
        cols = slice(n * COLS, (n + 1) * COLS)
        for yy in range(2):
            win[yy * 4 * size_in:(yy + 1) * 4 * size_in, cols] = grad_in[core_rows(size_in, yy, 1 - core), cols].astype(BF16)
            sent_in(n, yy).start()
    for n in range(blocks_of):
        grad_block(end, blocks_of + n)
        if n % 2 == 1:
            yy = n // 2
            wback[yy * COLS:(yy + 1) * COLS, :] = grad_back[core_rows(size_back, yy, 1 - core), :].astype(BF16)
            sent_back(n).start()
    for n in range(blocks_of):
        cols = slice(n * COLS, (n + 1) * COLS)
        for yy in range(2):
            sent_in(n, yy).wait_recv()
            rows = slice((2 + yy) * 4 * size_in, (3 + yy) * 4 * size_in)
            win[rows, cols] = (grad_in[core_rows(size_in, yy, core), cols] + win[rows, cols].astype(F32)).astype(BF16)
    for yy in range(2):
        for t in range(4):
            write_in(t, yy).start()
    for yy in range(2):
        sent_back(2 * yy).wait_recv()
        rows = slice((2 + yy) * COLS, (3 + yy) * COLS)
        wback[rows, :] = (grad_back[core_rows(size_back, yy, core), :] + wback[rows, :].astype(F32)).astype(BF16)
    for t in range(2):
        write_back(t).start()

    @pl.loop(0, steps)
    def _(i):
        to_heads.wait(i)
        for copy in results(i):
            copy.wait()

        @pl.when(section == 1)
        def _():
            to_tokens.wait_sent(i)
            passed(i).wait_send()

    for yy in range(2):
        for n in range(blocks_of):
            sent_in(n, yy).wait_send()
        sent_back(2 * yy).wait_send()
        write_back(yy).wait()
        for t in range(4):
            write_in(t, yy).wait()

    @pl.when(section == 1)
    def _():
        own_blocks.wait()


def back_call(dq, dk, dv, dr, x, g, slope, resid, c_t, act_t, wqkv, wo, win, wback, g1, g2, each):
    tokens, width = x.shape
    hidden = win.shape[1]
    steps = tokens // TOK
    blocks_of = hidden // COLS
    low, full, wide = sds(x.shape, BF16), sds(x.shape, F32), sds((tokens, hidden), BF16)
    one = sds((8, width), F32)
    buf = lambda s: pltpu.VMEM(s.shape, s.dtype)
    shares = [sds((width // 8, hidden), BF16)] * 4 + [sds((hidden // 4, width), BF16)] * 2
    return pl.pallas_call(
        back_kernel,
        in_specs=[ANY] * 14 + [VMEM, VMEM],
        out_specs=[ANY] * 10 + [VMEM] * 5,
        out_shape=[sds((each, tokens // each, width), BF16), full, low, sds((2 * tokens, width // 2), BF16)]
        + shares + [one, one, one, sds((8, hidden), F32), one],
        scratch_shapes=[buf(wqkv), buf(wo), buf(win), buf(wback), pltpu.VMEM((tokens, 3 * width), BF16),
                        buf(low), buf(low), buf(wide), buf(full), buf(low), buf(low), buf(c_t),
                        pltpu.VMEM((2, hidden, TOK), BF16), pltpu.VMEM((width, hidden), F32), pltpu.VMEM((hidden, width), F32),
                        DMA((5,)), DMA((2, steps)), DMA((2, steps)), DMA((steps,)), DMA((2, steps)), DMA((steps,)),
                        DMA((steps,)), DMA((steps,)), pltpu.SemaphoreType.REGULAR,
                        DMA((2 * blocks_of + 2,)), DMA((2 * blocks_of + 2,)), DMA((5, 2))]
        + swap_sems(3, steps) + swap_sems(1, steps) + block_scratch(each, 16, width)[1:],
        compiler_params=pltpu.CompilerParams(collective_id=4, has_side_effects=True, vmem_limit_bytes=62 * MIB),
        name="qkv_back_pass",
    )(dq, dk, dv, dr, x, g, slope, resid, c_t, act_t, wqkv, wo, win, wback, g1, g2)


def core_rows(size, yy, core):
    return span((2 * yy + core) * 4 * size, 4 * size)


def attn_plan(width):
    return [(width, width, 0, 0)] + [(width, width, 1, i * width) for i in range(3)]


def piece(left, right, at, cols, out):
    step = min(left.shape[0], 1024)

    @pl.loop(0, left.shape[0] // step)
    def _(r):
        block = span(r * step, step)
        out[block, :] = jnp.dot(left[block, :], right[:, at:at + cols], preferred_element_type=F32).astype(BF16)


def grads_kernel(n_small, *refs):
    refs = list(refs)
    d_parts = [refs.pop(0) for _ in range(3)]
    d_early = [refs.pop(0) for _ in range(3)]
    dx_early = refs.pop(0)
    dr_ref, x_ref, w_in, g1 = [refs.pop(0) for _ in range(4)]
    lefts = [refs.pop(0) for _ in range(2)]
    rights = [refs.pop(0)]
    ffn_in = [refs.pop(0) for _ in range(4)]
    back_in = [refs.pop(0) for _ in range(2)]
    sums = [refs.pop(0) for _ in range(n_small)]
    outs = [refs.pop(0) for _ in range(2)]
    ffn_out, back_out = refs.pop(0), refs.pop(0)
    small_out, dx_out = refs.pop(0), refs.pop(0)
    left_buf = [refs.pop(0) for _ in range(2)]
    right_buf = [refs.pop(0) for _ in range(2)]
    w, dr, x, dxb = [refs.pop(0) for _ in range(4)]
    own_sums = [refs.pop(0) for _ in range(4)]
    dj = right_buf[1]
    ffn_buf, ffn_rec, back_buf, back_rec = [refs.pop(0) for _ in range(4)]
    width, tokens = lefts[0].shape
    plan = attn_plan(width)
    buf1 = [refs.pop(0) for _ in plan]
    rec1 = [refs.pop(0) for _ in plan]
    rec2 = [refs.pop(0) for _ in plan]
    rec3 = [refs.pop(0) for _ in plan]
    small, small1, small2, small3 = [refs.pop(0) for _ in range(4)]
    (load_sem, s1_send, s1_recv, s2_send, s2_recv, s3_send, s3_recv,
     m_send, m_recv, f_send, f_recv, f_load, b_load, b_send, b_recv, in_sem) = refs[:16]
    relay, way_send, way_recv, on_send, on_recv, e_sem = refs[22:]

    section, dp, seq, core = place()
    y = dp // 2
    sibling = (section, dp + 1 - 2 * core, seq)
    across_y = (section, dp + 2 - 4 * y, seq)
    along = [(section, dp, lax.rem(seq + t, 4)) for t in range(1, 4)]
    count = len(plan)
    steps = tokens // TOK
    load_w = pltpu.make_async_copy(w_in, w, load_sem.at[1, 1])
    loads = [[pltpu.make_async_copy(lefts[0], left_buf[0], load_sem.at[0, 0]),
              pltpu.make_async_copy(rights[0], right_buf[0], load_sem.at[1, 0])],
             [pltpu.make_async_copy(lefts[1], left_buf[1], load_sem.at[0, 1])]]

    def given(i):
        return [pltpu.make_async_copy(a.at[chunk(i)], b.at[chunk(i)], in_sem.at[n, i])
                for n, (a, b) in enumerate(((x_ref, x), (dr_ref, dr)))]

    column = dp - core
    across = (1 - section, dp, seq)
    each, local, _ = dx_out.shape
    part = local // 2
    mates = [across_y] + column_mates(section, dp, seq, core)
    barrier = pltpu.get_barrier_semaphore()
    for mate in mates:
        pl.semaphore_signal(barrier, 1, device_id=mate, device_id_type=MESH)

    @pl.when(section == 1)
    def _():
        pl.semaphore_signal(barrier, 1, device_id=across, device_id_type=MESH)

    pl.semaphore_wait(barrier, len(mates) + 1 - section)
    to_tokens = ToTokens(d_parts, dj, tokens, width, refs[16:19], core, sibling)
    to_tokens_early = ToTokens(d_early, dj, tokens, width, refs[16:19], core, sibling)
    own_sem, way0_send, way0_recv = refs[19:22]

    def goal(j):
        target_core, target_seq = seq // each, core * each + j
        here = (target_core == core) & (target_seq == seq)
        return here, lax.rem(seq, each), (0, column + target_core, target_seq)

    def straight(j):
        _, slot, target = goal(j)
        return remote(dxb.at[pl.ds(j * local, part)], dx_out.at[slot, pl.ds(0, part)], way0_send.at[j], way0_recv.at[slot], target)

    def detour(j):
        return remote(dxb.at[pl.ds(j * local + part, part)], relay.at[j], way_send.at[j], way_recv.at[j], across)

    def onward(j):
        _, slot, target = goal(j)
        return remote(relay.at[j], dx_out.at[slot, pl.ds(part, part)], on_send.at[j], on_recv.at[slot], target)

    def stay(j):
        return pltpu.make_async_copy(dxb.at[pl.ds(j * local, local)], dx_out.at[lax.rem(seq, each)], own_sem)

    def dx_start(j):
        here = goal(j)[0]

        @pl.when((section == 0) & here)
        def _():
            stay(j).start()

        @pl.when((section == 0) & jnp.logical_not(here))
        def _():
            straight(j).start()
            detour(j).start()

    def dx_forward(j):
        @pl.when((section == 1) & jnp.logical_not(goal(j)[0]))
        def _():
            detour(j).wait_recv()
            onward(j).start()

    def dx_finish():
        for j in range(each):
            here = goal(j)[0]

            @pl.when((section == 0) & here)
            def _():
                stay(j).wait()

            @pl.when((section == 0) & jnp.logical_not(here))
            def _():
                straight(j).wait_send()
                detour(j).wait_send()

            @pl.when((section == 1) & jnp.logical_not(here))
            def _():
                onward(j).wait_send()
        for m in range(each):
            here = (seq // each == core) & (core * each + m == seq)

            @pl.when((section == 0) & jnp.logical_not(here))
            def _():
                remote(dxb.at[pl.ds(0, part)], dx_out.at[m, pl.ds(0, part)], way0_send.at[0], way0_recv.at[m], sibling).wait_recv()
                remote(relay.at[0], dx_out.at[m, pl.ds(part, part)], on_send.at[0], on_recv.at[m], sibling).wait_recv()

        @pl.when(section == 1)
        def _():
            for j in range(each):
                load = pltpu.make_async_copy(dx_early.at[j], dxb.at[pl.ds(j * local, local)], e_sem.at[0, j])
                load.start()
                load.wait()
                store = pltpu.make_async_copy(dxb.at[pl.ds(j * local, local)], dx_out.at[j], e_sem.at[1, j])
                store.start()
                store.wait()

    ffn_loads = [pltpu.make_async_copy(ffn_in[t], ffn_buf.at[t], f_load.at[t]) for t in range(4)]
    back_loads = [pltpu.make_async_copy(back_in[t], back_buf.at[t], b_load.at[t]) for t in range(2)]
    for load in back_loads:
        load.start()

    @pl.loop(0, steps)
    def _(i):
        @pl.when(section == 0)
        def _():
            to_tokens.start(i)

        @pl.when(section == 1)
        def _():
            to_tokens_early.start(i)

        for copy in given(i):
            copy.start()

    load_w.start()
    for pair in loads:
        for load in pair:
            load.start()
    for load in ffn_loads:
        load.start()

    def ffn_half(yy):
        rows = ffn_rec.shape[0]
        return span(yy * rows, rows)

    def ffn_sent():
        return remote(ffn_buf.at[0, ffn_half(1 - y)], ffn_rec, f_send, f_recv, across_y)

    def ffn_sum(yy):
        rows = ffn_half(yy)
        total = ffn_buf[0, rows, :].astype(F32)
        for t in range(1, 4):
            total = total + ffn_buf[t, rows, :].astype(F32)
        return total

    next_z = seq + 1 - 2 * lax.rem(seq, 2)
    far_z = lax.rem(seq + 2, 4)

    def back_rows(zz):
        rows = back_rec.shape[1]
        return span(zz * rows, rows)

    def back_near(t):
        return remote(back_buf.at[0, back_rows(lax.rem(next_z + 2 * t, 4))], back_rec.at[t],
                      b_send.at[t], b_recv.at[t], (section, dp, next_z))

    def back_far():
        return remote(back_buf.at[0, back_rows(far_z)], back_rec.at[2], b_send.at[2], b_recv.at[2], (section, dp, far_z))

    def back_add(rows, other):
        back_buf[0, rows, :] = (back_buf[0, rows, :].astype(F32) + other.astype(F32)).astype(BF16)

    size = width // 16

    def half(yy):
        return span(yy * 4 * size, 4 * size)

    def first(p, yy):
        return remote(buf1[p].at[core_rows(size, yy, 1 - core)], rec1[p].at[half(yy)],
                      s1_send.at[p, yy], s1_recv.at[p, yy], sibling)

    def second(p):
        return remote(rec1[p].at[half(1 - y)], rec2[p], s2_send.at[p], s2_recv.at[p], across_y)

    def shard(zz):
        return span(y * 4 * size + zz * size, size)

    def third(p, t):
        target = (section, dp, next_z)
        return remote(rec1[p].at[shard(lax.rem(next_z + 2 * t, 4))], rec3[p].at[t],
                      s3_send.at[p, t], s3_recv.at[p, t], target)

    def fourth(p):
        return remote(rec1[p].at[shard(far_z)], rec3[p].at[2], s3_send.at[p, 2], s3_recv.at[p, 2], (section, dp, far_z))

    def reduce_core(p):
        for yy in range(2):
            first(p, yy).wait_recv()
            total = buf1[p][core_rows(size, yy, core), :].astype(F32) + rec1[p][half(yy), :].astype(F32)
            rec1[p][half(yy), :] = total.astype(BF16)
        second(p).start()

    def reduce_y(p):
        second(p).wait_recv()
        mine = half(y)
        rec1[p][mine, :] = (rec1[p][mine, :].astype(F32) + rec2[p][...].astype(F32)).astype(BF16)
        for t in range(2):
            third(p, t).start()

    def reduce_next(p):
        for t, zz in enumerate((seq, far_z)):
            third(p, t).wait_recv()
            rec1[p][shard(zz), :] = (rec1[p][shard(zz), :].astype(F32) + rec3[p][t].astype(F32)).astype(BF16)
        fourth(p).start()

    def reduce_far(p):
        rows, cols, t_out, at = plan[p]
        fourth(p).wait_recv()
        outs[t_out][:, at:at + cols] = rec1[p][shard(seq), :].astype(F32) + rec3[p][2].astype(F32)

    for load in back_loads:
        load.wait()
    back_buf[0] = (back_buf[0].astype(F32) + back_buf[1].astype(F32)).astype(BF16)
    for t in range(2):
        back_near(t).start()

    for s in own_sums:
        s[...] = jnp.zeros_like(s)
    load_w.wait()
    per = steps // dx_out.shape[0]
    for j in range(dx_out.shape[0]):
        @pl.loop(j * per, (j + 1) * per)
        def _(i):
            to_tokens.wait(i)
            for copy in given(i):
                copy.wait()
            dxb[chunk(i), :] = input_back(i, dj, dr, x, w, g1, own_sums)

        dx_start(j)

    line = 0
    for s in own_sums + sums:
        row = jnp.sum(s[...], axis=0, keepdims=True)
        for t in range(s.shape[1] // 128):
            small[line:line + 1, :] = row[:, t * 128:(t + 1) * 128]
            line += 1
    v1 = remote(small, small1, m_send.at[0], m_recv.at[0], sibling)
    v2 = remote(small, small2, m_send.at[1], m_recv.at[1], across_y)

    def v3(t):
        return remote(small, small3.at[t - 1], m_send.at[1 + t], m_recv.at[1 + t], along[t - 1])

    v1.start()
    v1.wait()
    small[...] += small1[...]
    v2.start()
    ready = set()
    for p, (rows, cols, t, at) in enumerate(plan):
        if t not in ready:
            ready.add(t)
            for load in loads[t]:
                load.wait()
        piece(left_buf[t], right_buf[t], at, cols, buf1[p])
        for yy in range(2):
            first(p, yy).start()
        if p > 0:
            reduce_core(p - 1)
        if p == 1:
            v2.wait()
            small[...] += small2[...]
            for t in range(1, 4):
                v3(t).start()
    reduce_core(count - 1)
    for t, zz in enumerate((seq, far_z)):
        back_near(t).wait_recv()
        back_add(back_rows(zz), back_rec[t])
    back_far().start()
    for load in ffn_loads:
        load.wait()
    ffn_buf[0, ffn_half(1 - y), :] = ffn_sum(1 - y).astype(BF16)
    ffn_sent().start()
    for p in range(count):
        reduce_y(p)
        if p > 0:
            reduce_next(p - 1)
    reduce_next(count - 1)
    for j in range(each):
        dx_forward(j)
    own = ffn_sum(y)
    ffn_sent().wait_recv()
    ffn_out[...] = own + ffn_rec[...].astype(F32)
    back_far().wait_recv()
    back_out[...] = back_buf[0, back_rows(seq), :].astype(F32) + back_rec[2].astype(F32)
    for t in range(1, 4):
        v3(t).wait()
    small_out[...] = small[...] + small3[0] + small3[1] + small3[2]
    for p in range(count):
        reduce_far(p)

    for p in range(count):
        for yy in range(2):
            first(p, yy).wait_send()
        second(p).wait_send()
        for t in range(2):
            third(p, t).wait_send()
        fourth(p).wait_send()
    @pl.loop(0, steps)
    def _(i):
        to_tokens.wait_sent(i)

    ffn_sent().wait_send()
    for t in range(2):
        back_near(t).wait_send()
    back_far().wait_send()
    dx_finish()


def grads_call(d_parts, d_early, dx_early, dr, x, w, g1, att_t, norm_t, d_proj, ffn, back, sums, each):
    width, tokens = att_t.shape
    plan = attn_plan(width)
    count = len(plan)
    steps = tokens // TOK
    one = sds((8, width), F32)
    lines = (4 * width + sum(s.shape[1] for s in sums)) // 128
    vec = pltpu.VMEM((lines, 128), F32)
    buf = lambda s: pltpu.VMEM(s.shape, s.dtype)
    half = (ffn[0].shape[0] // 2, ffn[0].shape[1])
    quarter = (back[0].shape[0] // 4, back[0].shape[1])
    return pl.pallas_call(
        partial(grads_kernel, len(sums)),
        in_specs=[ANY] * 10 + [VMEM] + [ANY] * 9 + [VMEM] * len(sums),
        out_specs=[VMEM] * 5 + [ANY],
        out_shape=[sds((width // 16, width), F32), sds((width // 16, 3 * width), F32)]
        + [sds(half, F32), sds(quarter, F32)]
        + [sds((lines, 128), F32), sds((each, tokens // each, width), BF16)],
        scratch_shapes=(
            [buf(att_t), buf(norm_t), buf(d_proj), pltpu.VMEM((tokens, 3 * width), BF16), buf(w), buf(dr), buf(x), buf(x)]
            + [buf(one)] * 4
            + [pltpu.VMEM((4,) + ffn[0].shape, BF16), pltpu.VMEM(half, BF16),
               pltpu.VMEM((2,) + back[0].shape, BF16), pltpu.VMEM((3,) + quarter, BF16)]
            + [pltpu.VMEM((r, c), BF16) for r, c, *_ in plan]
            + [pltpu.VMEM((r // 2, c), BF16) for r, c, *_ in plan]
            + [pltpu.VMEM((r // 4, c), BF16) for r, c, *_ in plan]
            + [pltpu.VMEM((3, r // 16, c), BF16) for r, c, *_ in plan]
            + [vec, vec, vec, pltpu.VMEM((3, lines, 128), F32)]
            + [DMA((2, 2)), DMA((count, 2)), DMA((count, 2)), DMA((count,)), DMA((count,)),
               DMA((count, 3)), DMA((count, 3)), DMA((5,)), DMA((5,)), DMA, DMA, DMA((4,)), DMA((2,)), DMA((3,)), DMA((3,)),
               DMA((2, steps))]
            + swap_sems(3, steps) + [DMA, DMA((each,)), DMA((each,))]
            + [pltpu.VMEM((each, tokens // each // 2, width), BF16)] + [DMA((each,))] * 4 + [DMA((2, each))]),
        compiler_params=pltpu.CompilerParams(collective_id=8, has_side_effects=True, vmem_limit_bytes=62 * MIB),
        name="weight_grads",
    )(*d_parts, *d_early, dx_early, dr, x, w, g1, att_t, norm_t, d_proj, *ffn, *back, *sums)


def finish_kernel(each, dx_ref, *refs):
    ys, refs = refs[:each], refs[each:]
    count = (len(refs) - 2) // 2
    ins, (dx_out, y_out), outs = refs[:count], refs[count:count + 2], refs[count + 2:]
    dx_out[...] = dx_ref[...].astype(F32)
    step = lax.rem(pl.program_id(0) // 2 - lax.axis_index("seq") + 4 * each, each)
    value = ys[0][...]
    for n in range(1, each):
        value = jnp.where(step == n, ys[n][...], value)
    y_out[0] = value

    @pl.when(pl.program_id(0) == 0)
    def _():
        for a, b in zip(ins, outs):
            b[...] = a[...]


def finish_call(dx, ys, *arrays):
    each, local, width = dx.shape
    block = pl.BlockSpec((1, local // 2, width), lambda i: (i // 2, i % 2, 0))
    half = pl.BlockSpec((local // 2, width), lambda i: (i % 2, 0))
    whole = [pl.BlockSpec(a.shape, lambda i: (0, 0)) for a in arrays]
    return pl.pallas_call(
        partial(finish_kernel, each),
        grid=(2 * each,),
        in_specs=[block] + [half] * each + whole,
        out_specs=[block, block] + whole,
        out_shape=[sds(dx.shape, F32), sds(dx.shape, BF16)] + [sds(a.shape, a.dtype) for a in arrays],
        compiler_params=pltpu.CompilerParams(vmem_limit_bytes=62 * MIB),
        name="finish",
    )(dx, *ys, *arrays)


def swap_cores(x):
    size = lax.axis_size("dp")
    return lax.ppermute(x, "dp", [(i, i ^ 1) for i in range(size)])


def row_moves(each):
    n_dp, n_seq = lax.axis_size("dp"), lax.axis_size("seq")
    steps = []
    for k in range(each):
        pairs = []
        for d in range(n_dp):
            for z in range(n_seq):
                source = (2 * (d // 2) + z // each) * n_seq + (d % 2) * each + (z + k) % each
                pairs.append((source, d * n_seq + z))
        steps.append(pairs)
    return steps


def swap_y(x):
    size = lax.axis_size("dp")
    return lax.ppermute(x, "dp", [(i, i ^ 2) for i in range(size)])


def along_seq(x, by):
    size = lax.axis_size("seq")
    return lax.ppermute(x, "seq", [(i, (i + by) % size) for i in range(size)])


def on_device_rows(cell_tokens, cell_lengths, out_grad, *raw_weights):
    (gain1, bias1, wqkv, qb, vb, wo, bo, gain2, bias2, win, bi, wback, bb) = tuple(
        (w if w.ndim == 2 else w[0] for w in raw_weights)
    )
    each, local, width = cell_tokens.shape
    row_length = local * lax.axis_size("seq")
    core = lax.axis_index("dp") % 2
    z = lax.axis_index("seq")

    lengths = jnp.where(z // each == core, cell_lengths, swap_cores(cell_lengths))
    lengths = lax.dynamic_index_in_dim(lengths, z % each, 0, keepdims=False)
    fq, fk, lo, hi = segment_terms(lengths, row_length)

    x, q, k, v = first_call(cell_tokens, wqkv, gain1, bias1, qb, vb)
    o, _ = attn_fwd(lo, hi, q, k, v, fq, fk)
    x, g, norm_t, q, k, v = pass_call(
        o, x, out_grad, wo, win, wback, wqkv, (bo, gain2, bias2, bi, bb, gain1, bias1, qb, vb))
    o, lse = attn_fwd(lo, hi, q, k, v, fq, fk)
    *ys, resid, slope, att_t, c_t, act_t, dr, do = turn_call(
        o, x, g, wo, win, wback, (bo, gain2, bias2, bi, bb), each)
    ys = [lax.ppermute(part, ("dp", "seq"), pairs) for part, pairs in zip(ys, row_moves(each))]

    dq, dk, dv = attn_bwd(lo, hi, q, k, v, do, o, lse, fq, fk)
    dq, *ys = lax.optimization_barrier((dq, *ys))
    dx_early, dr, dp, do, *rest = back_call(
        dq, dk, dv, dr, x, g, slope, resid, c_t, act_t, wqkv, wo, win, wback, gain1, gain2, each)
    ffn = [w if t == 0 else along_seq(w, t) for t, w in enumerate(rest[:4])]
    back = [rest[4], swap_y(rest[5])]
    s_gain2, s_bias2, s_out, s_in, s_back = rest[6:]
    hi = jnp.where(lax.axis_index("section") == 1, lo, hi)
    d_late = attn_bwd(lo, hi, q, k, v, do, o, lse, fq, fk)
    sums = (s_out, s_gain2, s_bias2, s_in, s_back)
    g_out, g_qkv, g_in, g_back, small, in_grads = grads_call(
        d_late, (dq, dk, dv), dx_early, dr, x, wqkv, gain1, att_t, norm_t, dp, ffn, back, sums, each)
    in_grads, outputs, g_out, g_qkv, g_in, g_back = finish_call(in_grads, ys, g_out, g_qkv, g_in, g_back)

    flat = small.reshape(-1)
    parts = lax.axis_size("dp") * lax.axis_size("seq")
    owner = lax.axis_index("dp") * lax.axis_size("seq") + z
    shares, at = [], 0
    for total in [width] * 4 + [s.shape[1] for s in sums]:
        size = total // parts
        shares.append(lax.dynamic_slice_in_dim(flat, at + owner * size, size))
        at += total
    return (
        outputs[None],
        in_grads[None],
        shares[0][None],
        shares[1][None],
        g_qkv[None],
        shares[2][None],
        shares[3][None],
        g_out[None],
        shares[4][None],
        shares[5][None],
        shares[6][None],
        g_in[None],
        shares[7][None],
        g_back[None],
        shares[8][None],
    )


def either_plan(cell_tokens, *others):
    one_chip = lax.axis_size("dp") % 2 == 0 and lax.axis_size("seq") == 2 * cell_tokens.shape[0] and lax.axis_size("section") == 2 and lax.axis_size("dp") == lax.axis_size("seq") == 4
    return (on_device_rows if one_chip else on_device)(cell_tokens, *others)


def solution(mesh):
    in_specs = (
        P("dp", "seq", None),
        P("dp", None),
        P("dp", "seq", None),
        P("section", None),
        P("section", None),
        P("section", None, None),
        P("section", None),
        P("section", None),
        P("section", None, None),
        P("section", None),
        P("section", None),
        P("section", None),
        P("section", None, None),
        P("section", None),
        P("section", None, None),
        P("section", None),
    )
    out_specs = (
        P("section", "dp", "seq", None),
        P("section", "dp", "seq", None),
        P("section", ("dp", "seq")),
        P("section", ("dp", "seq")),
        P("section", ("dp", "seq"), None),
        P("section", ("dp", "seq")),
        P("section", ("dp", "seq")),
        P("section", ("dp", "seq"), None),
        P("section", ("dp", "seq")),
        P("section", ("dp", "seq")),
        P("section", ("dp", "seq")),
        P("section", ("dp", "seq"), None),
        P("section", ("dp", "seq")),
        P("section", ("dp", "seq"), None),
        P("section", ("dp", "seq")),
    )
    return jax.shard_map(
        either_plan, mesh=mesh, in_specs=in_specs, out_specs=out_specs, check_vma=False
    )
```
